128 devices in a mesh: fsdp: 8 (over x_hi, z), tp: 8 (over y, core), grp: 2 (over x_lo).
Axes of the slice: x: 4 (x_hi: 2, x_lo: 2; x = x_hi * 2 + x_lo), y: 4, z: 4, core: 2. Of those that a mesh axis runs over, the one named last changes fastest.
Arguments:
- noisy_latents: bfloat16 [16, 256, 64], P(('fsdp', 'grp')), may hold values from -20 to 20
- student_step: int32 [16], replicated, may hold values from 1 to 4
- teacher_step: int32 [16], replicated, may hold values from 1 to 1000
- teacher_noise: bfloat16 [16, 256, 64], P(('fsdp', 'grp')), may hold values from -6 to 6
- layer_pick: int32 [16, 2], P(('fsdp', 'grp')), may hold values from 0 to 1
- in_proj_s: bfloat16 [64, 2432], P(None, 'tp'), may hold values from -3 to 3
- in_proj_t: bfloat16 [64, 2432], P(None, 'tp'), may hold values from -3 to 3
- out_proj: bfloat16 [64, 2432], P(None, 'tp'), may hold values from -0.125 to 0.125
- s_mod: bfloat16 [2432, 7296], P(('fsdp', 'grp'), 'tp'), may hold values from -0.25 to 0.25
- s_w1: bfloat16 [2432, 9728], P(('fsdp', 'grp'), 'tp'), may hold values from -0.125 to 0.125
- s_w2: bfloat16 [9728, 2432], P('tp', ('fsdp', 'grp')), may hold values from -0.0625 to 0.0625
- t_mod: bfloat16 [2, 2432, 7296], P(None, ('fsdp', 'grp'), 'tp'), may hold values from -0.125 to 0.125
- t_w1: bfloat16 [2, 2432, 9728], P(None, None, 'tp'), may hold values from -0.125 to 0.125
- t_w2: bfloat16 [2, 9728, 2432], P(None, 'tp'), may hold values from -0.0625 to 0.0625
- d_w1: bfloat16 [2432, 2432], P(('fsdp', 'grp'), 'tp'), may hold values from -0.125 to 0.125
- d_w2: float32 [2, 2432], P(None, 'tp'), may hold values from -0.6 to 0.6
Outputs:
- latents: bfloat16 [16, 256, 64], P(('fsdp', 'grp'))
- disc_scores: float32 [16, 2, 256], P(('fsdp', 'grp'))
- latent_grad: float32 [16, 256, 64], P(('fsdp', 'grp'))
The draws below stay inside these ranges and needn't reach their ends.
All inputs are finite; a program needn't handle non-finite values.
Results may differ from the reference program's by a relative error of at most 0.03.
Values may be sent and summed in bfloat16 or wider, within the bound.
No kernel may reach another device: no remote copies, remote signals or barrier semaphores. Data moves between devices by JAX's collectives and lax.ppermute only.
A program may use at most 128 MiB of HBM per device.

```python
import math
import jax
import jax.numpy as jnp
from jax import lax

D = 2432
FF = 9728
P_SIZE = 64
DH = 2432
LT = 2
NH = 2
SEQ = 256
SAMPLES = 16
N_TP = 8


def column_scales(key, width):
    return jnp.exp(jax.random.uniform(key, (1, width), jnp.float32, math.log(0.3), math.log(3.0)))


def draw_noisy_latents(key, part):
    key = jax.random.fold_in(key, 11)
    first, second = jax.random.split(key, 2)
    scales = jnp.exp(jax.random.uniform(second, (SAMPLES, SEQ, 1), jnp.float32, math.log(0.5), math.log(5.0)))
    values = jnp.clip(jax.random.normal(first, (SAMPLES, SEQ, P_SIZE), jnp.float32), -4.0, 4.0)
    return (values * scales).astype(jnp.bfloat16)


def draw_in_proj_s(key, part):
    key = jax.random.fold_in(key, 21)
    first, second = jax.random.split(key)
    values = jnp.clip(jax.random.normal(first, (P_SIZE, D), jnp.float32), -4.0, 4.0)
    return (values * column_scales(second, D) * P_SIZE ** (-0.5)).astype(jnp.bfloat16)


def draw_in_proj_t(key, part):
    key = jax.random.fold_in(key, 22)
    first, second = jax.random.split(key)
    values = jnp.clip(jax.random.normal(first, (P_SIZE, D), jnp.float32), -4.0, 4.0)
    return (values * column_scales(second, D) * P_SIZE ** (-0.5)).astype(jnp.bfloat16)


def touch_ends(values, key, smallest, high):
    extent = values.shape
    spot = [jax.random.randint(jax.random.fold_in(key, axis), (), 0, extent[axis]) for axis in range(len(extent))]
    values = values.at[tuple(spot)].set(smallest)
    longest = extent.index(max(extent))
    spot[longest] = (spot[longest] + 1) % extent[longest]
    return values.at[tuple(spot)].set(high)


def block_scale(own_key, extent, shards, low, high):
    def one(axis_at, blocks):
        steps = jax.random.uniform(jax.random.fold_in(jax.random.fold_in(own_key, 6), axis_at), (blocks,), jnp.float32, low / len(shards), high / len(shards))
        return jnp.repeat(jnp.exp(steps), extent[axis_at] // blocks).reshape((-1,) + (1,) * (len(extent) - axis_at - 1))

    loudness = one(*shards[0])
    for cut in shards[1:]:
        loudness = loudness * one(*cut)
    return loudness


def bell_draw(own_key, dims, scale, reach, cuts=(), held_as=jnp.bfloat16):
    loudness = block_scale(own_key, dims, cuts, -0.22, 0.18) if cuts else 1.0
    values = jax.random.normal(own_key, dims, jnp.float32) * scale * loudness
    return jnp.minimum(jnp.maximum(values, -reach), reach).astype(held_as)


def setup_inputs(seed: int = 0) -> dict:
    keys = jax.random.split(jax.random.key(seed), 17)
    noisy_latents = draw_noisy_latents(jax.random.fold_in(keys[16], 71), 0)
    student_step = touch_ends(jax.random.randint(keys[1], (SAMPLES,), 1, 5), jax.random.fold_in(keys[1], 1), 1, 4).astype(jnp.int32)
    teacher_step = touch_ends(jax.random.randint(keys[2], (SAMPLES,), 1, 1001), jax.random.fold_in(keys[2], 1), 1, 1000).astype(jnp.int32)
    teacher_noise = bell_draw(keys[3], (SAMPLES, SEQ, P_SIZE), 1.0, 6.0, ((0, 16),))
    layer_pick = touch_ends(jax.random.randint(keys[4], (SAMPLES, NH), 0, LT), jax.random.fold_in(keys[4], 1), 0, LT - 1).astype(jnp.int32)
    in_proj_s = draw_in_proj_s(jax.random.fold_in(keys[16], 71), 0)
    in_proj_t = draw_in_proj_t(jax.random.fold_in(keys[16], 71), 0)
    out_proj = bell_draw(keys[7], (P_SIZE, D), D ** -0.5, 0.125, ((1, 8),))
    s_mod = bell_draw(keys[8], (D, 3 * D), (D // 4) ** -0.5, 0.25, ((0, 16), (1, 8)))
    s_w1 = bell_draw(keys[9], (D, FF), D ** -0.5, 0.125, ((0, 16), (1, 8)))
    s_w2 = bell_draw(keys[10], (FF, D), FF ** -0.5, 0.0625, ((0, 8), (1, 16)))
    t_mod = bell_draw(keys[11], (LT, D, 3 * D), D ** -0.5, 0.125, ((1, 16), (2, 8)))
    t_w1 = bell_draw(keys[12], (LT, D, FF), D ** -0.5, 0.125, ((2, 8),))
    t_w2 = bell_draw(keys[13], (LT, FF, D), FF ** -0.5, 0.0625, ((1, 8),))
    d_w1 = bell_draw(keys[14], (D, DH), D ** -0.5, 0.125, ((0, 16), (1, 8)))
    d_w2 = bell_draw(keys[15], (NH, DH), 0.1, 0.6, ((1, 8),), jnp.float32)
    return {"noisy_latents": noisy_latents, "student_step": student_step, "teacher_step": teacher_step, "teacher_noise": teacher_noise, "layer_pick": layer_pick, "in_proj_s": in_proj_s, "in_proj_t": in_proj_t, "out_proj": out_proj, "s_mod": s_mod, "s_w1": s_w1, "s_w2": s_w2, "t_mod": t_mod, "t_w1": t_w1, "t_w2": t_w2, "d_w1": d_w1, "d_w2": d_w2}


HIGH = lax.Precision.HIGHEST

def embed(times, width):
    half = width // 2
    steps = jnp.arange(half, dtype=jnp.float32)
    freq = jnp.exp(-math.log(10000.0) * steps / half)
    angle = times[:, None] * freq[None, :]
    return jnp.concatenate([jnp.cos(angle), jnp.sin(angle)], axis=1)

def normalize(values):
    mean = lax.optimization_barrier(jnp.mean(values, axis=-1, keepdims=True))
    centered = values - mean
    inverse = lax.rsqrt(lax.optimization_barrier(jnp.mean(centered * centered, axis=-1, keepdims=True)) + 1e-06)
    return (centered * inverse, inverse)

def ln_back(grad, normed, inverse):
    mean_grad = lax.optimization_barrier(jnp.mean(grad, axis=-1, keepdims=True))
    mean_cross = lax.optimization_barrier(jnp.mean(grad * normed, axis=-1, keepdims=True))
    return inverse * (grad - mean_grad - normed * mean_cross)

def gelu_tanh(values):
    inner = 0.7978845608 * (values + 0.044715 * values * values * values)
    return 0.5 * values * (1.0 + jnp.tanh(inner))

def gelu_slope(values):
    inner = 0.7978845608 * (values + 0.044715 * values * values * values)
    tangent = jnp.tanh(inner)
    return 0.5 * (1.0 + tangent) + 0.5 * values * (1.0 - tangent * tangent) * 0.7978845608 * (1.0 + 3.0 * 0.044715 * values * values)

def silu_slope(values):
    sigm = jax.nn.sigmoid(values)
    return sigm * (1.0 + values * (1.0 - sigm))

def block_sum(left, right_wide):
    rows = left.shape[0]
    inner = left.shape[1] // N_TP
    parts = jnp.einsum('ntk,tkm->tnm', left.reshape(rows, N_TP, inner).astype(jnp.float32), right_wide.reshape(N_TP, inner, right_wide.shape[1]))
    return lax.optimization_barrier(jnp.sum(parts.astype(jnp.bfloat16).astype(jnp.float32), axis=0))

def reference(noisy_latents, student_step, teacher_step, teacher_noise, layer_pick, in_proj_s, in_proj_t, out_proj, s_mod, s_w1, s_w2, t_mod, t_w1, t_w2, d_w1, d_w2):
    sig_s = student_step.astype(jnp.float32) * 0.25
    sig_t = teacher_step.astype(jnp.float32) * 0.001
    cond_s = jax.nn.silu(embed(1000.0 * sig_s, D))
    cond_t = jax.nn.silu(embed(1000.0 * sig_t, D))
    mod_s = jnp.dot(cond_s, s_mod.astype(jnp.float32), precision=HIGH)
    mod_t = jnp.einsum('sd,lde->sle', cond_t, t_mod.astype(jnp.float32), precision=HIGH)
    s_w2_wide = s_w2.astype(jnp.float32)
    t_w2_wide = t_w2.astype(jnp.float32)
    t_w1_back = jnp.swapaxes(t_w1, 1, 2).astype(jnp.float32)
    d_w1_back = d_w1.T.astype(jnp.float32)

    def one_sample(items):
        latent_in, noise, picks, mods, mods_t, sigma_s, sigma_t = items
        shift, scale, gate = (mods[:D], mods[D:2 * D], mods[2 * D:])
        h0 = jnp.dot(latent_in, in_proj_s, preferred_element_type=jnp.float32).astype(jnp.bfloat16)
        normed, inverse = normalize(h0.astype(jnp.float32))
        u_s = (normed * (1.0 + scale) + shift).astype(jnp.bfloat16)
        z_s = jnp.dot(u_s, s_w1, preferred_element_type=jnp.float32)
        a_s = gelu_tanh(z_s).astype(jnp.bfloat16)
        y_s = block_sum(a_s, s_w2_wide)
        h1 = (h0.astype(jnp.float32) + gate * y_s).astype(jnp.bfloat16)
        velocity = jnp.dot(h1, out_proj.T, preferred_element_type=jnp.float32)
        latents = (latent_in.astype(jnp.float32) - sigma_s * velocity).astype(jnp.bfloat16)
        noised = ((1.0 - sigma_t) * latents.astype(jnp.float32) + sigma_t * noise.astype(jnp.float32)).astype(jnp.bfloat16)
        hidden = jnp.dot(noised, in_proj_t, preferred_element_type=jnp.float32).astype(jnp.bfloat16)
        outputs = [hidden]
        saved = []
        for layer in range(LT):
            shift_l, scale_l, gate_l = (mods_t[layer, :D], mods_t[layer, D:2 * D], mods_t[layer, 2 * D:])
            normed, inverse = normalize(hidden.astype(jnp.float32))
            u_l = (normed * (1.0 + scale_l) + shift_l).astype(jnp.bfloat16)
            z_l = jnp.dot(u_l, t_w1[layer], preferred_element_type=jnp.float32)
            a_l = gelu_tanh(z_l).astype(jnp.bfloat16)
            y_l = block_sum(a_l, t_w2_wide[layer])
            hidden = (hidden.astype(jnp.float32) + gate_l * y_l).astype(jnp.bfloat16)
            saved.append((normed, inverse, z_l, scale_l, gate_l))
            outputs.append(hidden)
        into = [jnp.zeros((SEQ, D), jnp.float32) for layer in range(LT + 1)]
        scores = []
        for head in range(NH):
            chosen = jnp.zeros((SEQ, D), jnp.float32)
            for layer in range(LT):
                chosen = chosen + jnp.where(picks[head] == layer, outputs[layer + 1].astype(jnp.float32), 0.0)
            q_normed, q_inverse = normalize(chosen)
            e_h = jnp.dot(q_normed.astype(jnp.bfloat16), d_w1, preferred_element_type=jnp.float32)
            scores.append(jnp.dot(jax.nn.silu(e_h), d_w2[head], precision=HIGH))
            de_h = (-d_w2[head][None, :] * silu_slope(e_h)).astype(jnp.bfloat16)
            dq_h = ln_back(block_sum(de_h, d_w1_back), q_normed, q_inverse)
            for layer in range(LT):
                into[layer + 1] = into[layer + 1] + jnp.where(picks[head] == layer, dq_h, 0.0)
        grad = into[LT]
        for layer in reversed(range(LT)):
            normed, inverse, z_l, scale_l, gate_l = saved[layer]
            dy_l = (gate_l * grad).astype(jnp.bfloat16)
            da_l = jnp.dot(dy_l, t_w2[layer].T, preferred_element_type=jnp.float32)
            dz_l = (da_l * gelu_slope(z_l)).astype(jnp.bfloat16)
            du_l = block_sum(dz_l, t_w1_back[layer])
            grad = grad + ln_back(du_l * (1.0 + scale_l), normed, inverse) + into[layer]
        back = jnp.dot(grad.astype(jnp.bfloat16), in_proj_t.T, preferred_element_type=jnp.float32)
        return (latents, jnp.stack(scores), (1.0 - sigma_t) * back)
    return lax.map(one_sample, (noisy_latents, teacher_noise, layer_pick, mod_s, mod_t, sig_s, sig_t))
```

```python
import math

import jax
import jax.numpy as jnp
from jax import lax
from jax.sharding import Mesh
from jax.sharding import PartitionSpec as P

HIGH = lax.Precision.HIGHEST
SAMPLE = ("fsdp", "grp")
TP = ("y", "core")
STEPS = 4
BF = jnp.bfloat16
F32 = jnp.float32


def embed_block(times, width, block, start):
    half = width // 2
    column = start + jnp.arange(block)
    steps = jnp.where(column < half, column, column - half).astype(F32)
    freq = jnp.exp(-math.log(10000.0) * steps / half)
    angle = times[:, None] * freq[None, :]
    return jnp.where((column < half)[None, :], jnp.cos(angle), jnp.sin(angle))


def normalize(values):
    mean = jnp.mean(values, axis=-1, keepdims=True)
    centered = values - mean
    inverse = lax.rsqrt(jnp.mean(centered * centered, axis=-1, keepdims=True) + 1e-06)
    return (centered * inverse, inverse)


def ln_back(grad, normed, inverse):
    mean_grad = jnp.mean(grad, axis=-1, keepdims=True)
    mean_cross = jnp.mean(grad * normed, axis=-1, keepdims=True)
    return inverse * (grad - mean_grad - normed * mean_cross)


def gelu_tanh(values):
    inner = 0.7978845608 * (values + 0.044715 * values * values * values)
    return 0.5 * values * (1.0 + jnp.tanh(inner))


def gelu_slope(values):
    inner = 0.7978845608 * (values + 0.044715 * values * values * values)
    tangent = jnp.tanh(inner)
    return 0.5 * (1.0 + tangent) + 0.5 * values * (1.0 - tangent * tangent) * 0.7978845608 * (
        1.0 + 3.0 * 0.044715 * values * values
    )


def silu_slope(values):
    sigm = jax.nn.sigmoid(values)
    return sigm * (1.0 + values * (1.0 - sigm))


def dot(left, right):
    return jnp.dot(left, right, preferred_element_type=F32)


def dot_back(left, right):
    return lax.dot_general(left, right, (((1,), (1,)), ((), ())), preferred_element_type=F32)


def split(values):
    high = values.astype(BF)
    return high, (values - high.astype(F32)).astype(BF)


def sibling(values):
    return lax.ppermute(values, "core", [(0, 1), (1, 0)])


def scatter_y(partial):
    rows = partial.shape[0] // 4
    parts = lax.all_to_all(partial.astype(BF).reshape(4, rows, -1), "y", 0, 0)
    return jnp.sum(parts.astype(F32), axis=0)


def gather_y(values):
    return lax.all_gather(values, "y", axis=0, tiled=True)


def body(
    noisy_latents,
    student_step,
    teacher_step,
    teacher_noise,
    layer_pick,
    in_proj_s,
    in_proj_t,
    out_proj,
    s_mod,
    s_w1,
    s_w2,
    t_mod,
    t_w1,
    t_w2,
    d_w1,
    d_w2,
):
    cells = in_proj_s.shape[0]
    width = in_proj_s.shape[1] * 8
    samples = student_step.shape[0]
    layers = t_w1.shape[0]
    heads = d_w2.shape[0]
    seq = noisy_latents.shape[1]
    half = seq // 2
    quarter = half // 4
    rows = s_mod.shape[0]
    hidden = s_w1.shape[1]
    chunk = cells // samples
    sample = lax.axis_index(SAMPLE)
    at_y = lax.axis_index("y")
    at_core = lax.axis_index("core")
    start = sample * rows

    w1_sib = sibling(t_w1)
    w2_sib = sibling(t_w2)
    head_own = lax.all_gather(d_w1, SAMPLE, axis=0, tiled=True)
    d_w2_sib = sibling(d_w2)

    sig_all_t = teacher_step.astype(F32) * 0.001
    sig_steps = (1 + jnp.arange(STEPS)).astype(F32) * 0.25
    cond_s = jax.nn.silu(embed_block(1000.0 * sig_steps, width, rows, start))
    cond_t = jax.nn.silu(embed_block(1000.0 * sig_all_t, width, rows, start))
    mod_s = jnp.dot(cond_s, s_mod.astype(F32), precision=HIGH)
    mod_t = [jnp.dot(cond_t, t_mod[l].astype(F32), precision=HIGH) for l in range(layers)]
    mod_part = jnp.concatenate(
        [jnp.stack(mod_t, axis=1), jnp.broadcast_to(mod_s[None], (samples,) + mod_s.shape)], axis=1
    ).astype(BF)
    mod_part = lax.all_to_all(mod_part, SAMPLE, 0, 0)
    mods = jnp.sum(mod_part.astype(F32), axis=0)
    mods = lax.all_gather(mods[None], TP, axis=2, tiled=True)[0]
    mod_teacher, mod_student = mods[:layers], mods[layers:]

    packed = lax.all_gather(
        jnp.concatenate([in_proj_s, in_proj_t, out_proj], axis=0), TP, axis=1, tiled=True
    )
    proj_s, proj_t, proj_out = packed[:cells], packed[cells : 2 * cells], packed[2 * cells :]

    def my_rows(values):
        return lax.dynamic_slice_in_dim(values, start, rows, values.ndim - 1)

    proj_s_wide = proj_s.astype(F32)
    centered_s = proj_s_wide - jnp.mean(proj_s_wide, axis=1, keepdims=True)
    block_s = my_rows(mod_student.reshape(STEPS, 3, width))
    shift_s, scale_s, gate_s = block_s[:, 0], block_s[:, 1], block_s[:, 2]
    left_in = my_rows(centered_s).reshape(samples, 1, chunk, rows) * (1.0 + scale_s)[None, :, None, :]
    left_out = (
        my_rows(proj_out).astype(F32).reshape(samples, 1, chunk, rows) * gate_s[None, :, None, :]
    )
    piece = STEPS * chunk
    part_in = dot(left_in.reshape(samples * piece, rows).astype(BF), s_w1).astype(BF)
    part_out = dot_back(left_out.reshape(samples * piece, rows).astype(BF), s_w2).astype(BF)
    part_shift = dot(shift_s.astype(BF), s_w1).astype(BF)
    parts = jnp.concatenate(
        [
            part_in.reshape(samples, piece, hidden),
            part_out.reshape(samples, piece, hidden),
            jnp.broadcast_to(part_shift[None], (samples, STEPS, hidden)),
        ],
        axis=1,
    )
    sums = jnp.sum(lax.all_to_all(parts, SAMPLE, 0, 0).astype(F32), axis=0)
    my_step = lax.dynamic_index_in_dim(student_step, sample, keepdims=False)
    bias_s = lax.dynamic_index_in_dim(sums[2 * piece :], my_step - 1, keepdims=False)
    table = sums[: 2 * piece].astype(BF).reshape(2, STEPS, chunk, hidden)
    chosen = jnp.zeros((samples, 2, chunk, hidden), BF)
    for step in range(STEPS):
        chosen = jnp.where((student_step == step + 1)[:, None, None, None], table[None, :, step], chosen)
    mine = lax.all_to_all(chosen, SAMPLE, 0, 0)
    mat_in = mine[:, 0].reshape(cells, hidden)
    mat_out = mine[:, 1].reshape(cells, hidden)

    sigma_s = my_step.astype(F32) * 0.25
    sigma_t = lax.dynamic_index_in_dim(sig_all_t, sample, keepdims=False)
    latent_in = noisy_latents[0]
    h0 = dot(latent_in, proj_s).astype(BF)
    _, inverse_s = normalize(h0.astype(F32))
    z_s = inverse_s * dot(latent_in, mat_in) + bias_s[None]
    a_s = gelu_tanh(z_s).astype(BF)
    velocity = dot_back(a_s, mat_out)
    mine_first = lax.dynamic_slice_in_dim(velocity, at_core * half, half, 0)
    other = lax.dynamic_slice_in_dim(velocity, (1 - at_core) * half, half, 0)
    velocity = mine_first + sibling(other)
    velocity = velocity + lax.ppermute(velocity, "y", [(0, 1), (1, 0), (2, 3), (3, 2)])
    velocity = velocity + lax.ppermute(velocity, "y", [(0, 2), (2, 0), (1, 3), (3, 1)])

    def my_half(values):
        return lax.dynamic_slice_in_dim(values, at_core * half, half, 0)

    def my_quarter(values):
        return lax.dynamic_slice_in_dim(values, at_y * quarter, quarter, 0)

    velocity = velocity + dot_back(my_half(h0), proj_out)
    latents = (my_half(latent_in).astype(F32) - sigma_s * velocity).astype(BF)
    noised = (
        (1.0 - sigma_t) * latents.astype(F32) + sigma_t * my_half(teacher_noise[0]).astype(F32)
    ).astype(BF)

    shifts = [mod_teacher[l, :width] for l in range(layers)]
    scales = [mod_teacher[l, width : 2 * width] for l in range(layers)]
    gates = [mod_teacher[l, 2 * width :] for l in range(layers)]
    proj_t_wide = proj_t.astype(F32)
    centered_t = proj_t_wide - jnp.mean(proj_t_wide, axis=1, keepdims=True)
    left_t = (centered_t * (1.0 + scales[0])).astype(BF)
    shift_t = jnp.broadcast_to(shifts[0][None], (8, width)).astype(BF)
    w1 = [(t_w1[l], w1_sib[l]) for l in range(layers)]
    w2 = [(t_w2[l], w2_sib[l]) for l in range(layers)]
    head_weight = (head_own, sibling(head_own))
    head_out = (d_w2, d_w2_sib)
    mat_t = [split(dot(left_t, w)) for w in w1[0]]
    bias_t = [dot(shift_t, w)[:1] for w in w1[0]]

    g_0 = dot(noised, proj_t).astype(BF)
    normed_0, inverse_0 = normalize(g_0.astype(F32))
    z_0 = [
        inverse_0 * (dot(noised, high) + dot(noised, low)) + bias
        for (high, low), bias in zip(mat_t, bias_t)
    ]
    y_0 = sum(dot(gelu_tanh(z).astype(BF), w) for z, w in zip(z_0, w2[0]))
    g_1_mine = (my_quarter(g_0).astype(F32) + gates[0] * scatter_y(y_0)).astype(BF)
    g_1 = gather_y(g_1_mine)
    normed_1, _ = normalize(g_1.astype(F32))
    u_1 = (normed_1 * (1.0 + scales[1]) + shifts[1]).astype(BF)
    z_1 = [dot(u_1, w) for w in w1[1]]
    y_1 = sum(dot(gelu_tanh(z).astype(BF), w) for z, w in zip(z_1, w2[1]))
    g_2_mine = (g_1_mine.astype(F32) + gates[1] * scatter_y(y_1)).astype(BF)
    g_2 = gather_y(g_2_mine)
    normed_2, _ = normalize(g_2.astype(F32))

    picks = layer_pick[0]
    head_back = []
    scores = [jnp.zeros((half,), F32) for head in range(heads)]
    for layer, normed in enumerate((normed_1, normed_2)):
        quantised = normed.astype(BF)
        back = jnp.zeros((half, width), F32)
        for weight, out in zip(head_weight, head_out):
            e = dot(quantised, weight)
            active = jax.nn.silu(e)
            total = jnp.zeros((weight.shape[1],), F32)
            for head in range(heads):
                use = (picks[head] == layer).astype(F32)
                total = total - use * out[head]
                scores[head] = scores[head] + jnp.sum(active * (use * out[head])[None], axis=1)
            back = back + dot_back((total[None] * silu_slope(e)).astype(BF), weight)
        head_back.append(back)

    normed_2m, inverse_2m = normalize(g_2_mine.astype(F32))
    dg_2 = ln_back(scatter_y(head_back[1]), normed_2m, inverse_2m)
    dy_1 = gather_y((gates[1] * dg_2).astype(BF))
    du_1 = jnp.zeros((half, width), F32)
    for z, up, down in zip(z_1, w1[1], w2[1]):
        dz = (dot_back(dy_1, down) * gelu_slope(z)).astype(BF)
        du_1 = du_1 + dot_back(dz, up)
    normed_1m, inverse_1m = normalize(g_1_mine.astype(F32))
    dg_1 = dg_2 + ln_back(
        scatter_y(du_1 * (1.0 + scales[1]) + head_back[0]), normed_1m, inverse_1m
    )
    dy_0 = gather_y((gates[0] * dg_1).astype(BF))
    down_0 = jnp.zeros((half, cells), F32)
    for z, (high, low), down in zip(z_0, mat_t, w2[0]):
        dz = (dot_back(dy_0, down) * gelu_slope(z)).astype(BF)
        down_0 = down_0 + dot_back(dz, high) + dot_back(dz, low)
    direct = dot_back(dg_1.astype(BF), proj_t)
    direct = lax.dynamic_update_slice_in_dim(
        jnp.zeros((half, cells), F32), direct, at_y * quarter, 0
    )
    final = jnp.concatenate(
        [down_0, direct, jnp.stack(scores, axis=1), jnp.zeros((half, 128 - heads), F32)], axis=1
    )
    final = final + lax.ppermute(final, "y", [(0, 1), (1, 0), (2, 3), (3, 2)])
    final = final + lax.ppermute(final, "y", [(0, 2), (2, 0), (1, 3), (3, 1)])
    down_0, direct, scores = final[:, :cells], final[:, cells : 2 * cells], final[:, 2 * cells :]
    cross = inverse_0 * jnp.sum(noised.astype(F32) * down_0, axis=1, keepdims=True) / width
    normed_back = dot_back(normed_0.astype(BF), proj_t)
    grad = (1.0 - sigma_t) * (inverse_0 * (down_0 - normed_back * cross) + direct)
    result = jnp.concatenate([grad, scores[:, :cells]], axis=1)

    def both(values):
        other = sibling(values)
        first = jnp.where(at_core == 0, values, other)
        second = jnp.where(at_core == 0, other, values)
        return jnp.concatenate([first, second], axis=0)

    result = both(result)
    latents = both(latents)
    return (latents[None], result[:, cells : cells + heads].T[None], result[:, :cells][None])


def solution(mesh):
    names = list(mesh.axis_names)
    shape = list(mesh.devices.shape)
    at = names.index("tp")
    names[at : at + 1] = ["y", "core"]
    shape[at : at + 1] = [4, 2]
    fine = Mesh(mesh.devices.reshape(shape), tuple(names))
    placed = (
        P(SAMPLE, None, None),
        P(),
        P(),
        P(SAMPLE, None, None),
        P(SAMPLE, None),
        P(None, TP),
        P(None, TP),
        P(None, TP),
        P(SAMPLE, TP),
        P(SAMPLE, TP),
        P(TP, SAMPLE),
        P(None, SAMPLE, TP),
        P(None, None, TP),
        P(None, TP, None),
        P(SAMPLE, TP),
        P(None, TP),
    )
    return jax.shard_map(
        body,
        mesh=fine,
        in_specs=placed,
        out_specs=(P(SAMPLE, None, None), P(SAMPLE, None, None), P(SAMPLE, None, None)),
        check_vma=False,
    )
```

```python
import math

import jax
import jax.numpy as jnp
from jax import lax
from jax.sharding import Mesh
from jax.sharding import PartitionSpec as P

HIGH = lax.Precision.HIGHEST
SAMPLE = ("fsdp", "grp")
TP = ("y", "core")
STEPS = 4
BF = jnp.bfloat16
F32 = jnp.float32


def embed_block(times, width, block, start):
    half = width // 2
    column = start + jnp.arange(block)
    steps = jnp.where(column < half, column, column - half).astype(F32)
    freq = jnp.exp(-math.log(10000.0) * steps / half)
    angle = times[:, None] * freq[None, :]
    return jnp.where((column < half)[None, :], jnp.cos(angle), jnp.sin(angle))


def normalize(values):
    mean = jnp.mean(values, axis=-1, keepdims=True)
    centered = values - mean
    inverse = lax.rsqrt(jnp.mean(centered * centered, axis=-1, keepdims=True) + 1e-06)
    return (centered * inverse, inverse)


def ln_back(grad, normed, inverse):
    mean_grad = jnp.mean(grad, axis=-1, keepdims=True)
    mean_cross = jnp.mean(grad * normed, axis=-1, keepdims=True)
    return inverse * (grad - mean_grad - normed * mean_cross)


def gelu_tanh(values):
    inner = 0.7978845608 * (values + 0.044715 * values * values * values)
    return 0.5 * values * (1.0 + jnp.tanh(inner))


def gelu_slope(values):
    inner = 0.7978845608 * (values + 0.044715 * values * values * values)
    tangent = jnp.tanh(inner)
    return 0.5 * (1.0 + tangent) + 0.5 * values * (1.0 - tangent * tangent) * 0.7978845608 * (
        1.0 + 3.0 * 0.044715 * values * values
    )


def silu_slope(values):
    sigm = jax.nn.sigmoid(values)
    return sigm * (1.0 + values * (1.0 - sigm))


def dot(left, right):
    return jnp.dot(left, right, preferred_element_type=F32)


def dot_back(left, right):
    return lax.dot_general(left, right, (((1,), (1,)), ((), ())), preferred_element_type=F32)


def split(values):
    high = values.astype(BF)
    return high, (values - high.astype(F32)).astype(BF)


def sibling(values):
    return lax.ppermute(values, "core", [(0, 1), (1, 0)])


def scatter_y(partial):
    rows = partial.shape[0] // 4
    parts = lax.all_to_all(partial.astype(BF).reshape(4, rows, -1), "y", 0, 0)
    return jnp.sum(parts.astype(F32), axis=0)


def gather_y(values):
    return lax.all_gather(values, "y", axis=0, tiled=True)


def body(
    noisy_latents,
    student_step,
    teacher_step,
    teacher_noise,
    layer_pick,
    in_proj_s,
    in_proj_t,
    out_proj,
    s_mod,
    s_w1,
    s_w2,
    t_mod,
    t_w1,
    t_w2,
    d_w1,
    d_w2,
):
    cells = in_proj_s.shape[0]
    width = in_proj_s.shape[1] * 8
    samples = student_step.shape[0]
    layers = t_w1.shape[0]
    heads = d_w2.shape[0]
    seq = noisy_latents.shape[1]
    half = seq // 2
    quarter = half // 4
    rows = s_mod.shape[0]
    hidden = s_w1.shape[1]
    columns = in_proj_s.shape[1]
    sample = lax.axis_index(SAMPLE)
    at_y = lax.axis_index("y")
    at_core = lax.axis_index("core")
    start = sample * rows

    sig_all_t = teacher_step.astype(F32) * 0.001
    sig_steps = (1 + jnp.arange(STEPS)).astype(F32) * 0.25
    cond_s = jax.nn.silu(embed_block(1000.0 * sig_steps, width, rows, start))
    cond_t = jax.nn.silu(embed_block(1000.0 * sig_all_t, width, rows, start))
    mod_s = jnp.dot(cond_s, s_mod.astype(F32), precision=HIGH)
    mod_t = [jnp.dot(cond_t, t_mod[l].astype(F32), precision=HIGH) for l in range(layers)]
    mod_part = jnp.concatenate(
        [jnp.stack(mod_t, axis=1), jnp.broadcast_to(mod_s[None], (samples,) + mod_s.shape)], axis=1
    ).astype(BF)
    mod_part = lax.all_to_all(mod_part, SAMPLE, 0, 0)
    mods = jnp.sum(mod_part.astype(F32), axis=0)
    kinds = layers + STEPS
    mods_high, mods_low = split(mods.reshape(kinds * 3, columns))
    packed = jnp.concatenate([in_proj_s, in_proj_t, out_proj, mods_high, mods_low], axis=0)
    packed = lax.all_gather(packed, TP, axis=0, tiled=False)
    mods = packed[:, 3 * cells : 3 * cells + 3 * kinds].astype(F32) + packed[
        :, 3 * cells + 3 * kinds :
    ].astype(F32)
    mods = mods.reshape(8, kinds, 3, columns).transpose(1, 0, 2, 3).reshape(kinds, 3 * width)
    mod_teacher, mod_student = mods[:layers], mods[layers:]
    packed = packed[:, : 3 * cells].transpose(1, 0, 2).reshape(3 * cells, width)
    proj_s, proj_t, proj_out = packed[:cells], packed[cells : 2 * cells], packed[2 * cells :]

    t_w1_last, t_w2_all, mod_teacher = lax.optimization_barrier((t_w1[1], t_w2, mod_teacher))
    w2_sib = sibling(t_w2_all)
    w1_sib = sibling(t_w1_last)
    d_w2_sib = sibling(d_w2)

    def my_rows(values):
        return lax.dynamic_slice_in_dim(values, start, rows, values.ndim - 1)

    proj_s_wide = proj_s.astype(F32)
    centered_s = proj_s_wide - jnp.mean(proj_s_wide, axis=1, keepdims=True)
    block_s = my_rows(mod_student.reshape(STEPS, 3, width))
    shift_s, scale_s, gate_s = block_s[:, 0], block_s[:, 1], block_s[:, 2]
    row_at = jnp.arange(cells * STEPS)
    by_cell = (row_at[:, None] // STEPS == jnp.arange(cells)[None]).astype(BF)
    by_step = (row_at[:, None] % STEPS == jnp.arange(STEPS)[None]).astype(F32)
    high, low = split(my_rows(centered_s))
    spread_in = dot(by_cell, high) + dot(by_cell, low)
    spread_out = dot(by_cell, my_rows(proj_out))
    left_in = spread_in * jnp.dot(by_step, 1.0 + scale_s, precision=HIGH)
    left_out = spread_out * jnp.dot(by_step, gate_s, precision=HIGH)
    piece = cells * STEPS // samples
    part_in = dot(left_in.astype(BF), s_w1).astype(BF)
    part_out = dot_back(left_out.astype(BF), s_w2).astype(BF)
    part_shift = dot(shift_s.astype(BF), s_w1).astype(BF)
    step_of = (student_step[:, None] - 1 == jnp.arange(STEPS)[None]).astype(BF)
    part_shift = dot(step_of, part_shift).astype(BF).reshape(samples * piece, hidden // piece)
    gap = -hidden % 128
    parts = jnp.concatenate(
        [part_in, jnp.zeros((samples * piece, gap), BF), part_out, part_shift], axis=1
    ).reshape(samples, piece, -1)
    sums = jnp.sum(lax.all_to_all(parts, SAMPLE, 0, 0).astype(F32), axis=0)
    my_step = lax.dynamic_index_in_dim(student_step, sample, keepdims=False)
    both_wide = 2 * hidden + gap
    bias_s = sums[:, both_wide:].reshape(hidden)
    table = sums[:, :both_wide].astype(BF)
    chunk = cells // samples
    want = jnp.arange(samples * chunk)
    select = (
        (want[:, None] % chunk == jnp.arange(piece)[None] // STEPS)
        & (jnp.repeat(student_step - 1, chunk)[:, None] == jnp.arange(piece)[None] % STEPS)
    ).astype(BF)
    chosen = dot(select, table).astype(BF).reshape(samples, chunk, both_wide)
    mine = lax.all_to_all(chosen, SAMPLE, 0, 0).reshape(cells, both_wide)
    mat_in = mine[:, :hidden]
    mat_out = mine[:, hidden + gap :]
    d_w1, mine = lax.optimization_barrier((d_w1, mine))
    head_own = lax.all_gather(d_w1, SAMPLE, axis=0, tiled=True)

    sigma_s = my_step.astype(F32) * 0.25
    sigma_t = lax.dynamic_index_in_dim(sig_all_t, sample, keepdims=False)
    latent_in = noisy_latents[0]
    h0 = dot(latent_in, proj_s).astype(BF)
    _, inverse_s = normalize(h0.astype(F32))
    z_s = inverse_s * dot(latent_in, mat_in) + bias_s[None]
    a_s = gelu_tanh(z_s).astype(BF)
    velocity = dot_back(a_s, mat_out)
    mine_first = lax.dynamic_slice_in_dim(velocity, at_core * half, half, 0)
    other = lax.dynamic_slice_in_dim(velocity, (1 - at_core) * half, half, 0)
    velocity = mine_first + sibling(other)
    velocity = velocity + lax.ppermute(velocity, "y", [(0, 1), (1, 0), (2, 3), (3, 2)])
    velocity = velocity + lax.ppermute(velocity, "y", [(0, 2), (2, 0), (1, 3), (3, 1)])

    def my_half(values):
        return lax.dynamic_slice_in_dim(values, at_core * half, half, 0)

    def my_quarter(values):
        return lax.dynamic_slice_in_dim(values, at_y * quarter, quarter, 0)

    velocity = velocity + dot_back(my_half(h0), proj_out)
    latents = (my_half(latent_in).astype(F32) - sigma_s * velocity).astype(BF)
    noised = (
        (1.0 - sigma_t) * latents.astype(F32) + sigma_t * my_half(teacher_noise[0]).astype(F32)
    ).astype(BF)

    def both(values):
        other = sibling(values)
        first = jnp.where(at_core == 0, values, other)
        second = jnp.where(at_core == 0, other, values)
        return jnp.concatenate([first, second], axis=0)

    latents = both(latents)

    shifts = [mod_teacher[l, :width] for l in range(layers)]
    scales = [mod_teacher[l, width : 2 * width] for l in range(layers)]
    gates = [mod_teacher[l, 2 * width :] for l in range(layers)]
    proj_t_wide = proj_t.astype(F32)
    centered_t = proj_t_wide - jnp.mean(proj_t_wide, axis=1, keepdims=True)
    left_t = (centered_t * (1.0 + scales[0])).astype(BF)
    shift_t = jnp.broadcast_to(shifts[0][None], (8, width)).astype(BF)
    w1 = (t_w1[1], w1_sib)
    w2 = [(t_w2[l], w2_sib[l]) for l in range(layers)]
    head_weight = (head_own, sibling(head_own))
    head_out = (d_w2, d_w2_sib)
    mat_t = dot(left_t, t_w1[0])
    bias_t = dot(shift_t, t_w1[0])[:1]
    first_own = jnp.concatenate([mat_t, jnp.broadcast_to(bias_t, (8, hidden))], axis=0)
    first_all = (first_own, sibling(first_own))
    mat_t = [split(first[:cells]) for first in first_all]
    bias_t = [first[cells : cells + 1] for first in first_all]

    g_0 = dot(noised, proj_t).astype(BF)
    normed_0, inverse_0 = normalize(g_0.astype(F32))
    z_0 = [
        inverse_0 * (dot(noised, high) + dot(noised, low)) + bias
        for (high, low), bias in zip(mat_t, bias_t)
    ]
    y_0 = sum(dot(gelu_tanh(z).astype(BF), w) for z, w in zip(z_0, w2[0]))
    g_1_mine = (my_quarter(g_0).astype(F32) + gates[0] * scatter_y(y_0)).astype(BF)
    g_1 = gather_y(g_1_mine)
    normed_1, _ = normalize(g_1.astype(F32))
    u_1 = (normed_1 * (1.0 + scales[1]) + shifts[1]).astype(BF)
    z_1 = [dot(u_1, w) for w in w1]
    y_1 = sum(dot(gelu_tanh(z).astype(BF), w) for z, w in zip(z_1, w2[1]))
    g_2_mine = (g_1_mine.astype(F32) + gates[1] * scatter_y(y_1)).astype(BF)
    g_2 = gather_y(g_2_mine)
    normed_2, _ = normalize(g_2.astype(F32))

    picks = layer_pick[0]
    head_back = []
    scores = [jnp.zeros((half,), F32) for head in range(heads)]
    for layer, normed in enumerate((normed_1, normed_2)):
        quantised = normed.astype(BF)
        back = jnp.zeros((half, width), F32)
        for weight, out in zip(head_weight, head_out):
            e = dot(quantised, weight)
            active = jax.nn.silu(e)
            total = jnp.zeros((weight.shape[1],), F32)
            for head in range(heads):
                use = (picks[head] == layer).astype(F32)
                total = total - use * out[head]
                scores[head] = scores[head] + jnp.sum(active * (use * out[head])[None], axis=1)
            back = back + dot_back((total[None] * silu_slope(e)).astype(BF), weight)
        head_back.append(back)

    normed_2m, inverse_2m = normalize(g_2_mine.astype(F32))
    dg_2 = ln_back(scatter_y(head_back[1]), normed_2m, inverse_2m)
    dy_1 = gather_y((gates[1] * dg_2).astype(BF))
    du_1 = jnp.zeros((half, width), F32)
    for z, up, down in zip(z_1, w1, w2[1]):
        dz = (dot_back(dy_1, down) * gelu_slope(z)).astype(BF)
        du_1 = du_1 + dot_back(dz, up)
    normed_1m, inverse_1m = normalize(g_1_mine.astype(F32))
    dg_1 = dg_2 + ln_back(
        scatter_y(du_1 * (1.0 + scales[1]) + head_back[0]), normed_1m, inverse_1m
    )
    dy_0 = gather_y((gates[0] * dg_1).astype(BF))
    down_0 = jnp.zeros((half, cells), F32)
    for z, (high, low), down in zip(z_0, mat_t, w2[0]):
        dz = (dot_back(dy_0, down) * gelu_slope(z)).astype(BF)
        down_0 = down_0 + dot_back(dz, high) + dot_back(dz, low)
    direct = dot_back(dg_1.astype(BF), proj_t)
    direct = lax.dynamic_update_slice_in_dim(
        jnp.zeros((half, cells), F32), direct, at_y * quarter, 0
    )
    final = jnp.concatenate(
        [down_0, direct, jnp.stack(scores, axis=1), jnp.zeros((half, 128 - heads), F32)], axis=1
    )
    final = final + lax.ppermute(final, "y", [(0, 1), (1, 0), (2, 3), (3, 2)])
    final = final + lax.ppermute(final, "y", [(0, 2), (2, 0), (1, 3), (3, 1)])
    down_0, direct, scores = final[:, :cells], final[:, cells : 2 * cells], final[:, 2 * cells :]
    cross = inverse_0 * jnp.sum(noised.astype(F32) * down_0, axis=1, keepdims=True) / width
    normed_back = dot_back(normed_0.astype(BF), proj_t)
    grad = (1.0 - sigma_t) * (inverse_0 * (down_0 - normed_back * cross) + direct)
    result = jnp.concatenate([grad, scores[:, :cells]], axis=1)

    result = both(result)
    return (latents[None], result[:, cells : cells + heads].T[None], result[:, :cells][None])


def solution(mesh):
    names = list(mesh.axis_names)
    shape = list(mesh.devices.shape)
    at = names.index("tp")
    names[at : at + 1] = ["y", "core"]
    shape[at : at + 1] = [4, 2]
    fine = Mesh(mesh.devices.reshape(shape), tuple(names))
    placed = (
        P(SAMPLE, None, None),
        P(),
        P(),
        P(SAMPLE, None, None),
        P(SAMPLE, None),
        P(None, TP),
        P(None, TP),
        P(None, TP),
        P(SAMPLE, TP),
        P(SAMPLE, TP),
        P(TP, SAMPLE),
        P(None, SAMPLE, TP),
        P(None, None, TP),
        P(None, TP, None),
        P(SAMPLE, TP),
        P(None, TP),
    )
    return jax.shard_map(
        body,
        mesh=fine,
        in_specs=placed,
        out_specs=(P(SAMPLE, None, None), P(SAMPLE, None, None), P(SAMPLE, None, None)),
        check_vma=False,
    )
```

```python
import math

import jax
import jax.numpy as jnp
from jax import lax
from jax.experimental import pallas as pl
from jax.experimental.pallas import tpu as pltpu
from jax.sharding import Mesh
from jax.sharding import PartitionSpec as P

HIGH = lax.Precision.HIGHEST
SAMPLE = ("fsdp", "grp")
TP = ("y", "core")
STEPS = 4
BF = jnp.bfloat16
F32 = jnp.float32


def embed_block(times, width, block, start):
    half = width // 2
    column = start + jnp.arange(block)
    steps = jnp.where(column < half, column, column - half).astype(F32)
    freq = jnp.exp(-math.log(10000.0) * steps / half)
    angle = times[:, None] * freq[None, :]
    return jnp.where((column < half)[None, :], jnp.cos(angle), jnp.sin(angle))


def normalize(values):
    mean = jnp.mean(values, axis=-1, keepdims=True)
    centered = values - mean
    inverse = lax.rsqrt(jnp.mean(centered * centered, axis=-1, keepdims=True) + 1e-06)
    return (centered * inverse, inverse)


def ln_back(grad, normed, inverse):
    mean_grad = jnp.mean(grad, axis=-1, keepdims=True)
    mean_cross = jnp.mean(grad * normed, axis=-1, keepdims=True)
    return inverse * (grad - mean_grad - normed * mean_cross)


def gelu_tanh(values):
    inner = 0.7978845608 * (values + 0.044715 * values * values * values)
    return 0.5 * values * (1.0 + jnp.tanh(inner))


def gelu_both(values):
    inner = 0.7978845608 * (values + 0.044715 * values * values * values)
    tangent = jnp.tanh(inner)
    halved = 0.5 * (1.0 + tangent)
    slope = halved + 0.5 * values * (1.0 - tangent * tangent) * 0.7978845608 * (
        1.0 + 3.0 * 0.044715 * values * values
    )
    return values * halved, slope


def dot(left, right):
    return jnp.dot(left, right, preferred_element_type=F32)


def dot_back(left, right):
    return lax.dot_general(left, right, (((1,), (1,)), ((), ())), preferred_element_type=F32)


def split(values):
    high = values.astype(BF)
    return high, (values - high.astype(F32)).astype(BF)


def sibling(values):
    return lax.ppermute(values, "core", [(0, 1), (1, 0)])


def scatter_y(partial):
    rows = partial.shape[0] // 4
    parts = lax.all_to_all(partial.astype(BF).reshape(4, rows, -1), "y", 0, 0)
    return jnp.sum(parts.astype(F32), axis=0)


def gather_y(values):
    return lax.all_gather(values, "y", axis=0, tiled=True)


def cuts(extent, size=640):
    return [(at, min(size, extent - at)) for at in range(0, extent, size)]


def start_copies(plan, sems):
    copies = []
    for index, (source, target) in enumerate(plan):
        copy = pltpu.make_async_copy(source, target, sems.at[index])
        copy.start()
        copies.append(copy)
    return iter(copies)


def first_forward_kernel(x_ref, proj_ref, mat_ref, bias_ref, own, sib, y_ref, slope_ref, w_ref, acc_ref, sems):
    hidden, width = w_ref.shape[1:]
    plan = [
        (source.at[0, pl.ds(at, size)], w_ref.at[side, pl.ds(at, size)])
        for side, source in enumerate((own, sib))
        for at, size in cuts(hidden)
    ]
    copies = start_copies(plan, sems)
    x = x_ref[...]
    g_0 = dot(x, proj_ref[...]).astype(BF).astype(F32)
    centered = g_0 - jnp.mean(g_0, axis=1, keepdims=True)
    inverse = lax.rsqrt(jnp.mean(centered * centered, axis=1, keepdims=True) + 1e-06)
    for side in range(2):
        high, low = split(mat_ref[side])
        z = inverse * (dot(x, high) + dot(x, low)) + bias_ref[side]
        active, slope = gelu_both(z)
        slope_ref[side] = slope.astype(BF)
        active = active.astype(BF)
        for at, size in cuts(hidden):
            next(copies).wait()
            part = dot(active[:, at : at + size], w_ref[side, at : at + size, :])
            if side == 0 and at == 0:
                acc_ref[...] = part
            else:
                acc_ref[...] += part
    y_ref[...] = acc_ref[...].astype(BF)


def forward_kernel(
    g_ref, scale_ref, shift_ref, up_own, up_sib, down_own, down_sib, y_ref, slope_ref, up_ref, down_ref, acc_ref, sems
):
    width, hidden = up_ref.shape[1:]
    plan = [
        (source.at[pl.ds(at, size)], up_ref.at[side, pl.ds(at, size)])
        for side, source in enumerate((up_own.at[1], up_sib))
        for at, size in cuts(width)
    ] + [
        (source.at[1, pl.ds(at, size)], down_ref.at[side, pl.ds(at, size)])
        for side, source in enumerate((down_own, down_sib))
        for at, size in cuts(hidden)
    ]
    copies = start_copies(plan, sems)
    normed, _ = normalize(g_ref[...].astype(F32))
    u = (normed * (1.0 + scale_ref[...]) + shift_ref[...]).astype(BF)
    actives = []
    for side in range(2):
        z = None
        for at, size in cuts(width):
            next(copies).wait()
            part = dot(u[:, at : at + size], up_ref[side, at : at + size, :])
            z = part if z is None else z + part
        active, slope = gelu_both(z)
        slope_ref[side] = slope.astype(BF)
        actives.append(active.astype(BF))
    for side in range(2):
        for at, size in cuts(hidden):
            next(copies).wait()
            part = dot(actives[side][:, at : at + size], down_ref[side, at : at + size, :])
            if side == 0 and at == 0:
                acc_ref[...] = part
            else:
                acc_ref[...] += part
    y_ref[...] = acc_ref[...].astype(BF)


def backward_kernel(
    dy_ref, slope_ref, scale_ref, head_ref, up_own, up_sib, down_own, down_sib, out_ref, up_ref, down_ref, dz_ref, sems
):
    width, hidden = up_ref.shape[1:]
    plan = [
        (source.at[1, pl.ds(at, size)], down_ref.at[side, pl.ds(at, size)])
        for side, source in enumerate((down_own, down_sib))
        for at, size in cuts(hidden)
    ] + [
        (source.at[pl.ds(at, size)], up_ref.at[side, pl.ds(at, size)])
        for at, size in cuts(width)
        for side, source in enumerate((up_own.at[1], up_sib))
    ]
    copies = start_copies(plan, sems)
    dy = dy_ref[...]
    for side in range(2):
        for at, size in cuts(hidden):
            next(copies).wait()
            da = dot_back(dy, down_ref[side, at : at + size, :])
            dz_ref[side, :, at : at + size] = (
                da * slope_ref[side, :, at : at + size].astype(F32)
            ).astype(BF)
    dz = [dz_ref[side] for side in range(2)]
    for at, size in cuts(width):
        next(copies).wait()
        part = dot_back(dz[0], up_ref[0, at : at + size, :])
        next(copies).wait()
        part = part + dot_back(dz[1], up_ref[1, at : at + size, :])
        out_ref[:, at : at + size] = (
            part * (1.0 + scale_ref[:, at : at + size]) + head_ref[:, at : at + size].astype(F32)
        ).astype(BF)


def first_backward_kernel(dy_ref, slope_ref, mat_ref, own, sib, out_ref, w_ref, sems):
    hidden, width = w_ref.shape[1:]
    plan = [
        (source.at[0, pl.ds(at, size)], w_ref.at[side, pl.ds(at, size)])
        for side, source in enumerate((own, sib))
        for at, size in cuts(hidden)
    ]
    copies = start_copies(plan, sems)
    dy = dy_ref[...]
    total = None
    for side in range(2):
        high, low = split(mat_ref[side])
        for at, size in cuts(hidden):
            next(copies).wait()
            da = dot_back(dy, w_ref[side, at : at + size, :])
            dz = (da * slope_ref[side, :, at : at + size].astype(F32)).astype(BF)
            part = dot_back(dz, high[:, at : at + size]) + dot_back(dz, low[:, at : at + size])
            total = part if total is None else total + part
    out_ref[...] = total


def head_kernel(g_ref, use_ref, own_ref, sib_ref, back_ref, score_ref):
    normed, _ = normalize(g_ref[...].astype(F32))
    quantised = normed.astype(BF)
    back = None
    scores = None
    for side, weight_ref in enumerate((own_ref, sib_ref)):
        weight = weight_ref[...]
        e = dot(quantised, weight)
        sigm = 1.0 / (1.0 + jnp.exp(-e))
        active = e * sigm
        outs = use_ref[side]
        slope = sigm * (1.0 + e * (1.0 - sigm))
        part = dot_back((-(outs[0:1] + outs[1:2]) * slope).astype(BF), weight)
        back = part if back is None else back + part
        part = [jnp.sum(active * outs[head : head + 1], axis=1, keepdims=True) for head in range(2)]
        scores = part if scores is None else [old + new for old, new in zip(scores, part)]
    back_ref[...] = back.astype(BF)
    lane = lax.broadcasted_iota(jnp.int32, score_ref.shape, 1)
    score_ref[...] = jnp.where(lane == 0, scores[0], 0.0) + jnp.where(lane == 1, scores[1], 0.0)


WHOLE = pl.BlockSpec(memory_space=pltpu.VMEM)
FAR = pl.BlockSpec(memory_space=pl.ANY)
LIMIT = pltpu.CompilerParams(vmem_limit_bytes=48 * 2**20)


def first_forward(x, proj, mat, bias, own, sib):
    half = x.shape[0]
    _, hidden, width = own.shape
    return pl.pallas_call(
        first_forward_kernel,
        name="first_forward",
        out_shape=(
            jax.ShapeDtypeStruct((half, width), BF),
            jax.ShapeDtypeStruct((2, half, hidden), BF),
        ),
        in_specs=[WHOLE] * 4 + [FAR] * 2,
        out_specs=(WHOLE, WHOLE),
        scratch_shapes=[
            pltpu.VMEM((2, hidden, width), BF),
            pltpu.VMEM((half, width), F32),
            pltpu.SemaphoreType.DMA((2 * len(cuts(hidden)),)),
        ],
        compiler_params=LIMIT,
    )(x, proj, mat, bias, own, sib)


def forward(g, scale, shift, up_own, up_sib, down_own, down_sib):
    half, width = g.shape
    hidden = up_sib.shape[1]
    return pl.pallas_call(
        forward_kernel,
        name="forward",
        out_shape=(
            jax.ShapeDtypeStruct((half, width), BF),
            jax.ShapeDtypeStruct((2, half, hidden), BF),
        ),
        in_specs=[WHOLE] * 3 + [FAR] * 4,
        out_specs=(WHOLE, WHOLE),
        scratch_shapes=[
            pltpu.VMEM((2, width, hidden), BF),
            pltpu.VMEM((2, hidden, width), BF),
            pltpu.VMEM((half, width), F32),
            pltpu.SemaphoreType.DMA((2 * len(cuts(width)) + 2 * len(cuts(hidden)),)),
        ],
        compiler_params=LIMIT,
    )(g, scale, shift, up_own, up_sib, down_own, down_sib)


def backward(dy, slope, scale, head, up_own, up_sib, down_own, down_sib):
    half, width = dy.shape
    hidden = up_sib.shape[1]
    return pl.pallas_call(
        backward_kernel,
        name="backward",
        out_shape=jax.ShapeDtypeStruct((half, width), BF),
        in_specs=[WHOLE] * 4 + [FAR] * 4,
        out_specs=WHOLE,
        scratch_shapes=[
            pltpu.VMEM((2, width, hidden), BF),
            pltpu.VMEM((2, hidden, width), BF),
            pltpu.VMEM((2, half, hidden), BF),
            pltpu.SemaphoreType.DMA((2 * len(cuts(width)) + 2 * len(cuts(hidden)),)),
        ],
        compiler_params=LIMIT,
    )(dy, slope, scale, head, up_own, up_sib, down_own, down_sib)


def first_backward(dy, slope, mat, own, sib):
    half = dy.shape[0]
    _, hidden, width = own.shape
    return pl.pallas_call(
        first_backward_kernel,
        name="first_backward",
        out_shape=jax.ShapeDtypeStruct((half, mat.shape[1]), F32),
        in_specs=[WHOLE] * 3 + [FAR] * 2,
        out_specs=WHOLE,
        scratch_shapes=[
            pltpu.VMEM((2, hidden, width), BF),
            pltpu.SemaphoreType.DMA((2 * len(cuts(hidden)),)),
        ],
        compiler_params=LIMIT,
    )(dy, slope, mat, own, sib)


def head_pass(g, use, own, sib):
    half, width = g.shape
    return pl.pallas_call(
        head_kernel,
        name="head_pass",
        out_shape=(
            jax.ShapeDtypeStruct((half, width), BF),
            jax.ShapeDtypeStruct((half, 128), F32),
        ),
        in_specs=[WHOLE] * 4,
        out_specs=(WHOLE, WHOLE),
        compiler_params=LIMIT,
    )(g, use, own, sib)


def body(
    noisy_latents,
    student_step,
    teacher_step,
    teacher_noise,
    layer_pick,
    in_proj_s,
    in_proj_t,
    out_proj,
    s_mod,
    s_w1,
    s_w2,
    t_mod,
    t_w1,
    t_w2,
    d_w1,
    d_w2,
):
    cells = in_proj_s.shape[0]
    width = in_proj_s.shape[1] * 8
    samples = student_step.shape[0]
    layers = t_w1.shape[0]
    heads = d_w2.shape[0]
    seq = noisy_latents.shape[1]
    half = seq // 2
    quarter = half // 4
    rows = s_mod.shape[0]
    hidden = s_w1.shape[1]
    columns = in_proj_s.shape[1]
    sample = lax.axis_index(SAMPLE)
    at_y = lax.axis_index("y")
    at_core = lax.axis_index("core")
    start = sample * rows

    head_own = lax.all_gather(d_w1, SAMPLE, axis=0, tiled=True)

    sig_all_t = teacher_step.astype(F32) * 0.001
    sig_steps = (1 + jnp.arange(STEPS)).astype(F32) * 0.25
    cond_s = jax.nn.silu(embed_block(1000.0 * sig_steps, width, rows, start))
    cond_t = jax.nn.silu(embed_block(1000.0 * sig_all_t, width, rows, start))
    mod_s = jnp.dot(cond_s, s_mod.astype(F32), precision=HIGH)
    mod_t = [jnp.dot(cond_t, t_mod[l].astype(F32), precision=HIGH) for l in range(layers)]
    mod_part = jnp.concatenate(
        [jnp.stack(mod_t, axis=1), jnp.broadcast_to(mod_s[None], (samples,) + mod_s.shape)], axis=1
    ).astype(BF)
    mod_part = lax.all_to_all(mod_part, SAMPLE, 0, 0)
    mods = jnp.sum(mod_part.astype(F32), axis=0)
    kinds = layers + STEPS
    mods = mods.reshape(kinds * 3, columns).astype(BF)
    packed = jnp.concatenate([in_proj_s, in_proj_t, out_proj, mods], axis=0)
    packed = lax.all_gather(packed, TP, axis=0, tiled=False)
    mods = packed[:, 3 * cells :].astype(F32)
    mods = mods.reshape(8, kinds, 3, columns).transpose(1, 0, 2, 3).reshape(kinds, 3 * width)
    mod_teacher, mod_student = mods[:layers], mods[layers:]
    packed = packed[:, : 3 * cells].transpose(1, 0, 2).reshape(3 * cells, width)
    proj_s, proj_t, proj_out = packed[:cells], packed[cells : 2 * cells], packed[2 * cells :]

    t_w1_last, t_w2_all, mod_teacher = lax.optimization_barrier((t_w1[1], t_w2, mod_teacher))
    w2_sib = sibling(t_w2_all)
    w1_sib = sibling(t_w1_last)
    d_w2_sib = sibling(d_w2)

    def my_rows(values):
        return lax.dynamic_slice_in_dim(values, start, rows, values.ndim - 1)

    proj_s_wide = proj_s.astype(F32)
    centered_s = proj_s_wide - jnp.mean(proj_s_wide, axis=1, keepdims=True)
    block_s = my_rows(mod_student.reshape(STEPS, 3, width))
    shift_s, scale_s, gate_s = block_s[:, 0], block_s[:, 1], block_s[:, 2]
    row_at = jnp.arange(cells * STEPS)
    by_cell = (row_at[:, None] // STEPS == jnp.arange(cells)[None]).astype(BF)
    by_step = (row_at[:, None] % STEPS == jnp.arange(STEPS)[None]).astype(F32)
    high, low = split(my_rows(centered_s))
    spread_in = dot(by_cell, high) + dot(by_cell, low)
    spread_out = dot(by_cell, my_rows(proj_out))
    left_in = spread_in * jnp.dot(by_step, 1.0 + scale_s, precision=HIGH)
    left_out = spread_out * jnp.dot(by_step, gate_s, precision=HIGH)
    piece = cells * STEPS // samples
    part_in = dot(left_in.astype(BF), s_w1).astype(BF)
    part_out = dot_back(left_out.astype(BF), s_w2).astype(BF)
    part_shift = dot(shift_s.astype(BF), s_w1).astype(BF)
    step_of = (student_step[:, None] - 1 == jnp.arange(STEPS)[None]).astype(BF)
    part_shift = dot(step_of, part_shift).astype(BF).reshape(samples * piece, hidden // piece)
    gap = -hidden % 128
    parts = jnp.concatenate(
        [part_in, jnp.zeros((samples * piece, gap), BF), part_out, part_shift], axis=1
    ).reshape(samples, piece, -1)
    sums = jnp.sum(lax.all_to_all(parts, SAMPLE, 0, 0).astype(F32), axis=0)
    my_step = lax.dynamic_index_in_dim(student_step, sample, keepdims=False)
    both_wide = 2 * hidden + gap
    bias_s = sums[:, both_wide:].reshape(hidden)
    table = sums[:, :both_wide].astype(BF)
    chunk = cells // samples
    want = jnp.arange(samples * chunk)
    select = (
        (want[:, None] % chunk == jnp.arange(piece)[None] // STEPS)
        & (jnp.repeat(student_step - 1, chunk)[:, None] == jnp.arange(piece)[None] % STEPS)
    ).astype(BF)
    chosen = dot(select, table).astype(BF).reshape(samples, chunk, both_wide)
    mine = lax.all_to_all(chosen, SAMPLE, 0, 0).reshape(cells, both_wide)
    mat_in = mine[:, :hidden]
    mat_out = mine[:, hidden + gap :]

    sigma_s = my_step.astype(F32) * 0.25
    sigma_t = lax.dynamic_index_in_dim(sig_all_t, sample, keepdims=False)
    latent_in = noisy_latents[0]
    h0 = dot(latent_in, proj_s).astype(BF)
    _, inverse_s = normalize(h0.astype(F32))
    z_s = inverse_s * dot(latent_in, mat_in) + bias_s[None]
    a_s = gelu_tanh(z_s).astype(BF)
    velocity = dot_back(a_s, mat_out)
    mine_first = lax.dynamic_slice_in_dim(velocity, at_core * half, half, 0)
    other = lax.dynamic_slice_in_dim(velocity, (1 - at_core) * half, half, 0)
    velocity = mine_first + sibling(other)
    velocity = velocity + lax.ppermute(velocity, "y", [(0, 1), (1, 0), (2, 3), (3, 2)])
    velocity = velocity + lax.ppermute(velocity, "y", [(0, 2), (2, 0), (1, 3), (3, 1)])

    def my_half(values):
        return lax.dynamic_slice_in_dim(values, at_core * half, half, 0)

    def my_quarter(values):
        return lax.dynamic_slice_in_dim(values, at_y * quarter, quarter, 0)

    velocity = velocity + dot_back(my_half(h0), proj_out)
    latents = (my_half(latent_in).astype(F32) - sigma_s * velocity).astype(BF)
    noised = (
        (1.0 - sigma_t) * latents.astype(F32) + sigma_t * my_half(teacher_noise[0]).astype(F32)
    ).astype(BF)

    def both(values):
        other = sibling(values)
        first = jnp.where(at_core == 0, values, other)
        second = jnp.where(at_core == 0, other, values)
        return jnp.concatenate([first, second], axis=0)

    latents = both(latents)

    shifts = [mod_teacher[l, :width] for l in range(layers)]
    scales = [mod_teacher[l, width : 2 * width] for l in range(layers)]
    gates = [mod_teacher[l, 2 * width :] for l in range(layers)]
    proj_t_wide = proj_t.astype(F32)
    centered_t = proj_t_wide - jnp.mean(proj_t_wide, axis=1, keepdims=True)
    left_t = (centered_t * (1.0 + scales[0])).astype(BF)
    shift_t = jnp.broadcast_to(shifts[0][None], (8, width)).astype(BF)
    head_sib = sibling(head_own)
    mat_t = dot(left_t, t_w1[0])
    bias_t = dot(shift_t, t_w1[0])[:1]
    first_own = jnp.concatenate([mat_t, jnp.broadcast_to(bias_t, (8, hidden))], axis=0)
    first_all = jnp.stack([first_own, sibling(first_own)])
    mat_t, bias_t = first_all[:, :cells], first_all[:, cells : cells + 1]

    y_0, slope_0 = first_forward(noised, proj_t, mat_t, bias_t, t_w2, w2_sib)
    g_0 = dot(noised, proj_t).astype(BF)
    normed_0, inverse_0 = normalize(g_0.astype(F32))
    g_1_mine = (my_quarter(g_0).astype(F32) + gates[0] * scatter_y(y_0)).astype(BF)
    g_1 = gather_y(g_1_mine)
    y_1, slope_1 = forward(
        g_1, scales[1][None], shifts[1][None], t_w1, w1_sib, t_w2, w2_sib
    )
    g_2_mine = (g_1_mine.astype(F32) + gates[1] * scatter_y(y_1)).astype(BF)
    g_2 = gather_y(g_2_mine)

    outs = jnp.stack([d_w2, d_w2_sib])
    use = [outs * (layer_pick[0] == layer).astype(F32)[None, :, None] for layer in range(layers)]
    head_back_1, scores_1 = head_pass(g_1, use[0], head_own, head_sib)
    head_back_2, scores_2 = head_pass(g_2, use[1], head_own, head_sib)

    normed_2m, inverse_2m = normalize(g_2_mine.astype(F32))
    dg_2 = ln_back(scatter_y(head_back_2), normed_2m, inverse_2m)
    dy_1 = gather_y((gates[1] * dg_2).astype(BF))
    du_1 = backward(
        dy_1, slope_1, scales[1][None], head_back_1, t_w1, w1_sib, t_w2, w2_sib
    )
    normed_1m, inverse_1m = normalize(g_1_mine.astype(F32))
    dg_1 = dg_2 + ln_back(scatter_y(du_1), normed_1m, inverse_1m)
    dy_0 = gather_y((gates[0] * dg_1).astype(BF))
    down_0 = first_backward(dy_0, slope_0, mat_t, t_w2, w2_sib)
    direct = dot_back(dg_1.astype(BF), proj_t)
    direct = lax.dynamic_update_slice_in_dim(
        jnp.zeros((half, cells), F32), direct, at_y * quarter, 0
    )
    final = jnp.concatenate(
        [down_0, direct, scores_1 + scores_2], axis=1
    )
    final = final + lax.ppermute(final, "y", [(0, 1), (1, 0), (2, 3), (3, 2)])
    final = final + lax.ppermute(final, "y", [(0, 2), (2, 0), (1, 3), (3, 1)])
    down_0, direct, scores = final[:, :cells], final[:, cells : 2 * cells], final[:, 2 * cells :]
    cross = inverse_0 * jnp.sum(noised.astype(F32) * down_0, axis=1, keepdims=True) / width
    normed_back = dot_back(normed_0.astype(BF), proj_t)
    grad = (1.0 - sigma_t) * (inverse_0 * (down_0 - normed_back * cross) + direct)
    result = jnp.concatenate([grad, scores[:, :cells]], axis=1)

    result = both(result)
    return (latents[None], result[:, cells : cells + heads].T[None], result[:, :cells][None])


def solution(mesh):
    names = list(mesh.axis_names)
    shape = list(mesh.devices.shape)
    at = names.index("tp")
    names[at : at + 1] = ["y", "core"]
    shape[at : at + 1] = [4, 2]
    fine = Mesh(mesh.devices.reshape(shape), tuple(names))
    placed = (
        P(SAMPLE, None, None),
        P(),
        P(),
        P(SAMPLE, None, None),
        P(SAMPLE, None),
        P(None, TP),
        P(None, TP),
        P(None, TP),
        P(SAMPLE, TP),
        P(SAMPLE, TP),
        P(TP, SAMPLE),
        P(None, SAMPLE, TP),
        P(None, None, TP),
        P(None, TP, None),
        P(SAMPLE, TP),
        P(None, TP),
    )
    return jax.shard_map(
        body,
        mesh=fine,
        in_specs=placed,
        out_specs=(P(SAMPLE, None, None), P(SAMPLE, None, None), P(SAMPLE, None, None)),
        check_vma=False,
    )
```

```python
import functools
import math

import jax
import jax.numpy as jnp
from jax import lax
from jax.experimental import pallas as pl
from jax.experimental.pallas import tpu as pltpu
from jax.sharding import Mesh
from jax.sharding import PartitionSpec as P

HIGH = lax.Precision.HIGHEST
SAMPLE = ("fsdp", "grp")
TP = ("y", "core")
STEPS = 4
LAYERS = 2
BF = jnp.bfloat16
F32 = jnp.float32


def embed_block(times, width, block, start):
    half = width // 2
    column = start + jnp.arange(block)
    steps = jnp.where(column < half, column, column - half).astype(F32)
    freq = jnp.exp(-math.log(10000.0) * steps / half)
    angle = times[:, None] * freq[None, :]
    return jnp.where((column < half)[None, :], jnp.cos(angle), jnp.sin(angle))


def normalize(values):
    mean = jnp.mean(values, axis=-1, keepdims=True)
    centered = values - mean
    inverse = lax.rsqrt(jnp.mean(centered * centered, axis=-1, keepdims=True) + 1e-06)
    return (centered * inverse, inverse)


def ln_back(grad, normed, inverse):
    mean_grad = jnp.mean(grad, axis=-1, keepdims=True)
    mean_cross = jnp.mean(grad * normed, axis=-1, keepdims=True)
    return inverse * (grad - mean_grad - normed * mean_cross)


def gelu_both(values):
    inner = 0.7978845608 * (values + 0.044715 * values * values * values)
    tangent = jnp.tanh(inner)
    halved = 0.5 * (1.0 + tangent)
    slope = halved + 0.5 * values * (1.0 - tangent * tangent) * 0.7978845608 * (
        1.0 + 3.0 * 0.044715 * values * values
    )
    return values * halved, slope


def dot(left, right):
    return jnp.dot(left, right, preferred_element_type=F32)


def dot_back(left, right):
    return lax.dot_general(left, right, (((1,), (1,)), ((), ())), preferred_element_type=F32)


def split(values):
    high = values.astype(BF)
    return high, (values - high.astype(F32)).astype(BF)


def sibling(values):
    return lax.ppermute(values, "core", [(0, 1), (1, 0)])


def scatter_y(partial):
    rows = partial.shape[0] // 4
    parts = lax.all_to_all(partial.astype(BF).reshape(4, rows, -1), "y", 0, 0)
    return jnp.sum(parts.astype(F32), axis=0)


def gather_y(values):
    return lax.all_gather(values, "y", axis=0, tiled=True)


def resident_kernel(layer, own, sib, out_ref, sems):
    copies = [
        pltpu.make_async_copy(source.at[layer], out_ref.at[side], sems.at[side])
        for side, source in enumerate((own, sib))
    ]
    for copy in copies:
        copy.start()
    for copy in copies:
        copy.wait()


def product_kernel(at_ref, packed_ref, w1_ref, w2_ref, out_ref, bias_ref):
    blocks, _, columns = packed_ref.shape
    rows, hidden = w1_ref.shape
    cells = out_ref.shape[0] // STEPS
    pick_row = lax.broadcasted_iota(jnp.int32, (columns, rows), 0)
    pick_col = lax.broadcasted_iota(jnp.int32, (columns, rows), 1)
    mine = (pick_row == pick_col + rows * at_ref[1]).astype(BF)
    total = jnp.zeros((cells, columns), F32)
    for block in range(blocks):
        total = total + packed_ref[block, :cells, :].astype(F32)
    mean = jnp.sum(total, axis=1, keepdims=True) / (blocks * columns)
    local = packed_ref[at_ref[0]]
    centered = dot(local[:cells], mine) - mean
    out_rows = dot(local[2 * cells : 3 * cells], mine).astype(BF)

    def modulation(index):
        block = packed_ref[at_ref[2 * index + 2]][3 * cells :]
        kind = lax.broadcasted_iota(jnp.int32, (8, block.shape[0]), 0)
        row = lax.broadcasted_iota(jnp.int32, (8, block.shape[0]), 1)
        want = (row == 3 * (kind + LAYERS) + at_ref[2 * index + 3]) & (kind < STEPS)
        return dot(dot(want.astype(BF), block).astype(BF), mine).astype(BF)

    shift, scale, gate = modulation(0), modulation(1), modulation(2)
    cell_row = lax.broadcasted_iota(jnp.int32, (cells * STEPS, cells), 0)
    cell_col = lax.broadcasted_iota(jnp.int32, (cells * STEPS, cells), 1)
    by_cell = (cell_row // STEPS == cell_col).astype(BF)
    step_row = lax.broadcasted_iota(jnp.int32, (cells * STEPS, 8), 0)
    step_col = lax.broadcasted_iota(jnp.int32, (cells * STEPS, 8), 1)
    by_step = (step_row % STEPS == step_col).astype(BF)
    high, low = split(centered)
    left_in = (dot(by_cell, high) + dot(by_cell, low)) * (1.0 + dot(by_step, scale))
    left_out = dot(by_cell, out_rows) * dot(by_step, gate)
    gap = -hidden % 128
    out_ref[:, :hidden] = dot(left_in.astype(BF), w1_ref[...]).astype(BF)
    out_ref[:, hidden : hidden + gap] = jnp.zeros((cells * STEPS, gap), BF)
    out_ref[:, hidden + gap :] = dot(left_out.astype(BF), w2_ref[...]).astype(BF)
    bias_ref[...] = dot(shift, w1_ref[...]).astype(BF)


def select_kernel(parts_ref, pick_ref, pick_bias_ref, bias_ref, out_ref):
    hidden = bias_ref.shape[1]
    total = parts_ref[0].astype(F32)
    for source in range(1, parts_ref.shape[0]):
        total = total + parts_ref[source].astype(F32)
    chosen = dot(pick_ref[...], total.astype(BF))
    out_ref[...] = chosen.astype(BF)
    out_ref[:, :hidden] = (chosen[:, :hidden] + dot(pick_bias_ref[...], bias_ref[...])).astype(BF)


def student_kernel(x_ref, inverse_ref, mat_ref, out_ref):
    cells = x_ref.shape[1]
    lanes, wide = mat_ref.shape
    hidden = wide // 2 - (wide // 2) % 64
    gap = wide - 2 * hidden
    group = lanes * 4 // cells
    row = lax.broadcasted_iota(jnp.int32, (cells, lanes), 0)
    col = lax.broadcasted_iota(jnp.int32, (cells, lanes), 1)
    spread = (col == group * (row // 4) + row % 4).astype(BF)
    bias_col = lax.broadcasted_iota(jnp.int32, (8, lanes), 1)
    bias = dot((bias_col % group == 4).astype(BF), mat_ref[:, :hidden])[:1]
    x = dot(x_ref[...], spread).astype(BF)
    z = inverse_ref[...] * dot(x, mat_ref[:, :hidden]) + bias
    active = gelu_both(z)[0].astype(BF)
    high, low = split(dot_back(active, mat_ref[:, hidden + gap :]))
    out_ref[...] = dot_back(high, spread) + dot_back(low, spread)


def first_forward_kernel(x_ref, proj_ref, mat_ref, bias_ref, down_ref, y_ref, slope_ref):
    x = x_ref[...]
    g_0 = dot(x, proj_ref[...]).astype(BF).astype(F32)
    centered = g_0 - jnp.mean(g_0, axis=1, keepdims=True)
    inverse = lax.rsqrt(jnp.mean(centered * centered, axis=1, keepdims=True) + 1e-06)
    actives = []
    for side in range(2):
        high, low = split(mat_ref[side])
        active, slope = gelu_both(inverse * (dot(x, high) + dot(x, low)) + bias_ref[side])
        slope_ref[side] = slope.astype(BF)
        actives.append(active.astype(BF))
    y_ref[...] = (dot(actives[0], down_ref[0]) + dot(actives[1], down_ref[1])).astype(BF)


def forward_kernel(g_ref, scale_ref, shift_ref, up_ref, down_ref, y_ref, slope_ref):
    normed, _ = normalize(g_ref[...].astype(F32))
    u = (normed * (1.0 + scale_ref[...]) + shift_ref[...]).astype(BF)
    actives = []
    for side in range(2):
        active, slope = gelu_both(dot_back(u, up_ref[side]))
        slope_ref[side] = slope.astype(BF)
        actives.append(active.astype(BF))
    y_ref[...] = (dot(actives[0], down_ref[0]) + dot(actives[1], down_ref[1])).astype(BF)


def backward_kernel(dy_ref, slope_ref, scale_ref, head_ref, up_ref, down_ref, out_ref):
    dy = dy_ref[...]
    dz = [
        (dot_back(dy, down_ref[side]) * slope_ref[side].astype(F32)).astype(BF) for side in range(2)
    ]
    du = dot(dz[0], up_ref[0]) + dot(dz[1], up_ref[1])
    out_ref[...] = (du * (1.0 + scale_ref[...]) + head_ref[...].astype(F32)).astype(BF)


def first_backward_kernel(dy_ref, slope_ref, mat_ref, down_ref, out_ref):
    dy = dy_ref[...]
    total = None
    for side in range(2):
        high, low = split(mat_ref[side])
        dz = (dot_back(dy, down_ref[side]) * slope_ref[side].astype(F32)).astype(BF)
        part = dot_back(dz, high) + dot_back(dz, low)
        total = part if total is None else total + part
    out_ref[...] = total


def head_kernel(g_ref, use_ref, own_ref, sib_ref, back_ref, score_ref):
    normed, _ = normalize(g_ref[...].astype(F32))
    quantised = normed.astype(BF)
    back = None
    scores = None
    for side, weight_ref in enumerate((own_ref, sib_ref)):
        weight = weight_ref[...]
        e = dot(quantised, weight)
        sigm = 1.0 / (1.0 + jnp.exp(-e))
        active = e * sigm
        outs = use_ref[side]
        slope = sigm * (1.0 + e * (1.0 - sigm))
        part = dot_back((-(outs[0:1] + outs[1:2]) * slope).astype(BF), weight)
        back = part if back is None else back + part
        part = [jnp.sum(active * outs[head : head + 1], axis=1, keepdims=True) for head in range(2)]
        scores = part if scores is None else [old + new for old, new in zip(scores, part)]
    back_ref[...] = back.astype(BF)
    lane = lax.broadcasted_iota(jnp.int32, score_ref.shape, 1)
    score_ref[...] = jnp.where(lane == 0, scores[0], 0.0) + jnp.where(lane == 1, scores[1], 0.0)


WHOLE = pl.BlockSpec(memory_space=pltpu.VMEM)
FAR = pl.BlockSpec(memory_space=pltpu.HBM)


def here(kernel, name, out_shape, operands, scalars=0):
    many = isinstance(out_shape, tuple)
    return pl.pallas_call(
        kernel,
        name=name,
        out_shape=out_shape,
        in_specs=[pl.BlockSpec(memory_space=pltpu.SMEM)] * scalars
        + [WHOLE] * (len(operands) - scalars),
        out_specs=(WHOLE,) * len(out_shape) if many else WHOLE,
        compiler_params=pltpu.CompilerParams(vmem_limit_bytes=20 * 2**20),
    )(*operands)


def resident(layer, own, sib):
    return pl.pallas_call(
        functools.partial(resident_kernel, layer),
        name="resident",
        out_shape=pltpu.VMEM((2,) + own.shape[1:], own.dtype),
        in_specs=[FAR, FAR],
        out_specs=WHOLE,
        scratch_shapes=[pltpu.SemaphoreType.DMA((2,))],
        compiler_params=pltpu.CompilerParams(vmem_limit_bytes=8 * 2**20),
    )(own, sib)


def body(
    noisy_latents,
    student_step,
    teacher_step,
    teacher_noise,
    layer_pick,
    in_proj_s,
    in_proj_t,
    out_proj,
    s_mod,
    s_w1,
    s_w2,
    t_mod,
    t_w1,
    t_w2,
    d_w1,
    d_w2,
):
    cells = in_proj_s.shape[0]
    width = in_proj_s.shape[1] * 8
    samples = student_step.shape[0]
    layers = t_w1.shape[0]
    heads = d_w2.shape[0]
    seq = noisy_latents.shape[1]
    half = seq // 2
    quarter = half // 4
    rows = s_mod.shape[0]
    hidden = s_w1.shape[1]
    columns = in_proj_s.shape[1]
    sample = lax.axis_index(SAMPLE)
    at_y = lax.axis_index("y")
    at_core = lax.axis_index("core")
    start = sample * rows

    sig_all_t = teacher_step.astype(F32) * 0.001
    sig_steps = (1 + jnp.arange(STEPS)).astype(F32) * 0.25
    cond_s = jax.nn.silu(embed_block(1000.0 * sig_steps, width, rows, start))
    cond_t = jax.nn.silu(embed_block(1000.0 * sig_all_t, width, rows, start))
    mod_s = jnp.dot(cond_s, s_mod.astype(F32), precision=HIGH)
    mod_t = [jnp.dot(cond_t, t_mod[l].astype(F32), precision=HIGH) for l in range(layers)]
    mod_part = jnp.concatenate(
        [jnp.stack(mod_t, axis=1), jnp.broadcast_to(mod_s[None], (samples,) + mod_s.shape)], axis=1
    ).astype(BF)
    mod_part = lax.all_to_all(mod_part, SAMPLE, 0, 0)
    mods = jnp.sum(mod_part.astype(F32), axis=0)
    kinds = layers + STEPS
    mods = mods.reshape(kinds * 3, columns).astype(BF)
    packed = jnp.concatenate([in_proj_s, in_proj_t, out_proj, mods], axis=0)
    gathered = lax.all_gather(packed, TP, axis=0, tiled=False)

    block = lax.axis_index(SAMPLE) * rows // columns
    places = [block, sample * rows // rows % (columns // rows)]
    for offset in (0, 8, 16):
        places += [(block + offset) // 3, (block + offset) % 3]
    gap = -hidden % 128
    both_wide = 2 * hidden + gap
    parts, part_bias = here(
        product_kernel,
        "product",
        (
            jax.ShapeDtypeStruct((cells * STEPS, both_wide), BF),
            jax.ShapeDtypeStruct((8, hidden), BF),
        ),
        (jnp.stack(places).astype(jnp.int32), gathered, s_w1, s_w2.T),
        scalars=1,
    )
    piece = cells * STEPS // samples
    chunk = cells // samples
    t_w1 = jnp.swapaxes(t_w1, 1, 2)
    parts, gathered, t_w1, t_w2 = lax.optimization_barrier((parts, gathered, t_w1, t_w2))
    received = lax.all_to_all(parts.reshape(samples, piece, both_wide), SAMPLE, 0, 0)

    w2_sib = sibling(t_w2)
    w1_sib = sibling(t_w1)

    at_row = jnp.arange(samples * 8)
    step_at = jnp.repeat(student_step - 1, 8)
    pick = (
        ((at_row % 8 * STEPS + step_at)[:, None] == jnp.arange(piece)[None])
        & (at_row % 8 < chunk)[:, None]
    ).astype(BF)
    pick_bias = ((step_at[:, None] == jnp.arange(8)[None]) & (at_row % 8 == chunk)[:, None]).astype(BF)
    chosen = here(
        select_kernel,
        "select",
        jax.ShapeDtypeStruct((samples * 8, both_wide), BF),
        (received, pick, pick_bias, part_bias),
    )
    spare = -columns % 128
    head_block = jnp.pad(d_w1, ((0, 0), (0, spare)))
    head_block, chosen = lax.optimization_barrier((head_block, chosen))
    head_own = lax.all_gather(head_block, SAMPLE, axis=0, tiled=True)
    mine = lax.all_to_all(chosen.reshape(samples, 8, both_wide), SAMPLE, 0, 0)
    mine = mine.reshape(samples * 8, both_wide)
    my_step = lax.dynamic_index_in_dim(student_step, sample, keepdims=False)

    mods = gathered[:, 3 * cells :].astype(F32)
    mods = mods.reshape(8, kinds, 3, columns).transpose(1, 0, 2, 3).reshape(kinds, 3 * width)
    mod_teacher = mods[:layers]
    packed = gathered[:, : 3 * cells].transpose(1, 0, 2).reshape(3 * cells, width)
    proj_s, proj_t, proj_out = packed[:cells], packed[cells : 2 * cells], packed[2 * cells :]

    sigma_s = my_step.astype(F32) * 0.25
    sigma_t = lax.dynamic_index_in_dim(sig_all_t, sample, keepdims=False)
    latent_in = noisy_latents[0]
    h0 = dot(latent_in, proj_s).astype(BF)
    _, inverse_s = normalize(h0.astype(F32))
    velocity = here(
        student_kernel,
        "student",
        jax.ShapeDtypeStruct((seq, cells), F32),
        (latent_in, inverse_s, mine),
    )
    mine_first = lax.dynamic_slice_in_dim(velocity, at_core * half, half, 0)
    other = lax.dynamic_slice_in_dim(velocity, (1 - at_core) * half, half, 0)
    velocity = mine_first + sibling(other)
    velocity = velocity + lax.ppermute(velocity, "y", [(0, 1), (1, 0), (2, 3), (3, 2)])
    velocity = velocity + lax.ppermute(velocity, "y", [(0, 2), (2, 0), (1, 3), (3, 1)])

    def my_half(values):
        return lax.dynamic_slice_in_dim(values, at_core * half, half, 0)

    def my_quarter(values):
        return lax.dynamic_slice_in_dim(values, at_y * quarter, quarter, 0)

    velocity = velocity + dot_back(my_half(h0), proj_out)
    latents = (my_half(latent_in).astype(F32) - sigma_s * velocity).astype(BF)
    noised = (
        (1.0 - sigma_t) * latents.astype(F32) + sigma_t * my_half(teacher_noise[0]).astype(F32)
    ).astype(BF)

    def both(values):
        other = sibling(values)
        first = jnp.where(at_core == 0, values, other)
        second = jnp.where(at_core == 0, other, values)
        return jnp.concatenate([first, second], axis=0)

    latents = both(latents)

    shifts = [mod_teacher[l, :width] for l in range(layers)]
    scales = [mod_teacher[l, width : 2 * width] for l in range(layers)]
    gates = [mod_teacher[l, 2 * width :] for l in range(layers)]
    proj_t_wide = proj_t.astype(F32)
    centered_t = proj_t_wide - jnp.mean(proj_t_wide, axis=1, keepdims=True)
    left_t = (centered_t * (1.0 + scales[0])).astype(BF)
    shift_t = jnp.broadcast_to(shifts[0][None], (8, width)).astype(BF)
    head_sib = sibling(head_own)
    d_w2_sib = sibling(d_w2)
    mat_t = dot_back(left_t, t_w1[0])
    bias_t = dot_back(shift_t, t_w1[0])[:1]
    first_own = jnp.concatenate([mat_t, jnp.broadcast_to(bias_t, (8, hidden))], axis=0)
    first_all = jnp.stack([first_own, sibling(first_own)])
    mat_t, bias_t = first_all[:, :cells], first_all[:, cells : cells + 1]

    down_first = resident(0, t_w2, w2_sib)
    up_last = resident(1, t_w1, w1_sib)
    down_last = resident(1, t_w2, w2_sib)

    activity = (
        jax.ShapeDtypeStruct((half, width), BF),
        jax.ShapeDtypeStruct((2, half, hidden), BF),
    )
    y_0, slope_0 = here(
        first_forward_kernel, "first_forward", activity, (noised, proj_t, mat_t, bias_t, down_first)
    )
    g_0 = dot(noised, proj_t).astype(BF)
    normed_0, inverse_0 = normalize(g_0.astype(F32))
    g_1_mine = (my_quarter(g_0).astype(F32) + gates[0] * scatter_y(y_0)).astype(BF)
    g_1 = gather_y(g_1_mine)
    y_1, slope_1 = here(
        forward_kernel,
        "forward",
        activity,
        (g_1, scales[1][None], shifts[1][None], up_last, down_last),
    )
    g_2_mine = (g_1_mine.astype(F32) + gates[1] * scatter_y(y_1)).astype(BF)
    g_2 = gather_y(g_2_mine)

    outs = jnp.pad(jnp.stack([d_w2, d_w2_sib]), ((0, 0), (0, 0), (0, spare)))
    use = [outs * (layer_pick[0] == layer).astype(F32)[None, :, None] for layer in range(layers)]
    head_shapes = (
        jax.ShapeDtypeStruct((half, width), BF),
        jax.ShapeDtypeStruct((half, 128), F32),
    )
    head_back_2, scores_2 = here(
        head_kernel, "head_last", head_shapes, (g_2, use[1], head_own, head_sib)
    )
    g_1, head_back_2 = lax.optimization_barrier((g_1, head_back_2))
    head_back_1, scores_1 = here(
        head_kernel, "head_first", head_shapes, (g_1, use[0], head_own, head_sib)
    )
    scores = (scores_1 + scores_2)[:, :heads].T
    scores = scores + lax.ppermute(scores, "y", [(0, 1), (1, 0), (2, 3), (3, 2)])
    scores = scores + lax.ppermute(scores, "y", [(0, 2), (2, 0), (1, 3), (3, 1)])
    scores_other = sibling(scores)
    scores = jnp.concatenate(
        [jnp.where(at_core == 0, scores, scores_other), jnp.where(at_core == 0, scores_other, scores)],
        axis=1,
    )

    normed_2m, inverse_2m = normalize(g_2_mine.astype(F32))
    dg_2 = ln_back(scatter_y(head_back_2), normed_2m, inverse_2m)
    dy_1 = gather_y((gates[1] * dg_2).astype(BF))
    du_1 = here(
        backward_kernel,
        "backward",
        jax.ShapeDtypeStruct((half, width), BF),
        (dy_1, slope_1, scales[1][None], head_back_1, up_last, down_last),
    )
    normed_1m, inverse_1m = normalize(g_1_mine.astype(F32))
    dg_1 = dg_2 + ln_back(scatter_y(du_1), normed_1m, inverse_1m)
    dy_0 = gather_y((gates[0] * dg_1).astype(BF))
    down_0 = here(
        first_backward_kernel,
        "first_backward",
        jax.ShapeDtypeStruct((half, cells), F32),
        (dy_0, slope_0, mat_t, down_first),
    )
    direct = dot_back(dg_1.astype(BF), proj_t)
    direct = lax.dynamic_update_slice_in_dim(
        jnp.zeros((half, cells), F32), direct, at_y * quarter, 0
    )
    final = jnp.concatenate([down_0, direct], axis=1)
    final = final + lax.ppermute(final, "y", [(0, 1), (1, 0), (2, 3), (3, 2)])
    final = final + lax.ppermute(final, "y", [(0, 2), (2, 0), (1, 3), (3, 1)])
    down_0, direct = final[:, :cells], final[:, cells:]
    cross = inverse_0 * jnp.sum(noised.astype(F32) * down_0, axis=1, keepdims=True) / width
    normed_back = dot_back(normed_0.astype(BF), proj_t)
    grad = (1.0 - sigma_t) * (inverse_0 * (down_0 - normed_back * cross) + direct)
    return (latents[None], scores[None], both(grad)[None])


def solution(mesh):
    names = list(mesh.axis_names)
    shape = list(mesh.devices.shape)
    at = names.index("tp")
    names[at : at + 1] = ["y", "core"]
    shape[at : at + 1] = [4, 2]
    fine = Mesh(mesh.devices.reshape(shape), tuple(names))
    placed = (
        P(SAMPLE, None, None),
        P(),
        P(),
        P(SAMPLE, None, None),
        P(SAMPLE, None),
        P(None, TP),
        P(None, TP),
        P(None, TP),
        P(SAMPLE, TP),
        P(SAMPLE, TP),
        P(TP, SAMPLE),
        P(None, SAMPLE, TP),
        P(None, None, TP),
        P(None, TP, None),
        P(SAMPLE, TP),
        P(None, TP),
    )
    return jax.shard_map(
        body,
        mesh=fine,
        in_specs=placed,
        out_specs=(P(SAMPLE, None, None), P(SAMPLE, None, None), P(SAMPLE, None, None)),
        check_vma=False,
    )
```

```python
import functools
import math

import jax
import jax.numpy as jnp
from jax import lax
from jax.experimental import pallas as pl
from jax.experimental.pallas import tpu as pltpu
from jax.sharding import Mesh
from jax.sharding import PartitionSpec as P

HIGH = lax.Precision.HIGHEST
SAMPLE = ("fsdp", "grp")
TP = ("y", "core")
STEPS = 4
LAYERS = 2
BF = jnp.bfloat16
F32 = jnp.float32


def embed_block(times, width, block, start):
    half = width // 2
    column = start + jnp.arange(block)
    steps = jnp.where(column < half, column, column - half).astype(F32)
    freq = jnp.exp(-math.log(10000.0) * steps / half)
    angle = times[:, None] * freq[None, :]
    return jnp.where((column < half)[None, :], jnp.cos(angle), jnp.sin(angle))


def normalize(values):
    mean = jnp.mean(values, axis=-1, keepdims=True)
    centered = values - mean
    inverse = lax.rsqrt(jnp.mean(centered * centered, axis=-1, keepdims=True) + 1e-06)
    return (centered * inverse, inverse)


def ln_back(grad, normed, inverse):
    mean_grad = jnp.mean(grad, axis=-1, keepdims=True)
    mean_cross = jnp.mean(grad * normed, axis=-1, keepdims=True)
    return inverse * (grad - mean_grad - normed * mean_cross)


def gelu_both(values):
    inner = 0.7978845608 * (values + 0.044715 * values * values * values)
    tangent = jnp.tanh(inner)
    halved = 0.5 * (1.0 + tangent)
    slope = halved + 0.5 * values * (1.0 - tangent * tangent) * 0.7978845608 * (
        1.0 + 3.0 * 0.044715 * values * values
    )
    return values * halved, slope


def dot(left, right):
    return jnp.dot(left, right, preferred_element_type=F32)


def dot_back(left, right):
    return lax.dot_general(left, right, (((1,), (1,)), ((), ())), preferred_element_type=F32)


def dot_across(left, right):
    return lax.dot_general(left, right, (((0,), (0,)), ((), ())), preferred_element_type=F32)


def split(values):
    high = values.astype(BF)
    return high, (values - high.astype(F32)).astype(BF)


def sibling(values):
    return lax.ppermute(values, "core", [(0, 1), (1, 0)])


def swap_y(values):
    return lax.all_to_all(values, "y", 0, 0)


def cuts(extent):
    size = extent // 3 // 128 * 128
    return [(0, size), (size, size), (2 * size, extent - 2 * size)]


class Stream:
    def __init__(self, plan, sems, ahead=3):
        self.copies = [
            pltpu.make_async_copy(source, target, sems.at[index])
            for index, (source, target) in enumerate(plan)
        ]
        self.ahead = ahead
        self.at = 0
        for copy in self.copies[:ahead]:
            copy.start()

    def next(self):
        self.copies[self.at].wait()
        if self.at + self.ahead < len(self.copies):
            self.copies[self.at + self.ahead].start()
        self.at += 1


def rows_of(layer, sources, target):
    return [
        (source.at[layer, pl.ds(at, size)], target.at[side, pl.ds(at, size)])
        for side, source in enumerate(sources)
        for at, size in cuts(target.shape[1])
    ]


def turned(values):
    extent = values.shape[1]
    row = lax.broadcasted_iota(jnp.int32, (extent, extent), 0)
    col = lax.broadcasted_iota(jnp.int32, (extent, extent), 1)
    return dot_back((row == col).astype(BF), values)


def product_kernel(at_ref, packed_ref, w1_ref, w2_ref, out_ref, bias_ref):
    blocks, columns, _ = packed_ref.shape
    rows, hidden = w1_ref.shape
    cells = out_ref.shape[0] // STEPS
    pick_row = lax.broadcasted_iota(jnp.int32, (rows, columns), 0)
    pick_col = lax.broadcasted_iota(jnp.int32, (rows, columns), 1)
    mine = (pick_col == pick_row + rows * at_ref[1]).astype(BF)
    total = jnp.zeros((columns, cells), F32)
    for block in range(blocks):
        total = total + packed_ref[block, :, :cells].astype(F32)
    mean = jnp.sum(total, axis=0, keepdims=True) / (blocks * columns)
    local = dot(mine, packed_ref[at_ref[0]])
    high, low = split(local[:, :cells] - mean)
    out_rows = local[:, 2 * cells : 3 * cells].astype(BF)

    def modulation(index):
        block = dot(mine, packed_ref[at_ref[2 * index + 2]]).astype(BF)[:, 3 * cells :]
        row = lax.broadcasted_iota(jnp.int32, (block.shape[1], 8), 0)
        kind = lax.broadcasted_iota(jnp.int32, (block.shape[1], 8), 1)
        want = (row == 3 * (kind + LAYERS) + at_ref[2 * index + 3]) & (kind < STEPS)
        return dot(block, want.astype(BF)).astype(BF)

    shift, scale, gate = modulation(0), modulation(1), modulation(2)
    cell_row = lax.broadcasted_iota(jnp.int32, (cells, cells * STEPS), 0)
    cell_col = lax.broadcasted_iota(jnp.int32, (cells, cells * STEPS), 1)
    by_cell = (cell_col // STEPS == cell_row).astype(BF)
    step_row = lax.broadcasted_iota(jnp.int32, (8, cells * STEPS), 0)
    step_col = lax.broadcasted_iota(jnp.int32, (8, cells * STEPS), 1)
    by_step = (step_col % STEPS == step_row).astype(BF)
    left_in = (dot(high, by_cell) + dot(low, by_cell)) * (1.0 + dot(scale, by_step))
    left_out = dot(out_rows, by_cell) * dot(gate, by_step)
    gap = -hidden % 128
    out_ref[:, :hidden] = dot_across(left_in.astype(BF), w1_ref[...]).astype(BF)
    out_ref[:, hidden : hidden + gap] = jnp.zeros((cells * STEPS, gap), BF)
    out_ref[:, hidden + gap :] = dot_across(left_out.astype(BF), w2_ref[...]).astype(BF)
    bias_ref[...] = dot_across(shift, w1_ref[...]).astype(BF)


def select_kernel(parts_ref, pick_ref, pick_bias_ref, bias_ref, out_ref):
    hidden = bias_ref.shape[1]
    total = parts_ref[0].astype(F32)
    for source in range(1, parts_ref.shape[0]):
        total = total + parts_ref[source].astype(F32)
    chosen = dot(pick_ref[...], total.astype(BF))
    out_ref[...] = chosen.astype(BF)
    out_ref[:, :hidden] = (chosen[:, :hidden] + dot(pick_bias_ref[...], bias_ref[...])).astype(BF)


def student_kernel(x_ref, inverse_ref, mat_ref, out_ref):
    cells = x_ref.shape[1]
    lanes, wide = mat_ref.shape
    hidden = wide // 2 - (wide // 2) % 64
    gap = wide - 2 * hidden
    group = lanes * 4 // cells
    row = lax.broadcasted_iota(jnp.int32, (cells, lanes), 0)
    col = lax.broadcasted_iota(jnp.int32, (cells, lanes), 1)
    spread = (col == group * (row // 4) + row % 4).astype(BF)
    bias_col = lax.broadcasted_iota(jnp.int32, (8, lanes), 1)
    bias = dot((bias_col % group == 4).astype(BF), mat_ref[:, :hidden])[:1]
    x = dot(x_ref[...], spread).astype(BF)
    z = inverse_ref[...] * dot(x, mat_ref[:, :hidden]) + bias
    active = gelu_both(z)[0].astype(BF)
    high, low = split(dot_back(active, mat_ref[:, hidden + gap :]))
    out_ref[...] = dot_back(high, spread) + dot_back(low, spread)


def first_product_kernel(proj_ref, scale_ref, shift_ref, up, out_ref, up_ref, sems):
    cells = proj_ref.shape[1]
    stream = Stream(rows_of(0, (up,), up_ref), sems)
    proj = turned(proj_ref[...])
    centered = proj - jnp.mean(proj, axis=1, keepdims=True)
    left = (centered * (1.0 + scale_ref[...])).astype(BF)
    shift = jnp.broadcast_to(shift_ref[...], (8, shift_ref.shape[1])).astype(BF)
    for at, size in cuts(up_ref.shape[1]):
        stream.next()
        out_ref[:cells, at : at + size] = dot_back(left, up_ref[0, at : at + size, :])
        out_ref[cells:, at : at + size] = dot_back(shift, up_ref[0, at : at + size, :])


def first_forward_kernel(
    x_ref, proj_ref, mat_own, mat_sib, own, sib, y_ref, slope_ref, g_ref, back_ref, w_ref, acc_ref, sems
):
    cells = x_ref.shape[1]
    stream = Stream(rows_of(0, (own, sib), w_ref), sems)
    x = x_ref[...]
    g_0 = dot_back(x, proj_ref[...]).astype(BF)
    g_ref[...] = g_0
    normed, inverse = normalize(g_0.astype(F32))
    back_ref[:, :cells] = dot(normed.astype(BF), proj_ref[...])
    back_ref[:, cells:] = jnp.broadcast_to(inverse, (x.shape[0], cells))
    for side, mat_ref in enumerate((mat_own, mat_sib)):
        high, low = split(mat_ref[:cells])
        z = inverse * (dot(x, high) + dot(x, low)) + mat_ref[cells : cells + 1]
        active, slope = gelu_both(z)
        slope_ref[side] = slope.astype(BF)
        active = active.astype(BF)
        for at, size in cuts(w_ref.shape[1]):
            stream.next()
            part = dot(active[:, at : at + size], w_ref[side, at : at + size, :])
            if side == 0 and at == 0:
                acc_ref[...] = part
            else:
                acc_ref[...] += part
    y_ref[...] = acc_ref[...].astype(BF)


def forward_kernel(
    g_ref, scale_ref, shift_ref, up_own, up_sib, down_own, down_sib, y_ref, slope_ref,
    up_ref, down_ref, active_ref, acc_ref, sems
):
    stream = Stream(
        rows_of(1, (up_own, up_sib), up_ref) + rows_of(1, (down_own, down_sib), down_ref), sems
    )
    normed, _ = normalize(g_ref[...].astype(F32))
    u = (normed * (1.0 + scale_ref[...]) + shift_ref[...]).astype(BF)
    for side in range(2):
        for at, size in cuts(up_ref.shape[1]):
            stream.next()
            active, slope = gelu_both(dot_back(u, up_ref[side, at : at + size, :]))
            slope_ref[side, :, at : at + size] = slope.astype(BF)
            active_ref[side, :, at : at + size] = active.astype(BF)
    for side in range(2):
        for at, size in cuts(down_ref.shape[1]):
            stream.next()
            part = dot(active_ref[side, :, at : at + size], down_ref[side, at : at + size, :])
            if side == 0 and at == 0:
                acc_ref[...] = part
            else:
                acc_ref[...] += part
    y_ref[...] = acc_ref[...].astype(BF)


def backward_kernel(
    dy_ref, slope_ref, scale_ref, head_ref, up_own, up_sib, down_own, down_sib, out_ref,
    up_ref, down_ref, dz_ref, acc_ref, sems
):
    stream = Stream(
        rows_of(1, (down_own, down_sib), down_ref) + rows_of(1, (up_own, up_sib), up_ref), sems
    )
    dy = dy_ref[...]
    for side in range(2):
        for at, size in cuts(down_ref.shape[1]):
            stream.next()
            da = dot_back(dy, down_ref[side, at : at + size, :])
            dz_ref[side, :, at : at + size] = (
                da * slope_ref[side, :, at : at + size].astype(F32)
            ).astype(BF)
    for side in range(2):
        for at, size in cuts(up_ref.shape[1]):
            stream.next()
            part = dot(dz_ref[side, :, at : at + size], up_ref[side, at : at + size, :])
            if side == 0 and at == 0:
                acc_ref[...] = part
            else:
                acc_ref[...] += part
    out_ref[...] = (acc_ref[...] * (1.0 + scale_ref[...]) + head_ref[...].astype(F32)).astype(BF)


def first_backward_kernel(dy_ref, slope_ref, mat_own, mat_sib, own, sib, out_ref, w_ref, sems):
    cells = out_ref.shape[1]
    stream = Stream(rows_of(0, (own, sib), w_ref), sems)
    dy = dy_ref[...]
    total = None
    for side, mat_ref in enumerate((mat_own, mat_sib)):
        high, low = split(mat_ref[:cells])
        for at, size in cuts(w_ref.shape[1]):
            stream.next()
            da = dot_back(dy, w_ref[side, at : at + size, :])
            dz = (da * slope_ref[side, :, at : at + size].astype(F32)).astype(BF)
            part = dot_back(dz, high[:, at : at + size]) + dot_back(dz, low[:, at : at + size])
            total = part if total is None else total + part
    out_ref[...] = total


def sum_parts(parts_ref):
    total = parts_ref[0].astype(F32)
    for source in range(1, parts_ref.shape[0]):
        total = total + parts_ref[source].astype(F32)
    return total


def share(values, all_ref):
    for target in range(all_ref.shape[0]):
        all_ref[target] = values


def first_middle_kernel(at_ref, parts_ref, g_ref, gate_ref, mine_ref, all_ref):
    rows = mine_ref.shape[0]
    before = g_ref[pl.ds(pl.multiple_of(at_ref[0] * rows, rows), rows), :].astype(F32)
    after = (before + gate_ref[...] * sum_parts(parts_ref)).astype(BF)
    mine_ref[...] = after
    share(after, all_ref)


def last_middle_kernel(parts_ref, g_ref, gate_ref, mine_ref, all_ref):
    after = (g_ref[...].astype(F32) + gate_ref[...] * sum_parts(parts_ref)).astype(BF)
    mine_ref[...] = after
    share(after, all_ref)


def last_back_kernel(parts_ref, g_ref, gate_ref, grad_ref, all_ref):
    normed, inverse = normalize(g_ref[...].astype(F32))
    grad = ln_back(sum_parts(parts_ref), normed, inverse)
    grad_ref[...] = grad
    share((gate_ref[...] * grad).astype(BF), all_ref)


def first_back_kernel(parts_ref, g_ref, old_ref, gate_ref, proj_ref, direct_ref, all_ref):
    normed, inverse = normalize(g_ref[...].astype(F32))
    grad = old_ref[...] + ln_back(sum_parts(parts_ref), normed, inverse)
    direct_ref[...] = dot(grad.astype(BF), proj_ref[...])
    share((gate_ref[...] * grad).astype(BF), all_ref)


def head_kernel(g_ref, use_ref, own_ref, sib_ref, back_ref, score_ref):
    normed, _ = normalize(g_ref[...].astype(F32))
    quantised = normed.astype(BF)
    back = None
    scores = None
    for side, weight_ref in enumerate((own_ref, sib_ref)):
        weight = weight_ref[...]
        e = dot(quantised, weight)
        sigm = 1.0 / (1.0 + jnp.exp(-e))
        active = e * sigm
        outs = use_ref[side]
        slope = sigm * (1.0 + e * (1.0 - sigm))
        part = dot_back((-(outs[0:1] + outs[1:2]) * slope).astype(BF), weight)
        back = part if back is None else back + part
        part = [jnp.sum(active * outs[head : head + 1], axis=1, keepdims=True) for head in range(2)]
        scores = part if scores is None else [old + new for old, new in zip(scores, part)]
    back_ref[...] = back.astype(BF)
    lane = lax.broadcasted_iota(jnp.int32, score_ref.shape, 1)
    score_ref[...] = jnp.where(lane == 0, scores[0], 0.0) + jnp.where(lane == 1, scores[1], 0.0)


WHOLE = pl.BlockSpec(memory_space=pltpu.VMEM)
FAR = pl.BlockSpec(memory_space=pltpu.HBM)


def here(kernel, name, out_shape, operands, scalars=0, far=0, scratch=()):
    many = isinstance(out_shape, tuple)
    near = len(operands) - scalars - far
    return pl.pallas_call(
        kernel,
        name=name,
        out_shape=out_shape,
        in_specs=[pl.BlockSpec(memory_space=pltpu.SMEM)] * scalars + [WHOLE] * near + [FAR] * far,
        out_specs=(WHOLE,) * len(out_shape) if many else WHOLE,
        scratch_shapes=list(scratch),
        compiler_params=pltpu.CompilerParams(vmem_limit_bytes=(44 if far else 20) * 2**20),
    )(*operands)


def array(shape, dtype):
    return jax.ShapeDtypeStruct(shape, dtype)


def body(
    noisy_latents,
    student_step,
    teacher_step,
    teacher_noise,
    layer_pick,
    in_proj_s,
    in_proj_t,
    out_proj,
    s_mod,
    s_w1,
    s_w2,
    t_mod,
    t_w1,
    t_w2,
    d_w1,
    d_w2,
):
    cells = in_proj_s.shape[0]
    width = in_proj_s.shape[1] * 8
    samples = student_step.shape[0]
    layers = t_w1.shape[0]
    heads = d_w2.shape[0]
    seq = noisy_latents.shape[1]
    half = seq // 2
    quarter = half // 4
    rows = s_mod.shape[0]
    hidden = s_w1.shape[1]
    columns = in_proj_s.shape[1]
    sample = lax.axis_index(SAMPLE)
    at_y = lax.axis_index("y")
    at_core = lax.axis_index("core")
    start = sample * rows

    sig_all_t = teacher_step.astype(F32) * 0.001
    sig_steps = (1 + jnp.arange(STEPS)).astype(F32) * 0.25
    cond_s = jax.nn.silu(embed_block(1000.0 * sig_steps, width, rows, start))
    cond_t = jax.nn.silu(embed_block(1000.0 * sig_all_t, width, rows, start))
    mod_s = jnp.dot(cond_s, s_mod.astype(F32), precision=HIGH)
    mod_t = [jnp.dot(cond_t, t_mod[l].astype(F32), precision=HIGH) for l in range(layers)]
    mod_part = jnp.concatenate(
        [jnp.stack(mod_t, axis=1), jnp.broadcast_to(mod_s[None], (samples,) + mod_s.shape)], axis=1
    ).astype(BF)
    mod_part = lax.all_to_all(mod_part, SAMPLE, 0, 0)
    mods = jnp.sum(mod_part.astype(F32), axis=0)
    kinds = layers + STEPS
    mods = mods.reshape(kinds * 3, columns).astype(BF)
    packed = jnp.concatenate([in_proj_s, in_proj_t, out_proj, mods], axis=0).T
    gathered = lax.all_gather(packed, TP, axis=0, tiled=False)

    block = lax.axis_index(SAMPLE) * rows // columns
    places = [block, sample * rows // rows % (columns // rows)]
    for offset in (0, 8, 16):
        places += [(block + offset) // 3, (block + offset) % 3]
    gap = -hidden % 128
    both_wide = 2 * hidden + gap
    parts, part_bias = here(
        product_kernel,
        "product",
        (
            jax.ShapeDtypeStruct((cells * STEPS, both_wide), BF),
            jax.ShapeDtypeStruct((8, hidden), BF),
        ),
        (jnp.stack(places).astype(jnp.int32), gathered, s_w1, s_w2.T),
        scalars=1,
    )
    piece = cells * STEPS // samples
    chunk = cells // samples
    t_w1 = jnp.swapaxes(t_w1, 1, 2)
    parts, gathered, t_w1, t_w2 = lax.optimization_barrier((parts, gathered, t_w1, t_w2))
    received = lax.all_to_all(parts.reshape(samples, piece, both_wide), SAMPLE, 0, 0)

    w2_sib = sibling(t_w2)
    w1_sib = sibling(t_w1)

    at_row = jnp.arange(samples * 8)
    step_at = jnp.repeat(student_step - 1, 8)
    pick = (
        ((at_row % 8 * STEPS + step_at)[:, None] == jnp.arange(piece)[None])
        & (at_row % 8 < chunk)[:, None]
    ).astype(BF)
    pick_bias = ((step_at[:, None] == jnp.arange(8)[None]) & (at_row % 8 == chunk)[:, None]).astype(BF)
    chosen = here(
        select_kernel,
        "select",
        jax.ShapeDtypeStruct((samples * 8, both_wide), BF),
        (received, pick, pick_bias, part_bias),
    )
    mine = lax.all_to_all(chosen.reshape(samples, 8, both_wide), SAMPLE, 0, 0)
    mine = mine.reshape(samples * 8, both_wide)
    my_step = lax.dynamic_index_in_dim(student_step, sample, keepdims=False)

    spare = -columns % 128
    head_block, _ = lax.optimization_barrier((jnp.pad(d_w1, ((0, 0), (0, spare))), mine))
    head_own = lax.all_gather(head_block, SAMPLE, axis=0, tiled=True)

    mods = gathered[:, :, 3 * cells :].astype(F32).reshape(8, columns, kinds, 3)
    mod_teacher = mods[:, :, :layers].transpose(2, 0, 3, 1).reshape(layers, 1, 3 * width)
    packed = gathered.reshape(width, -1)
    proj_s, proj_t, proj_out = (packed[:, at * cells : (at + 1) * cells] for at in range(3))

    sigma_s = my_step.astype(F32) * 0.25
    sigma_t = lax.dynamic_index_in_dim(sig_all_t, sample, keepdims=False)
    latent_in = noisy_latents[0]
    h0 = dot_back(latent_in, proj_s).astype(BF)
    _, inverse_s = normalize(h0.astype(F32))
    velocity = here(
        student_kernel,
        "student",
        jax.ShapeDtypeStruct((seq, cells), F32),
        (latent_in, inverse_s, mine),
    )
    mine_first = lax.dynamic_slice_in_dim(velocity, at_core * half, half, 0)
    other = lax.dynamic_slice_in_dim(velocity, (1 - at_core) * half, half, 0)
    velocity = mine_first + sibling(other)
    velocity = velocity + lax.ppermute(velocity, "y", [(0, 1), (1, 0), (2, 3), (3, 2)])
    velocity = velocity + lax.ppermute(velocity, "y", [(0, 2), (2, 0), (1, 3), (3, 1)])

    def my_half(values):
        return lax.dynamic_slice_in_dim(values, at_core * half, half, 0)

    velocity = velocity + dot(my_half(h0), proj_out)
    latents = (my_half(latent_in).astype(F32) - sigma_s * velocity).astype(BF)
    noised = (
        (1.0 - sigma_t) * latents.astype(F32) + sigma_t * my_half(teacher_noise[0]).astype(F32)
    ).astype(BF)

    def both(values):
        other = sibling(values)
        first = jnp.where(at_core == 0, values, other)
        second = jnp.where(at_core == 0, other, values)
        return jnp.concatenate([first, second], axis=0)

    latents = both(latents)

    shifts = [mod_teacher[l, :, :width] for l in range(layers)]
    scales = [mod_teacher[l, :, width : 2 * width] for l in range(layers)]
    gates = [mod_teacher[l, :, 2 * width :] for l in range(layers)]
    matrix = pltpu.VMEM((2, hidden, width), BF)
    total = pltpu.VMEM((half, width), F32)
    inner = pltpu.VMEM((2, half, hidden), BF)
    copies = len(cuts(hidden))
    first_own = here(
        first_product_kernel,
        "first_product",
        array((cells + 8, hidden), F32),
        (proj_t, scales[0], shifts[0], t_w1),
        far=1,
        scratch=(pltpu.VMEM((1, hidden, width), BF), pltpu.SemaphoreType.DMA((copies,))),
    )
    first_sib = sibling(first_own)

    rows_out = array((4, quarter, width), BF)
    mine_out = array((quarter, width), BF)
    inner_out = array((2, half, hidden), BF)
    y_0, slope_0, g_0, back_0 = here(
        first_forward_kernel,
        "first_forward",
        (array((half, width), BF), inner_out, array((half, width), BF), array((half, 2 * cells), F32)),
        (noised, proj_t, first_own, first_sib, t_w2, w2_sib),
        far=2,
        scratch=(matrix, total, pltpu.SemaphoreType.DMA((2 * copies,))),
    )
    g_1_mine, g_1 = here(
        first_middle_kernel,
        "first_middle",
        (mine_out, rows_out),
        (at_y.reshape(1), swap_y(y_0.reshape(4, quarter, width)), g_0, gates[0]),
        scalars=1,
    )
    g_1 = swap_y(g_1).reshape(half, width)
    y_1, slope_1 = here(
        forward_kernel,
        "forward",
        (array((half, width), BF), inner_out),
        (g_1, scales[1], shifts[1], t_w1, w1_sib, t_w2, w2_sib),
        far=4,
        scratch=(matrix, matrix, inner, total, pltpu.SemaphoreType.DMA((4 * copies,))),
    )
    head_own, d_w2_late, _ = lax.optimization_barrier((head_own, d_w2, y_1))
    head_sib = sibling(head_own)
    d_w2_sib = sibling(d_w2_late)
    g_2_mine, g_2 = here(
        last_middle_kernel,
        "last_middle",
        (mine_out, rows_out),
        (swap_y(y_1.reshape(4, quarter, width)), g_1_mine, gates[1]),
    )
    g_2 = swap_y(g_2).reshape(half, width)

    outs = jnp.pad(jnp.stack([d_w2, d_w2_sib]), ((0, 0), (0, 0), (0, spare)))
    use = [outs * (layer_pick[0] == layer).astype(F32)[None, :, None] for layer in range(layers)]
    head_shapes = (array((half, width), BF), array((half, 128), F32))
    head_back_2, scores_2 = here(
        head_kernel, "head_last", head_shapes, (g_2, use[1], head_own, head_sib)
    )
    g_1, _ = lax.optimization_barrier((g_1, head_back_2))
    head_back_1, scores_1 = here(
        head_kernel, "head_first", head_shapes, (g_1, use[0], head_own, head_sib)
    )
    scores = (scores_1 + scores_2)[:, :heads].T
    scores = scores + lax.ppermute(scores, "y", [(0, 1), (1, 0), (2, 3), (3, 2)])
    scores = scores + lax.ppermute(scores, "y", [(0, 2), (2, 0), (1, 3), (3, 1)])
    scores_other = sibling(scores)
    scores = jnp.concatenate(
        [jnp.where(at_core == 0, scores, scores_other), jnp.where(at_core == 0, scores_other, scores)],
        axis=1,
    )

    dg_2, dy_1 = here(
        last_back_kernel,
        "last_back",
        (array((quarter, width), F32), rows_out),
        (swap_y(head_back_2.reshape(4, quarter, width)), g_2_mine, gates[1]),
    )
    du_1 = here(
        backward_kernel,
        "backward",
        array((half, width), BF),
        (
            swap_y(dy_1).reshape(half, width),
            slope_1,
            scales[1],
            head_back_1,
            t_w1,
            w1_sib,
            t_w2,
            w2_sib,
        ),
        far=4,
        scratch=(matrix, matrix, inner, total, pltpu.SemaphoreType.DMA((4 * copies,))),
    )
    direct, dy_0 = here(
        first_back_kernel,
        "first_back",
        (array((quarter, cells), F32), rows_out),
        (swap_y(du_1.reshape(4, quarter, width)), g_1_mine, dg_2, gates[0], proj_t),
    )
    down_0 = here(
        first_backward_kernel,
        "first_backward",
        array((half, cells), F32),
        (swap_y(dy_0).reshape(half, width), slope_0, first_own, first_sib, t_w2, w2_sib),
        far=2,
        scratch=(matrix, pltpu.SemaphoreType.DMA((2 * copies,))),
    )
    direct = lax.dynamic_update_slice_in_dim(
        jnp.zeros((half, cells), F32), direct, at_y * quarter, 0
    )
    final = jnp.concatenate([down_0, direct], axis=1)
    final = final + lax.ppermute(final, "y", [(0, 1), (1, 0), (2, 3), (3, 2)])
    final = final + lax.ppermute(final, "y", [(0, 2), (2, 0), (1, 3), (3, 1)])
    down_0, direct = final[:, :cells], final[:, cells:]
    normed_back, inverse_0 = back_0[:, :cells], back_0[:, cells : cells + 1]
    cross = inverse_0 * jnp.sum(noised.astype(F32) * down_0, axis=1, keepdims=True) / width
    grad = (1.0 - sigma_t) * (inverse_0 * (down_0 - normed_back * cross) + direct)
    return (latents[None], scores[None], both(grad)[None])


def solution(mesh):
    names = list(mesh.axis_names)
    shape = list(mesh.devices.shape)
    at = names.index("tp")
    names[at : at + 1] = ["y", "core"]
    shape[at : at + 1] = [4, 2]
    fine = Mesh(mesh.devices.reshape(shape), tuple(names))
    placed = (
        P(SAMPLE, None, None),
        P(),
        P(),
        P(SAMPLE, None, None),
        P(SAMPLE, None),
        P(None, TP),
        P(None, TP),
        P(None, TP),
        P(SAMPLE, TP),
        P(SAMPLE, TP),
        P(TP, SAMPLE),
        P(None, SAMPLE, TP),
        P(None, None, TP),
        P(None, TP, None),
        P(SAMPLE, TP),
        P(None, TP),
    )
    return jax.shard_map(
        body,
        mesh=fine,
        in_specs=placed,
        out_specs=(P(SAMPLE, None, None), P(SAMPLE, None, None), P(SAMPLE, None, None)),
        check_vma=False,
    )
```

```python
import functools
import math

import jax
import jax.numpy as jnp
from jax import lax
from jax.experimental import pallas as pl
from jax.experimental.pallas import tpu as pltpu
from jax.sharding import Mesh
from jax.sharding import PartitionSpec as P

HIGH = lax.Precision.HIGHEST
SAMPLE = ("fsdp", "grp")
TP = ("y", "core")
STEPS = 4
LAYERS = 2
BF = jnp.bfloat16
F32 = jnp.float32


def embed_block(times, width, block, start):
    half = width // 2
    column = start + jnp.arange(block)
    steps = jnp.where(column < half, column, column - half).astype(F32)
    freq = jnp.exp(-math.log(10000.0) * steps / half)
    angle = times[:, None] * freq[None, :]
    return jnp.where((column < half)[None, :], jnp.cos(angle), jnp.sin(angle))


def normalize(values):
    mean = jnp.mean(values, axis=-1, keepdims=True)
    centered = values - mean
    inverse = lax.rsqrt(jnp.mean(centered * centered, axis=-1, keepdims=True) + 1e-06)
    return (centered * inverse, inverse)


def ln_back(grad, normed, inverse):
    mean_grad = jnp.mean(grad, axis=-1, keepdims=True)
    mean_cross = jnp.mean(grad * normed, axis=-1, keepdims=True)
    return inverse * (grad - mean_grad - normed * mean_cross)


def gelu_both(values):
    inner = 0.7978845608 * (values + 0.044715 * values * values * values)
    tangent = jnp.tanh(inner)
    halved = 0.5 * (1.0 + tangent)
    slope = halved + 0.5 * values * (1.0 - tangent * tangent) * 0.7978845608 * (
        1.0 + 3.0 * 0.044715 * values * values
    )
    return values * halved, slope


def dot(left, right):
    return jnp.dot(left, right, preferred_element_type=F32)


def dot_back(left, right):
    return lax.dot_general(left, right, (((1,), (1,)), ((), ())), preferred_element_type=F32)


def dot_across(left, right):
    return lax.dot_general(left, right, (((0,), (0,)), ((), ())), preferred_element_type=F32)


def split(values):
    high = values.astype(BF)
    return high, (values - high.astype(F32)).astype(BF)


def sibling(values):
    return lax.ppermute(values, "core", [(0, 1), (1, 0)])


def swap_y(values):
    return lax.all_to_all(values, "y", 0, 0)


class Stream:
    def __init__(self, plan, sems):
        self.copies = [
            pltpu.make_async_copy(source, target, sems.at[index])
            for index, (source, target) in enumerate(plan)
        ]
        for copy in self.copies:
            copy.start()
        self.at = 0

    def next(self):
        self.copies[self.at].wait()
        self.at += 1


def matrices(layer, sources, target):
    return [(source.at[layer], target.at[side]) for side, source in enumerate(sources)]


def turned(values):
    extent = values.shape[1]
    row = lax.broadcasted_iota(jnp.int32, (extent, extent), 0)
    col = lax.broadcasted_iota(jnp.int32, (extent, extent), 1)
    return dot_back((row == col).astype(BF), values)


def product_kernel(at_ref, packed_ref, w1_ref, w2_ref, out_ref, bias_ref):
    blocks, columns, _ = packed_ref.shape
    rows, hidden = w1_ref.shape
    cells = out_ref.shape[0] // STEPS
    pick_row = lax.broadcasted_iota(jnp.int32, (rows, columns), 0)
    pick_col = lax.broadcasted_iota(jnp.int32, (rows, columns), 1)
    mine = (pick_col == pick_row + rows * at_ref[1]).astype(BF)
    total = jnp.zeros((columns, cells), F32)
    for block in range(blocks):
        total = total + packed_ref[block, :, :cells].astype(F32)
    mean = jnp.sum(total, axis=0, keepdims=True) / (blocks * columns)
    local = dot(mine, packed_ref[at_ref[0]])
    high, low = split(local[:, :cells] - mean)
    out_rows = local[:, 2 * cells : 3 * cells].astype(BF)

    def modulation(index):
        block = dot(mine, packed_ref[at_ref[2 * index + 2]]).astype(BF)[:, 3 * cells :]
        row = lax.broadcasted_iota(jnp.int32, (block.shape[1], 8), 0)
        kind = lax.broadcasted_iota(jnp.int32, (block.shape[1], 8), 1)
        want = (row == 3 * (kind + LAYERS) + at_ref[2 * index + 3]) & (kind < STEPS)
        return dot(block, want.astype(BF)).astype(BF)

    shift, scale, gate = modulation(0), modulation(1), modulation(2)
    cell_row = lax.broadcasted_iota(jnp.int32, (cells, cells * STEPS), 0)
    cell_col = lax.broadcasted_iota(jnp.int32, (cells, cells * STEPS), 1)
    by_cell = (cell_col // STEPS == cell_row).astype(BF)
    step_row = lax.broadcasted_iota(jnp.int32, (8, cells * STEPS), 0)
    step_col = lax.broadcasted_iota(jnp.int32, (8, cells * STEPS), 1)
    by_step = (step_col % STEPS == step_row).astype(BF)
    left_in = (dot(high, by_cell) + dot(low, by_cell)) * (1.0 + dot(scale, by_step))
    left_out = dot(out_rows, by_cell) * dot(gate, by_step)
    gap = -hidden % 128
    out_ref[:, :hidden] = dot_across(left_in.astype(BF), w1_ref[...]).astype(BF)
    out_ref[:, hidden : hidden + gap] = jnp.zeros((cells * STEPS, gap), BF)
    out_ref[:, hidden + gap :] = dot_across(left_out.astype(BF), w2_ref[...]).astype(BF)
    bias_ref[...] = dot_across(shift, w1_ref[...]).astype(BF)


def select_kernel(parts_ref, pick_ref, pick_bias_ref, bias_ref, out_ref):
    hidden = bias_ref.shape[1]
    total = parts_ref[0].astype(F32)
    for source in range(1, parts_ref.shape[0]):
        total = total + parts_ref[source].astype(F32)
    chosen = dot(pick_ref[...], total.astype(BF))
    out_ref[...] = chosen.astype(BF)
    out_ref[:, :hidden] = (chosen[:, :hidden] + dot(pick_bias_ref[...], bias_ref[...])).astype(BF)


def student_kernel(x_ref, inverse_ref, mat_ref, out_ref):
    cells = x_ref.shape[1]
    lanes, wide = mat_ref.shape
    hidden = wide // 2 - (wide // 2) % 64
    gap = wide - 2 * hidden
    group = lanes * 4 // cells
    row = lax.broadcasted_iota(jnp.int32, (cells, lanes), 0)
    col = lax.broadcasted_iota(jnp.int32, (cells, lanes), 1)
    spread = (col == group * (row // 4) + row % 4).astype(BF)
    bias_col = lax.broadcasted_iota(jnp.int32, (8, lanes), 1)
    bias = dot((bias_col % group == 4).astype(BF), mat_ref[:, :hidden])[:1]
    x = dot(x_ref[...], spread).astype(BF)
    z = inverse_ref[...] * dot(x, mat_ref[:, :hidden]) + bias
    active = gelu_both(z)[0].astype(BF)
    high, low = split(dot_back(active, mat_ref[:, hidden + gap :]))
    out_ref[...] = dot_back(high, spread) + dot_back(low, spread)


def first_product_kernel(proj_ref, scale_ref, shift_ref, up, out_ref, up_ref, sems):
    cells = proj_ref.shape[1]
    stream = Stream(matrices(0, (up,), up_ref), sems)
    proj = turned(proj_ref[...])
    centered = proj - jnp.mean(proj, axis=1, keepdims=True)
    left = (centered * (1.0 + scale_ref[...])).astype(BF)
    shift = jnp.broadcast_to(shift_ref[...], (16, shift_ref.shape[1])).astype(BF)
    left = jnp.concatenate([left, shift], axis=0)
    stream.next()
    out_ref[...] = dot_back(left, up_ref[0])[: cells + 8]


def first_forward_kernel(
    x_ref, proj_ref, mat_own, mat_sib, own, sib, y_out, slope_out, g_ref, back_ref, w_ref, y_ref, slope_ref, sems
):
    cells = x_ref.shape[1]
    stream = Stream(matrices(0, (own, sib), w_ref), sems)
    x = x_ref[...]
    g_0 = dot_back(x, proj_ref[...]).astype(BF)
    g_ref[...] = g_0
    normed, inverse = normalize(g_0.astype(F32))
    back_ref[:, :cells] = dot(normed.astype(BF), proj_ref[...])
    back_ref[:, cells:] = jnp.broadcast_to(inverse, (x.shape[0], cells))
    twice = jnp.concatenate([x, x], axis=1)
    actives = []
    for side, mat_ref in enumerate((mat_own, mat_sib)):
        high, low = split(mat_ref[:cells])
        z = inverse * dot(twice, jnp.concatenate([high, low], axis=0)) + mat_ref[cells : cells + 1]
        active, slope = gelu_both(z)
        slope_ref[side] = slope.astype(BF)
        actives.append(active.astype(BF))
    keep = pltpu.make_async_copy(slope_ref, slope_out, sems.at[2])
    keep.start()
    stream.next()
    y = dot(actives[0], w_ref[0])
    stream.next()
    y_ref[...] = (y + dot(actives[1], w_ref[1])).astype(BF)
    send = pltpu.make_async_copy(y_ref, y_out, sems.at[3])
    send.start()
    keep.wait()
    send.wait()


def resident_kernel(plan, *refs):
    sources, out_refs, sems = refs[: 2 * len(plan)], refs[2 * len(plan) : -1], refs[-1]
    copies = []
    for index, layer in enumerate(plan):
        copies += matrices(layer, sources[2 * index : 2 * index + 2], out_refs[index])
    stream = Stream(copies, sems)
    for _ in copies:
        stream.next()


def forward_kernel(
    g_ref, scale_ref, shift_ref, up_ref, down_ref, y_out, slope_out, y_ref, slope_ref, sems
):
    normed, _ = normalize(g_ref[...].astype(F32))
    u = (normed * (1.0 + scale_ref[...]) + shift_ref[...]).astype(BF)
    actives = []
    for side in range(2):
        active, slope = gelu_both(dot_back(u, up_ref[side]))
        slope_ref[side] = slope.astype(BF)
        actives.append(active.astype(BF))
    keep = pltpu.make_async_copy(slope_ref, slope_out, sems.at[0])
    keep.start()
    y_ref[...] = (dot(actives[0], down_ref[0]) + dot(actives[1], down_ref[1])).astype(BF)
    send = pltpu.make_async_copy(y_ref, y_out, sems.at[1])
    send.start()
    keep.wait()
    send.wait()


def backward_kernel(
    dy_ref, scale_ref, up_ref, down_ref, slope, head, out, slope_ref, head_ref, out_ref, sems
):
    stream = Stream([(slope, slope_ref), (head, head_ref)], sems)
    dy = dy_ref[...]
    da = dot_back(dy, down_ref[0])
    stream.next()
    dz_own = (da * slope_ref[0].astype(F32)).astype(BF)
    dz_sib = (dot_back(dy, down_ref[1]) * slope_ref[1].astype(F32)).astype(BF)
    du = dot(dz_own, up_ref[0]) + dot(dz_sib, up_ref[1])
    stream.next()
    out_ref[...] = (du * (1.0 + scale_ref[...]) + head_ref[...].astype(F32)).astype(BF)
    send = pltpu.make_async_copy(out_ref, out, sems.at[2])
    send.start()
    send.wait()


def first_backward_kernel(
    at_ref, rest_ref, dy_ref, x_ref, back_ref, score_ref, direct_ref, mat_own, mat_sib, down_ref, slope,
    out_ref, slope_ref, sems
):
    cells = x_ref.shape[1]
    stream = Stream([(slope, slope_ref)], sems)
    dy = dy_ref[...]
    total = None
    for side, mat_ref in enumerate((mat_own, mat_sib)):
        high, low = split(mat_ref[:cells])
        da = dot_back(dy, down_ref[side])
        if side == 0:
            stream.next()
        dz = (da * slope_ref[side].astype(F32)).astype(BF)
        part = dot_back(dz, high) + dot_back(dz, low)
        total = part if total is None else total + part
    inverse = back_ref[:, cells : cells + 1]
    cross = inverse * jnp.sum(x_ref[...].astype(F32) * total, axis=1, keepdims=True) / dy.shape[1]
    rest = rest_ref[0]
    out_ref[:, :cells] = rest * (inverse * (total - back_ref[:, :cells] * cross))
    out_ref[:, cells:] = score_ref[:, :cells]
    rows = direct_ref.shape[0]
    mine = pl.ds(pl.multiple_of(at_ref[0] * rows, rows), rows)
    out_ref[mine, :cells] += rest * direct_ref[...]


def modulation_kernel(cond_s_ref, cond_t_ref, s_ref, t_ref, out_ref):
    samples = cond_t_ref.shape[0]

    def product(cond, weight):
        extent = cond.shape[0]
        high, rest = split(cond)
        rest = cond - high.astype(F32)
        middle, low = split(rest)
        parts = dot(jnp.concatenate([high, middle, low], axis=0), weight)
        return (parts[:extent] + (parts[extent : 2 * extent] + parts[2 * extent :])).astype(BF)

    def place(extent, first, every):
        row = lax.broadcasted_iota(jnp.int32, (samples * 8, extent), 0)
        col = lax.broadcasted_iota(jnp.int32, (samples * 8, extent), 1)
        if every:
            return (row % 8 == first + col).astype(BF)
        return ((row // 8 == col) & (row % 8 == first)).astype(BF)

    total = dot(place(16, LAYERS, True), product(cond_s_ref[...], s_ref[...]))
    for layer in range(LAYERS):
        part = product(cond_t_ref[...], t_ref[layer])
        total = total + dot(place(samples, layer, False), part)
    out_ref[...] = total.astype(BF)


def sum_parts(parts_ref):
    total = parts_ref[0].astype(F32)
    for source in range(1, parts_ref.shape[0]):
        total = total + parts_ref[source].astype(F32)
    return total


def share(values, all_ref):
    for target in range(all_ref.shape[0]):
        all_ref[target] = values


def first_middle_kernel(at_ref, parts_ref, g_ref, gate_ref, mine_ref, all_ref):
    rows = mine_ref.shape[0]
    before = g_ref[pl.ds(pl.multiple_of(at_ref[0] * rows, rows), rows), :].astype(F32)
    after = (before + gate_ref[...] * sum_parts(parts_ref)).astype(BF)
    mine_ref[...] = after
    share(after, all_ref)


def last_middle_kernel(parts_ref, g_ref, gate_ref, mine_ref, all_ref):
    after = (g_ref[...].astype(F32) + gate_ref[...] * sum_parts(parts_ref)).astype(BF)
    mine_ref[...] = after
    share(after, all_ref)


def last_back_kernel(parts_ref, g_ref, gate_ref, grad_ref, all_ref):
    normed, inverse = normalize(g_ref[...].astype(F32))
    grad = ln_back(sum_parts(parts_ref), normed, inverse)
    grad_ref[...] = grad
    share((gate_ref[...] * grad).astype(BF), all_ref)


def first_back_kernel(parts_ref, g_ref, old_ref, gate_ref, proj_ref, direct_ref, all_ref):
    normed, inverse = normalize(g_ref[...].astype(F32))
    grad = old_ref[...] + ln_back(sum_parts(parts_ref), normed, inverse)
    direct_ref[...] = dot(grad.astype(BF), proj_ref[...])
    share((gate_ref[...] * grad).astype(BF), all_ref)


def head_kernel(g_ref, use_ref, own, sib, back_out, score_ref, weight_ref, back_ref, sems):
    stream = Stream([(own, weight_ref.at[0]), (sib, weight_ref.at[1])], sems)
    normed, _ = normalize(g_ref[...].astype(F32))
    quantised = normed.astype(BF)
    back = None
    scores = None
    for side in range(2):
        stream.next()
        weight = weight_ref[side]
        e = dot(quantised, weight)
        sigm = 1.0 / (1.0 + jnp.exp(-e))
        active = e * sigm
        outs = use_ref[side]
        slope = sigm * (1.0 + e * (1.0 - sigm))
        part = dot_back((-(outs[0:1] + outs[1:2]) * slope).astype(BF), weight)
        back = part if back is None else back + part
        part = [jnp.sum(active * outs[head : head + 1], axis=1, keepdims=True) for head in range(2)]
        scores = part if scores is None else [old + new for old, new in zip(scores, part)]
    back_ref[...] = back.astype(BF)
    send = pltpu.make_async_copy(back_ref, back_out, sems.at[2])
    send.start()
    lane = lax.broadcasted_iota(jnp.int32, score_ref.shape, 1)
    score_ref[...] = jnp.where(lane == 0, scores[0], 0.0) + jnp.where(lane == 1, scores[1], 0.0)
    send.wait()


WHOLE = pl.BlockSpec(memory_space=pltpu.VMEM)
FAR = pl.BlockSpec(memory_space=pltpu.HBM)


def here(kernel, name, out_shape, operands, scalars=0, far=0, far_out=(), scratch=(), limit=20):
    many = isinstance(out_shape, tuple)
    near = len(operands) - scalars - far
    specs = tuple(
        FAR if index in far_out else WHOLE for index in range(len(out_shape) if many else 1)
    )
    return pl.pallas_call(
        kernel,
        name=name,
        out_shape=out_shape,
        in_specs=[pl.BlockSpec(memory_space=pltpu.SMEM)] * scalars + [WHOLE] * near + [FAR] * far,
        out_specs=specs if many else specs[0],
        scratch_shapes=list(scratch),
        compiler_params=pltpu.CompilerParams(vmem_limit_bytes=limit * 2**20),
    )(*operands)


def resident(plan, sources):
    shapes = tuple(
        pltpu.VMEM((2,) + sources[2 * index].shape[1:], sources[2 * index].dtype)
        for index in range(len(plan))
    )
    return pl.pallas_call(
        functools.partial(resident_kernel, plan),
        name="resident",
        out_shape=shapes,
        in_specs=[FAR] * len(sources),
        out_specs=(WHOLE,) * len(plan),
        scratch_shapes=[pltpu.SemaphoreType.DMA((len(sources),))],
        compiler_params=pltpu.CompilerParams(vmem_limit_bytes=4 * 2**20),
    )(*sources)


def array(shape, dtype):
    return jax.ShapeDtypeStruct(shape, dtype)


def body(
    noisy_latents,
    student_step,
    teacher_step,
    teacher_noise,
    layer_pick,
    in_proj_s,
    in_proj_t,
    out_proj,
    s_mod,
    s_w1,
    s_w2,
    t_mod,
    t_w1,
    t_w2,
    d_w1,
    d_w2,
):
    cells = in_proj_s.shape[0]
    width = in_proj_s.shape[1] * 8
    samples = student_step.shape[0]
    layers = t_w1.shape[0]
    heads = d_w2.shape[0]
    seq = noisy_latents.shape[1]
    half = seq // 2
    quarter = half // 4
    rows = s_mod.shape[0]
    hidden = s_w1.shape[1]
    columns = in_proj_s.shape[1]
    sample = lax.axis_index(SAMPLE)
    at_y = lax.axis_index("y")
    at_core = lax.axis_index("core")
    start = sample * rows

    sig_all_t = teacher_step.astype(F32) * 0.001
    sig_steps = (1 + jnp.arange(STEPS)).astype(F32) * 0.25
    cond_s = jax.nn.silu(embed_block(1000.0 * sig_steps, width, rows, start))
    cond_t = jax.nn.silu(embed_block(1000.0 * sig_all_t, width, rows, start))
    mod_part = here(
        modulation_kernel,
        "modulation",
        array((samples * 8, s_mod.shape[1]), BF),
        (jnp.pad(cond_s, ((0, 16 - STEPS), (0, 0))), cond_t, s_mod, t_mod),
    ).reshape(samples, 8, s_mod.shape[1])
    mods = jnp.sum(lax.all_to_all(mod_part, SAMPLE, 0, 0).astype(F32), axis=0)
    kinds = layers + STEPS
    mods = mods[:kinds].reshape(kinds * 3, columns).astype(BF)
    packed = jnp.concatenate([in_proj_s, in_proj_t, out_proj, mods], axis=0).T
    gathered = lax.all_gather(packed, TP, axis=0, tiled=False)

    block = lax.axis_index(SAMPLE) * rows // columns
    places = [block, sample * rows // rows % (columns // rows)]
    for offset in (0, 8, 16):
        places += [(block + offset) // 3, (block + offset) % 3]
    gap = -hidden % 128
    both_wide = 2 * hidden + gap
    parts, part_bias = here(
        product_kernel,
        "product",
        (
            jax.ShapeDtypeStruct((cells * STEPS, both_wide), BF),
            jax.ShapeDtypeStruct((8, hidden), BF),
        ),
        (jnp.stack(places).astype(jnp.int32), gathered, s_w1, s_w2.T),
        scalars=1,
    )
    piece = cells * STEPS // samples
    chunk = cells // samples
    t_w1 = jnp.swapaxes(t_w1, 1, 2)
    parts, gathered, t_w1, t_w2 = lax.optimization_barrier((parts, gathered, t_w1, t_w2))
    received = lax.all_to_all(parts.reshape(samples, piece, both_wide), SAMPLE, 0, 0)

    mods = gathered[:, :, 3 * cells :].astype(F32).reshape(8, columns, kinds, 3)
    mod_teacher = mods[:, :, :layers].transpose(2, 0, 3, 1).reshape(layers, 1, 3 * width)
    packed = gathered.reshape(width, -1)
    proj_s, proj_t, proj_out = (packed[:, at * cells : (at + 1) * cells] for at in range(3))
    shifts = [mod_teacher[l, :, :width] for l in range(layers)]
    scales = [mod_teacher[l, :, width : 2 * width] for l in range(layers)]
    gates = [mod_teacher[l, :, 2 * width :] for l in range(layers)]
    first_own = here(
        first_product_kernel,
        "first_product",
        array((cells + 8, hidden), F32),
        (proj_t, scales[0], shifts[0], t_w1),
        far=1,
        scratch=(pltpu.VMEM((1, hidden, width), BF), pltpu.SemaphoreType.DMA((1,))),
    )
    latent_in = noisy_latents[0]
    h0 = dot_back(latent_in, proj_s).astype(BF)
    _, inverse_s = normalize(h0.astype(F32))
    received, first_own, inverse_s = lax.optimization_barrier((received, first_own, inverse_s))

    w2_sib = sibling(t_w2)
    w1_sib = sibling(t_w1)

    at_row = jnp.arange(samples * 8)
    step_at = jnp.repeat(student_step - 1, 8)
    pick = (
        ((at_row % 8 * STEPS + step_at)[:, None] == jnp.arange(piece)[None])
        & (at_row % 8 < chunk)[:, None]
    ).astype(BF)
    pick_bias = ((step_at[:, None] == jnp.arange(8)[None]) & (at_row % 8 == chunk)[:, None]).astype(BF)
    chosen = here(
        select_kernel,
        "select",
        jax.ShapeDtypeStruct((samples * 8, both_wide), BF),
        (received, pick, pick_bias, part_bias),
    )
    mine = lax.all_to_all(chosen.reshape(samples, 8, both_wide), SAMPLE, 0, 0)
    mine = mine.reshape(samples * 8, both_wide)
    my_step = lax.dynamic_index_in_dim(student_step, sample, keepdims=False)

    spare = -columns % 128
    head_block, _ = lax.optimization_barrier((jnp.pad(d_w1, ((0, 0), (0, spare))), mine))
    head_own = lax.all_gather(head_block, SAMPLE, axis=0, tiled=True)

    sigma_s = my_step.astype(F32) * 0.25
    sigma_t = lax.dynamic_index_in_dim(sig_all_t, sample, keepdims=False)
    velocity = here(
        student_kernel,
        "student",
        jax.ShapeDtypeStruct((seq, cells), F32),
        (latent_in, inverse_s, mine),
    )
    mine_first = lax.dynamic_slice_in_dim(velocity, at_core * half, half, 0)
    other = lax.dynamic_slice_in_dim(velocity, (1 - at_core) * half, half, 0)
    velocity = mine_first + sibling(other)
    velocity = velocity + lax.ppermute(velocity, "y", [(0, 1), (1, 0), (2, 3), (3, 2)])
    velocity = velocity + lax.ppermute(velocity, "y", [(0, 2), (2, 0), (1, 3), (3, 1)])

    def my_half(values):
        return lax.dynamic_slice_in_dim(values, at_core * half, half, 0)

    velocity = velocity + dot(my_half(h0), proj_out)
    latents = (my_half(latent_in).astype(F32) - sigma_s * velocity).astype(BF)
    noised = (
        (1.0 - sigma_t) * latents.astype(F32) + sigma_t * my_half(teacher_noise[0]).astype(F32)
    ).astype(BF)

    def both(values):
        other = sibling(values)
        first = jnp.where(at_core == 0, values, other)
        second = jnp.where(at_core == 0, other, values)
        return jnp.concatenate([first, second], axis=0)

    latents = both(latents)

    first_sib = sibling(first_own)

    token_rows = pltpu.VMEM((half, width), BF)
    inner = pltpu.VMEM((2, half, hidden), BF)
    rows_out = array((4, quarter, width), BF)
    mine_out = array((quarter, width), BF)
    inner_out = array((2, half, hidden), BF)
    y_0, slope_0, g_0, back_0 = here(
        first_forward_kernel,
        "first_forward",
        (array((half, width), BF), inner_out, array((half, width), BF), array((half, 2 * cells), F32)),
        (noised, proj_t, first_own, first_sib, t_w2, w2_sib),
        far=2,
        far_out=(0, 1),
        scratch=(
            pltpu.VMEM((2, hidden, width), BF),
            token_rows,
            inner,
            pltpu.SemaphoreType.DMA((4,)),
        ),
        limit=32,
    )

    def sums(partial, plan, sources):
        parts = swap_y(partial.reshape(4, quarter, width))
        sources, _ = lax.optimization_barrier((sources, partial))
        weights = resident(plan, sources)
        parts, weights = lax.optimization_barrier((parts, weights))
        return parts, weights

    last = (t_w1, w1_sib, t_w2, w2_sib)
    parts, weights = sums(y_0, (1, 1), last)
    g_1_mine, g_1 = here(
        first_middle_kernel,
        "first_middle",
        (mine_out, rows_out),
        (at_y.reshape(1), parts, g_0, gates[0]),
        scalars=1,
    )
    g_1 = swap_y(g_1).reshape(half, width)
    y_1, slope_1 = here(
        forward_kernel,
        "forward",
        (array((half, width), BF), inner_out),
        (g_1, scales[1], shifts[1]) + tuple(weights),
        far_out=(0, 1),
        scratch=(token_rows, inner, pltpu.SemaphoreType.DMA((2,))),
    )
    g_2_mine, g_2 = here(
        last_middle_kernel,
        "last_middle",
        (mine_out, rows_out),
        (swap_y(y_1.reshape(4, quarter, width)), g_1_mine, gates[1]),
    )
    head_own, d_w2_late, _ = lax.optimization_barrier((head_own, d_w2, g_2_mine))
    head_sib = sibling(head_own)
    d_w2_sib = sibling(d_w2_late)
    g_2 = swap_y(g_2).reshape(half, width)

    outs = jnp.pad(jnp.stack([d_w2, d_w2_sib]), ((0, 0), (0, 0), (0, spare)))
    use = [outs * (layer_pick[0] == layer).astype(F32)[None, :, None] for layer in range(layers)]

    def head(name, g, use):
        return here(
            head_kernel,
            name,
            (array((half, width), BF), array((half, 128), F32)),
            (g, use, head_own, head_sib),
            far=2,
            far_out=(0,),
            scratch=(
                pltpu.VMEM((2,) + head_own.shape, BF),
                token_rows,
                pltpu.SemaphoreType.DMA((3,)),
            ),
        )

    head_back_2, scores_2 = head("head_last", g_2, use[1])

    parts, weights = sums(head_back_2, (1, 1), last)
    dg_2, dy_1 = here(
        last_back_kernel,
        "last_back",
        (array((quarter, width), F32), rows_out),
        (parts, g_2_mine, gates[1]),
    )
    g_1, _ = lax.optimization_barrier((g_1, dg_2))
    head_back_1, scores_1 = head("head_first", g_1, use[0])
    du_1 = here(
        backward_kernel,
        "backward",
        array((half, width), BF),
        (swap_y(dy_1).reshape(half, width), scales[1]) + tuple(weights) + (slope_1, head_back_1),
        far=2,
        far_out=(0,),
        scratch=(inner, token_rows, token_rows, pltpu.SemaphoreType.DMA((3,))),
    )
    parts, weights = sums(du_1, (0,), (t_w2, w2_sib))
    direct, dy_0 = here(
        first_back_kernel,
        "first_back",
        (array((quarter, cells), F32), rows_out),
        (parts, g_1_mine, dg_2, gates[0], proj_t),
    )
    final = here(
        first_backward_kernel,
        "first_backward",
        array((half, 2 * cells), F32),
        (
            at_y.reshape(1),
            (1.0 - sigma_t).reshape(1),
            swap_y(dy_0).reshape(half, width),
            noised,
            back_0,
            scores_1 + scores_2,
            direct,
            first_own,
            first_sib,
        )
        + tuple(weights)
        + (slope_0,),
        scalars=2,
        far=1,
        scratch=(inner, pltpu.SemaphoreType.DMA((1,))),
    )
    final = final + lax.ppermute(final, "y", [(0, 1), (1, 0), (2, 3), (3, 2)])
    final = final + lax.ppermute(final, "y", [(0, 2), (2, 0), (1, 3), (3, 1)])
    final = both(final)
    return (latents[None], final[:, cells : cells + heads].T[None], final[:, :cells][None])


def solution(mesh):
    names = list(mesh.axis_names)
    shape = list(mesh.devices.shape)
    at = names.index("tp")
    names[at : at + 1] = ["y", "core"]
    shape[at : at + 1] = [4, 2]
    fine = Mesh(mesh.devices.reshape(shape), tuple(names))
    placed = (
        P(SAMPLE, None, None),
        P(),
        P(),
        P(SAMPLE, None, None),
        P(SAMPLE, None),
        P(None, TP),
        P(None, TP),
        P(None, TP),
        P(SAMPLE, TP),
        P(SAMPLE, TP),
        P(TP, SAMPLE),
        P(None, SAMPLE, TP),
        P(None, None, TP),
        P(None, TP, None),
        P(SAMPLE, TP),
        P(None, TP),
    )
    return jax.shard_map(
        body,
        mesh=fine,
        in_specs=placed,
        out_specs=(P(SAMPLE, None, None), P(SAMPLE, None, None), P(SAMPLE, None, None)),
        check_vma=False,
    )
```

```python
import functools
import math

import jax
import jax.numpy as jnp
from jax import lax
from jax.experimental import pallas as pl
from jax.experimental.pallas import tpu as pltpu
from jax.sharding import Mesh
from jax.sharding import PartitionSpec as P

HIGH = lax.Precision.HIGHEST
SAMPLE = ("fsdp", "grp")
TP = ("y", "core")
STEPS = 4
LAYERS = 2
BF = jnp.bfloat16
F32 = jnp.float32


def embed_block(times, width, block, start):
    half = width // 2
    column = start + jnp.arange(block)
    steps = jnp.where(column < half, column, column - half).astype(F32)
    freq = jnp.exp(-math.log(10000.0) * steps / half)
    angle = times[:, None] * freq[None, :]
    return jnp.where((column < half)[None, :], jnp.cos(angle), jnp.sin(angle))


def normalize(values):
    mean = jnp.mean(values, axis=-1, keepdims=True)
    centered = values - mean
    inverse = lax.rsqrt(jnp.mean(centered * centered, axis=-1, keepdims=True) + 1e-06)
    return (centered * inverse, inverse)


def ln_back(grad, normed, inverse):
    mean_grad = jnp.mean(grad, axis=-1, keepdims=True)
    mean_cross = jnp.mean(grad * normed, axis=-1, keepdims=True)
    return inverse * (grad - mean_grad - normed * mean_cross)


def gelu_both(values):
    inner = 0.7978845608 * (values + 0.044715 * values * values * values)
    tangent = jnp.tanh(inner)
    halved = 0.5 * (1.0 + tangent)
    slope = halved + 0.5 * values * (1.0 - tangent * tangent) * 0.7978845608 * (
        1.0 + 3.0 * 0.044715 * values * values
    )
    return values * halved, slope


def dot(left, right):
    return jnp.dot(left, right, preferred_element_type=F32)


def dot_back(left, right):
    return lax.dot_general(left, right, (((1,), (1,)), ((), ())), preferred_element_type=F32)


def dot_across(left, right):
    return lax.dot_general(left, right, (((0,), (0,)), ((), ())), preferred_element_type=F32)


def split(values):
    high = values.astype(BF)
    return high, (values - high.astype(F32)).astype(BF)


def sibling(values):
    return lax.ppermute(values, "core", [(0, 1), (1, 0)])


def swap_y(values):
    return lax.all_to_all(values, "y", 0, 0)


class Stream:
    def __init__(self, plan, sems):
        self.copies = [
            pltpu.make_async_copy(source, target, sems.at[index])
            for index, (source, target) in enumerate(plan)
        ]
        for copy in self.copies:
            copy.start()
        self.at = 0

    def next(self):
        self.copies[self.at].wait()
        self.at += 1


def matrices(layer, sources, target):
    return [(source.at[layer], target.at[side]) for side, source in enumerate(sources)]


def turned(values):
    extent = values.shape[1]
    row = lax.broadcasted_iota(jnp.int32, (extent, extent), 0)
    col = lax.broadcasted_iota(jnp.int32, (extent, extent), 1)
    return dot_back((row == col).astype(BF), values)


def product_kernel(at_ref, packed_ref, w1_ref, w2_ref, out_ref, bias_ref):
    blocks, columns, _ = packed_ref.shape
    rows, hidden = w1_ref.shape
    cells = out_ref.shape[0] // STEPS
    pick_row = lax.broadcasted_iota(jnp.int32, (rows, columns), 0)
    pick_col = lax.broadcasted_iota(jnp.int32, (rows, columns), 1)
    mine = (pick_col == pick_row + rows * at_ref[1]).astype(BF)
    total = jnp.zeros((columns, cells), F32)
    for block in range(blocks):
        total = total + packed_ref[block, :, :cells].astype(F32)
    mean = jnp.sum(total, axis=0, keepdims=True) / (blocks * columns)
    local = dot(mine, packed_ref[at_ref[0]])
    high, low = split(local[:, :cells] - mean)
    out_rows = local[:, 2 * cells : 3 * cells].astype(BF)

    def modulation(index):
        block = dot(mine, packed_ref[at_ref[2 * index + 2]]).astype(BF)[:, 3 * cells :]
        row = lax.broadcasted_iota(jnp.int32, (block.shape[1], 8), 0)
        kind = lax.broadcasted_iota(jnp.int32, (block.shape[1], 8), 1)
        want = (row == 3 * (kind + LAYERS) + at_ref[2 * index + 3]) & (kind < STEPS)
        return dot(block, want.astype(BF)).astype(BF)

    shift, scale, gate = modulation(0), modulation(1), modulation(2)
    cell_row = lax.broadcasted_iota(jnp.int32, (cells, cells * STEPS), 0)
    cell_col = lax.broadcasted_iota(jnp.int32, (cells, cells * STEPS), 1)
    by_cell = (cell_col // STEPS == cell_row).astype(BF)
    step_row = lax.broadcasted_iota(jnp.int32, (8, cells * STEPS), 0)
    step_col = lax.broadcasted_iota(jnp.int32, (8, cells * STEPS), 1)
    by_step = (step_col % STEPS == step_row).astype(BF)
    left_in = (dot(high, by_cell) + dot(low, by_cell)) * (1.0 + dot(scale, by_step))
    left_out = dot(out_rows, by_cell) * dot(gate, by_step)
    gap = -hidden % 128
    out_ref[:, :hidden] = dot_across(left_in.astype(BF), w1_ref[...]).astype(BF)
    out_ref[:, hidden : hidden + gap] = jnp.zeros((cells * STEPS, gap), BF)
    out_ref[:, hidden + gap :] = dot_across(left_out.astype(BF), w2_ref[...]).astype(BF)
    bias_ref[...] = dot_across(shift, w1_ref[...]).astype(BF)


def select_kernel(parts_ref, pick_ref, pick_bias_ref, bias_ref, out_ref):
    hidden = bias_ref.shape[1]
    total = parts_ref[0].astype(F32)
    for source in range(1, parts_ref.shape[0]):
        total = total + parts_ref[source].astype(F32)
    chosen = dot(pick_ref[...], total.astype(BF))
    out_ref[...] = chosen.astype(BF)
    out_ref[:, :hidden] = (chosen[:, :hidden] + dot(pick_bias_ref[...], bias_ref[...])).astype(BF)


def student_kernel(x_ref, inverse_ref, mat_ref, out_ref):
    cells = x_ref.shape[1]
    lanes, wide = mat_ref.shape
    hidden = wide // 2 - (wide // 2) % 64
    gap = wide - 2 * hidden
    group = lanes * 4 // cells
    row = lax.broadcasted_iota(jnp.int32, (cells, lanes), 0)
    col = lax.broadcasted_iota(jnp.int32, (cells, lanes), 1)
    spread = (col == group * (row // 4) + row % 4).astype(BF)
    bias_col = lax.broadcasted_iota(jnp.int32, (8, lanes), 1)
    bias = dot((bias_col % group == 4).astype(BF), mat_ref[:, :hidden])[:1]
    x = dot(x_ref[...], spread).astype(BF)
    z = inverse_ref[...] * dot(x, mat_ref[:, :hidden]) + bias
    active = gelu_both(z)[0].astype(BF)
    high, low = split(dot_back(active, mat_ref[:, hidden + gap :]))
    out_ref[...] = dot_back(high, spread) + dot_back(low, spread)


def first_product_kernel(proj_ref, scale_ref, shift_ref, up, out_ref, up_ref, sems):
    cells = proj_ref.shape[1]
    stream = Stream(matrices(0, (up,), up_ref), sems)
    proj = turned(proj_ref[...])
    centered = proj - jnp.mean(proj, axis=1, keepdims=True)
    left = (centered * (1.0 + scale_ref[...])).astype(BF)
    shift = jnp.broadcast_to(shift_ref[...], (16, shift_ref.shape[1])).astype(BF)
    left = jnp.concatenate([left, shift], axis=0)
    stream.next()
    out_ref[...] = dot_back(left, up_ref[0])[: cells + 8]


def first_forward_kernel(
    x_ref, proj_ref, mat_own, mat_sib, own, sib, y_out, slope_out, g_ref, back_ref, w_ref, y_ref, slope_ref, sems
):
    cells = x_ref.shape[1]
    stream = Stream(matrices(0, (own, sib), w_ref), sems)
    x = x_ref[...]
    g_0 = dot_back(x, proj_ref[...]).astype(BF)
    g_ref[...] = g_0
    normed, inverse = normalize(g_0.astype(F32))
    back_ref[:, :cells] = dot(normed.astype(BF), proj_ref[...])
    back_ref[:, cells:] = jnp.broadcast_to(inverse, (x.shape[0], cells))
    twice = jnp.concatenate([x, x], axis=1)
    actives = []
    for side, mat_ref in enumerate((mat_own, mat_sib)):
        high, low = split(mat_ref[:cells])
        z = inverse * dot(twice, jnp.concatenate([high, low], axis=0)) + mat_ref[cells : cells + 1]
        active, slope = gelu_both(z)
        slope_ref[side] = slope.astype(BF)
        actives.append(active.astype(BF))
    keep = pltpu.make_async_copy(slope_ref, slope_out, sems.at[2])
    keep.start()
    stream.next()
    y = dot(actives[0], w_ref[0])
    stream.next()
    y_ref[...] = (y + dot(actives[1], w_ref[1])).astype(BF)
    send = pltpu.make_async_copy(y_ref, y_out, sems.at[3])
    send.start()
    keep.wait()
    send.wait()


def forward_kernel(
    g_ref, scale_ref, shift_ref, up_own, up_sib, down_own, down_sib, y_out, slope_out,
    up_ref, down_ref, y_ref, slope_ref, sems
):
    stream = Stream(
        matrices(1, (up_own, up_sib), up_ref) + matrices(1, (down_own, down_sib), down_ref), sems
    )
    normed, _ = normalize(g_ref[...].astype(F32))
    u = (normed * (1.0 + scale_ref[...]) + shift_ref[...]).astype(BF)
    actives = []
    for side in range(2):
        stream.next()
        active, slope = gelu_both(dot_back(u, up_ref[side]))
        slope_ref[side] = slope.astype(BF)
        actives.append(active.astype(BF))
    keep = pltpu.make_async_copy(slope_ref, slope_out, sems.at[4])
    keep.start()
    stream.next()
    y = dot(actives[0], down_ref[0])
    stream.next()
    y_ref[...] = (y + dot(actives[1], down_ref[1])).astype(BF)
    send = pltpu.make_async_copy(y_ref, y_out, sems.at[5])
    send.start()
    keep.wait()
    send.wait()


def backward_kernel(
    dy_ref, scale_ref, slope, head, up_own, up_sib, down_own, down_sib, out,
    up_ref, down_ref, slope_ref, head_ref, out_ref, sems
):
    stream = Stream(
        [(slope, slope_ref)]
        + matrices(1, (down_own, down_sib), down_ref)
        + matrices(1, (up_own, up_sib), up_ref)
        + [(head, head_ref)],
        sems,
    )
    dy = dy_ref[...]
    stream.next()
    dz = []
    for side in range(2):
        stream.next()
        dz.append((dot_back(dy, down_ref[side]) * slope_ref[side].astype(F32)).astype(BF))
    stream.next()
    du = dot(dz[0], up_ref[0])
    stream.next()
    du = du + dot(dz[1], up_ref[1])
    stream.next()
    out_ref[...] = (du * (1.0 + scale_ref[...]) + head_ref[...].astype(F32)).astype(BF)
    send = pltpu.make_async_copy(out_ref, out, sems.at[6])
    send.start()
    send.wait()


def first_backward_kernel(
    at_ref, rest_ref, dy_ref, x_ref, back_ref, score_ref, direct_ref, mat_own, mat_sib, slope, own, sib,
    out_ref, w_ref, slope_ref, sems
):
    cells = x_ref.shape[1]
    stream = Stream([(slope, slope_ref)] + matrices(0, (own, sib), w_ref), sems)
    dy = dy_ref[...]
    stream.next()
    total = None
    for side, mat_ref in enumerate((mat_own, mat_sib)):
        high, low = split(mat_ref[:cells])
        stream.next()
        dz = (dot_back(dy, w_ref[side]) * slope_ref[side].astype(F32)).astype(BF)
        part = dot_back(dz, high) + dot_back(dz, low)
        total = part if total is None else total + part
    inverse = back_ref[:, cells : cells + 1]
    cross = inverse * jnp.sum(x_ref[...].astype(F32) * total, axis=1, keepdims=True) / dy.shape[1]
    rest = rest_ref[0]
    out_ref[:, :cells] = rest * (inverse * (total - back_ref[:, :cells] * cross))
    out_ref[:, cells:] = score_ref[:, :cells]
    rows = direct_ref.shape[0]
    mine = pl.ds(pl.multiple_of(at_ref[0] * rows, rows), rows)
    out_ref[mine, :cells] += rest * direct_ref[...]


def modulation_kernel(cond_s_ref, cond_t_ref, s_ref, t_ref, out_ref):
    samples = cond_t_ref.shape[0]

    def product(cond, weight):
        extent = cond.shape[0]
        high, rest = split(cond)
        rest = cond - high.astype(F32)
        middle, low = split(rest)
        parts = dot(jnp.concatenate([high, middle, low], axis=0), weight)
        return (parts[:extent] + (parts[extent : 2 * extent] + parts[2 * extent :])).astype(BF)

    def place(extent, first, every):
        row = lax.broadcasted_iota(jnp.int32, (samples * 8, extent), 0)
        col = lax.broadcasted_iota(jnp.int32, (samples * 8, extent), 1)
        if every:
            return (row % 8 == first + col).astype(BF)
        return ((row // 8 == col) & (row % 8 == first)).astype(BF)

    total = dot(place(16, LAYERS, True), product(cond_s_ref[...], s_ref[...]))
    for layer in range(LAYERS):
        part = product(cond_t_ref[...], t_ref[layer])
        total = total + dot(place(samples, layer, False), part)
    out_ref[...] = total.astype(BF)


def sum_parts(parts_ref):
    total = parts_ref[0].astype(F32)
    for source in range(1, parts_ref.shape[0]):
        total = total + parts_ref[source].astype(F32)
    return total


def share(values, all_ref):
    for target in range(all_ref.shape[0]):
        all_ref[target] = values


def first_middle_kernel(at_ref, parts_ref, g_ref, gate_ref, mine_ref, all_ref):
    rows = mine_ref.shape[0]
    before = g_ref[pl.ds(pl.multiple_of(at_ref[0] * rows, rows), rows), :].astype(F32)
    after = (before + gate_ref[...] * sum_parts(parts_ref)).astype(BF)
    mine_ref[...] = after
    share(after, all_ref)


def last_middle_kernel(parts_ref, g_ref, gate_ref, mine_ref, all_ref):
    after = (g_ref[...].astype(F32) + gate_ref[...] * sum_parts(parts_ref)).astype(BF)
    mine_ref[...] = after
    share(after, all_ref)


def last_back_kernel(parts_ref, g_ref, gate_ref, grad_ref, all_ref):
    normed, inverse = normalize(g_ref[...].astype(F32))
    grad = ln_back(sum_parts(parts_ref), normed, inverse)
    grad_ref[...] = grad
    share((gate_ref[...] * grad).astype(BF), all_ref)


def first_back_kernel(parts_ref, g_ref, old_ref, gate_ref, proj_ref, direct_ref, all_ref):
    normed, inverse = normalize(g_ref[...].astype(F32))
    grad = old_ref[...] + ln_back(sum_parts(parts_ref), normed, inverse)
    direct_ref[...] = dot(grad.astype(BF), proj_ref[...])
    share((gate_ref[...] * grad).astype(BF), all_ref)


def head_kernel(g_ref, use_ref, own, sib, back_out, score_ref, weight_ref, back_ref, sems):
    stream = Stream([(own, weight_ref.at[0]), (sib, weight_ref.at[1])], sems)
    normed, _ = normalize(g_ref[...].astype(F32))
    quantised = normed.astype(BF)
    back = None
    scores = None
    for side in range(2):
        stream.next()
        weight = weight_ref[side]
        e = dot(quantised, weight)
        sigm = 1.0 / (1.0 + jnp.exp(-e))
        active = e * sigm
        outs = use_ref[side]
        slope = sigm * (1.0 + e * (1.0 - sigm))
        part = dot_back((-(outs[0:1] + outs[1:2]) * slope).astype(BF), weight)
        back = part if back is None else back + part
        part = [jnp.sum(active * outs[head : head + 1], axis=1, keepdims=True) for head in range(2)]
        scores = part if scores is None else [old + new for old, new in zip(scores, part)]
    back_ref[...] = back.astype(BF)
    send = pltpu.make_async_copy(back_ref, back_out, sems.at[2])
    send.start()
    lane = lax.broadcasted_iota(jnp.int32, score_ref.shape, 1)
    score_ref[...] = jnp.where(lane == 0, scores[0], 0.0) + jnp.where(lane == 1, scores[1], 0.0)
    send.wait()


WHOLE = pl.BlockSpec(memory_space=pltpu.VMEM)
FAR = pl.BlockSpec(memory_space=pltpu.HBM)


def here(kernel, name, out_shape, operands, scalars=0, far=0, far_out=(), scratch=(), limit=20):
    many = isinstance(out_shape, tuple)
    near = len(operands) - scalars - far
    shapes = tuple(
        pltpu.HBM(shape.shape, shape.dtype) if index in far_out else shape
        for index, shape in enumerate(out_shape if many else (out_shape,))
    )
    operands = operands[: scalars + near] + tuple(
        pltpu.with_memory_space_constraint(operand, pltpu.HBM) for operand in operands[scalars + near :]
    )
    specs = tuple(
        FAR if index in far_out else WHOLE for index in range(len(out_shape) if many else 1)
    )
    return pl.pallas_call(
        kernel,
        name=name,
        out_shape=shapes if many else shapes[0],
        in_specs=[pl.BlockSpec(memory_space=pltpu.SMEM)] * scalars + [WHOLE] * near + [FAR] * far,
        out_specs=specs if many else specs[0],
        scratch_shapes=list(scratch),
        compiler_params=pltpu.CompilerParams(vmem_limit_bytes=limit * 2**20),
    )(*operands)


def array(shape, dtype):
    return jax.ShapeDtypeStruct(shape, dtype)


def body(
    noisy_latents,
    student_step,
    teacher_step,
    teacher_noise,
    layer_pick,
    in_proj_s,
    in_proj_t,
    out_proj,
    s_mod,
    s_w1,
    s_w2,
    t_mod,
    t_w1,
    t_w2,
    d_w1,
    d_w2,
):
    cells = in_proj_s.shape[0]
    width = in_proj_s.shape[1] * 8
    samples = student_step.shape[0]
    layers = t_w1.shape[0]
    heads = d_w2.shape[0]
    seq = noisy_latents.shape[1]
    half = seq // 2
    quarter = half // 4
    rows = s_mod.shape[0]
    hidden = s_w1.shape[1]
    columns = in_proj_s.shape[1]
    sample = lax.axis_index(SAMPLE)
    at_y = lax.axis_index("y")
    at_core = lax.axis_index("core")
    start = sample * rows

    sig_all_t = teacher_step.astype(F32) * 0.001
    sig_steps = (1 + jnp.arange(STEPS)).astype(F32) * 0.25
    cond_s = jax.nn.silu(embed_block(1000.0 * sig_steps, width, rows, start))
    cond_t = jax.nn.silu(embed_block(1000.0 * sig_all_t, width, rows, start))
    mod_part = here(
        modulation_kernel,
        "modulation",
        array((samples * 8, s_mod.shape[1]), BF),
        (jnp.pad(cond_s, ((0, 16 - STEPS), (0, 0))), cond_t, s_mod, t_mod),
    ).reshape(samples, 8, s_mod.shape[1])
    mods = jnp.sum(lax.all_to_all(mod_part, SAMPLE, 0, 0).astype(F32), axis=0)
    kinds = layers + STEPS
    mods = mods[:kinds].reshape(kinds * 3, columns).astype(BF)
    packed = jnp.concatenate([in_proj_s, in_proj_t, out_proj, mods], axis=0).T
    gathered = lax.all_gather(packed, TP, axis=0, tiled=False)

    block = lax.axis_index(SAMPLE) * rows // columns
    places = [block, sample * rows // rows % (columns // rows)]
    for offset in (0, 8, 16):
        places += [(block + offset) // 3, (block + offset) % 3]
    gap = -hidden % 128
    both_wide = 2 * hidden + gap
    parts, part_bias = here(
        product_kernel,
        "product",
        (
            jax.ShapeDtypeStruct((cells * STEPS, both_wide), BF),
            jax.ShapeDtypeStruct((8, hidden), BF),
        ),
        (jnp.stack(places).astype(jnp.int32), gathered, s_w1, s_w2.T),
        scalars=1,
    )
    piece = cells * STEPS // samples
    chunk = cells // samples
    t_w1 = jnp.swapaxes(t_w1, 1, 2)
    parts, gathered, t_w1, t_w2 = lax.optimization_barrier((parts, gathered, t_w1, t_w2))
    received = lax.all_to_all(parts.reshape(samples, piece, both_wide), SAMPLE, 0, 0)

    mods = gathered[:, :, 3 * cells :].astype(F32).reshape(8, columns, kinds, 3)
    mod_teacher = mods[:, :, :layers].transpose(2, 0, 3, 1).reshape(layers, 1, 3 * width)
    packed = gathered.reshape(width, -1)
    proj_s, proj_t, proj_out = (packed[:, at * cells : (at + 1) * cells] for at in range(3))
    shifts = [mod_teacher[l, :, :width] for l in range(layers)]
    scales = [mod_teacher[l, :, width : 2 * width] for l in range(layers)]
    gates = [mod_teacher[l, :, 2 * width :] for l in range(layers)]
    first_own = here(
        first_product_kernel,
        "first_product",
        array((cells + 8, hidden), F32),
        (proj_t, scales[0], shifts[0], t_w1),
        far=1,
        scratch=(pltpu.VMEM((1, hidden, width), BF), pltpu.SemaphoreType.DMA((1,))),
        limit=44,
    )
    latent_in = noisy_latents[0]
    h0 = dot_back(latent_in, proj_s).astype(BF)
    _, inverse_s = normalize(h0.astype(F32))
    received, first_own, inverse_s = lax.optimization_barrier((received, first_own, inverse_s))

    w2_sib = sibling(t_w2)
    w1_sib = sibling(t_w1)

    at_row = jnp.arange(samples * 8)
    step_at = jnp.repeat(student_step - 1, 8)
    pick = (
        ((at_row % 8 * STEPS + step_at)[:, None] == jnp.arange(piece)[None])
        & (at_row % 8 < chunk)[:, None]
    ).astype(BF)
    pick_bias = ((step_at[:, None] == jnp.arange(8)[None]) & (at_row % 8 == chunk)[:, None]).astype(BF)
    chosen = here(
        select_kernel,
        "select",
        jax.ShapeDtypeStruct((samples * 8, both_wide), BF),
        (received, pick, pick_bias, part_bias),
    )
    mine = lax.all_to_all(chosen.reshape(samples, 8, both_wide), SAMPLE, 0, 0)
    mine = mine.reshape(samples * 8, both_wide)
    my_step = lax.dynamic_index_in_dim(student_step, sample, keepdims=False)

    spare = -columns % 128
    head_block, _ = lax.optimization_barrier((jnp.pad(d_w1, ((0, 0), (0, spare))), mine))
    head_own = lax.all_gather(head_block, SAMPLE, axis=0, tiled=True)

    sigma_s = my_step.astype(F32) * 0.25
    sigma_t = lax.dynamic_index_in_dim(sig_all_t, sample, keepdims=False)
    velocity = here(
        student_kernel,
        "student",
        jax.ShapeDtypeStruct((seq, cells), F32),
        (latent_in, inverse_s, mine),
    )
    mine_first = lax.dynamic_slice_in_dim(velocity, at_core * half, half, 0)
    other = lax.dynamic_slice_in_dim(velocity, (1 - at_core) * half, half, 0)
    velocity = mine_first + sibling(other)
    velocity = velocity + lax.ppermute(velocity, "y", [(0, 1), (1, 0), (2, 3), (3, 2)])
    velocity = velocity + lax.ppermute(velocity, "y", [(0, 2), (2, 0), (1, 3), (3, 1)])

    def my_half(values):
        return lax.dynamic_slice_in_dim(values, at_core * half, half, 0)

    velocity = velocity + dot(my_half(h0), proj_out)
    latents = (my_half(latent_in).astype(F32) - sigma_s * velocity).astype(BF)
    noised = (
        (1.0 - sigma_t) * latents.astype(F32) + sigma_t * my_half(teacher_noise[0]).astype(F32)
    ).astype(BF)

    def both(values):
        other = sibling(values)
        first = jnp.where(at_core == 0, values, other)
        second = jnp.where(at_core == 0, other, values)
        return jnp.concatenate([first, second], axis=0)

    latents = both(latents)

    first_sib = sibling(first_own)

    token_rows = pltpu.VMEM((half, width), BF)
    inner = pltpu.VMEM((2, half, hidden), BF)
    rows_out = array((4, quarter, width), BF)
    mine_out = array((quarter, width), BF)
    inner_out = array((2, half, hidden), BF)
    y_0, slope_0, g_0, back_0 = here(
        first_forward_kernel,
        "first_forward",
        (array((half, width), BF), inner_out, array((half, width), BF), array((half, 2 * cells), F32)),
        (noised, proj_t, first_own, first_sib, t_w2, w2_sib),
        far=2,
        far_out=(0, 1),
        scratch=(
            pltpu.VMEM((2, hidden, width), BF),
            token_rows,
            inner,
            pltpu.SemaphoreType.DMA((4,)),
        ),
        limit=44,
    )

    def sums(partial):
        return swap_y(partial.reshape(4, quarter, width))

    last = (t_w1, w1_sib, t_w2, w2_sib)
    matrix = pltpu.VMEM((2, hidden, width), BF)
    g_1_mine, g_1 = here(
        first_middle_kernel,
        "first_middle",
        (mine_out, rows_out),
        (at_y.reshape(1), sums(y_0), g_0, gates[0]),
        scalars=1,
    )
    g_1 = swap_y(g_1).reshape(half, width)
    y_1, slope_1 = here(
        forward_kernel,
        "forward",
        (array((half, width), BF), inner_out),
        (g_1, scales[1], shifts[1]) + last,
        far=4,
        far_out=(0, 1),
        scratch=(matrix, matrix, token_rows, inner, pltpu.SemaphoreType.DMA((6,))),
        limit=44,
    )
    g_2_mine, g_2 = here(
        last_middle_kernel,
        "last_middle",
        (mine_out, rows_out),
        (sums(y_1), g_1_mine, gates[1]),
    )
    head_own, d_w2_late, _ = lax.optimization_barrier((head_own, d_w2, g_2_mine))
    head_sib = sibling(head_own)
    d_w2_sib = sibling(d_w2_late)
    g_2 = swap_y(g_2).reshape(half, width)

    outs = jnp.pad(jnp.stack([d_w2, d_w2_sib]), ((0, 0), (0, 0), (0, spare)))
    use = [outs * (layer_pick[0] == layer).astype(F32)[None, :, None] for layer in range(layers)]

    def head(name, g, use):
        return here(
            head_kernel,
            name,
            (array((half, width), BF), array((half, 128), F32)),
            (g, use, head_own, head_sib),
            far=2,
            far_out=(0,),
            scratch=(
                pltpu.VMEM((2,) + head_own.shape, BF),
                token_rows,
                pltpu.SemaphoreType.DMA((3,)),
            ),
        )

    head_back_2, scores_2 = head("head_last", g_2, use[1])

    dg_2, dy_1 = here(
        last_back_kernel,
        "last_back",
        (array((quarter, width), F32), rows_out),
        (sums(head_back_2), g_2_mine, gates[1]),
    )
    g_1, _ = lax.optimization_barrier((g_1, dg_2))
    head_back_1, scores_1 = head("head_first", g_1, use[0])
    du_1 = here(
        backward_kernel,
        "backward",
        array((half, width), BF),
        (swap_y(dy_1).reshape(half, width), scales[1], slope_1, head_back_1) + last,
        far=6,
        far_out=(0,),
        scratch=(matrix, matrix, inner, token_rows, token_rows, pltpu.SemaphoreType.DMA((7,))),
        limit=44,
    )
    direct, dy_0 = here(
        first_back_kernel,
        "first_back",
        (array((quarter, cells), F32), rows_out),
        (sums(du_1), g_1_mine, dg_2, gates[0], proj_t),
    )
    final = here(
        first_backward_kernel,
        "first_backward",
        array((half, 2 * cells), F32),
        (
            at_y.reshape(1),
            (1.0 - sigma_t).reshape(1),
            swap_y(dy_0).reshape(half, width),
            noised,
            back_0,
            scores_1 + scores_2,
            direct,
            first_own,
            first_sib,
            slope_0,
            t_w2,
            w2_sib,
        ),
        scalars=2,
        far=3,
        scratch=(matrix, inner, pltpu.SemaphoreType.DMA((3,))),
        limit=44,
    )
    final = final + lax.ppermute(final, "y", [(0, 1), (1, 0), (2, 3), (3, 2)])
    final = final + lax.ppermute(final, "y", [(0, 2), (2, 0), (1, 3), (3, 1)])
    final = both(final)
    return (latents[None], final[:, cells : cells + heads].T[None], final[:, :cells][None])


def solution(mesh):
    names = list(mesh.axis_names)
    shape = list(mesh.devices.shape)
    at = names.index("tp")
    names[at : at + 1] = ["y", "core"]
    shape[at : at + 1] = [4, 2]
    fine = Mesh(mesh.devices.reshape(shape), tuple(names))
    placed = (
        P(SAMPLE, None, None),
        P(),
        P(),
        P(SAMPLE, None, None),
        P(SAMPLE, None),
        P(None, TP),
        P(None, TP),
        P(None, TP),
        P(SAMPLE, TP),
        P(SAMPLE, TP),
        P(TP, SAMPLE),
        P(None, SAMPLE, TP),
        P(None, None, TP),
        P(None, TP, None),
        P(SAMPLE, TP),
        P(None, TP),
    )
    return jax.shard_map(
        body,
        mesh=fine,
        in_specs=placed,
        out_specs=(P(SAMPLE, None, None), P(SAMPLE, None, None), P(SAMPLE, None, None)),
        check_vma=False,
    )
```

```python
import functools
import math

import jax
import jax.numpy as jnp
from jax import lax
from jax.experimental import pallas as pl
from jax.experimental.pallas import tpu as pltpu
from jax.sharding import Mesh
from jax.sharding import PartitionSpec as P

HIGH = lax.Precision.HIGHEST
SAMPLE = ("fsdp", "grp")
TP = ("y", "core")
STEPS = 4
LAYERS = 2
BF = jnp.bfloat16
F32 = jnp.float32


def embed_block(times, width, block, start):
    half = width // 2
    column = start + jnp.arange(block)
    steps = jnp.where(column < half, column, column - half).astype(F32)
    freq = jnp.exp(-math.log(10000.0) * steps / half)
    angle = times[:, None] * freq[None, :]
    return jnp.where((column < half)[None, :], jnp.cos(angle), jnp.sin(angle))


def normalize(values):
    mean = jnp.mean(values, axis=-1, keepdims=True)
    centered = values - mean
    inverse = lax.rsqrt(jnp.mean(centered * centered, axis=-1, keepdims=True) + 1e-06)
    return (centered * inverse, inverse)


def ln_back(grad, normed, inverse):
    mean_grad = jnp.mean(grad, axis=-1, keepdims=True)
    mean_cross = jnp.mean(grad * normed, axis=-1, keepdims=True)
    return inverse * (grad - mean_grad - normed * mean_cross)


def gelu_both(values):
    inner = 0.7978845608 * (values + 0.044715 * values * values * values)
    tangent = jnp.tanh(inner)
    halved = 0.5 * (1.0 + tangent)
    slope = halved + 0.5 * values * (1.0 - tangent * tangent) * 0.7978845608 * (
        1.0 + 3.0 * 0.044715 * values * values
    )
    return values * halved, slope


def dot(left, right):
    return jnp.dot(left, right, preferred_element_type=F32)


def dot_back(left, right):
    return lax.dot_general(left, right, (((1,), (1,)), ((), ())), preferred_element_type=F32)


def dot_across(left, right):
    return lax.dot_general(left, right, (((0,), (0,)), ((), ())), preferred_element_type=F32)


def split(values):
    high = values.astype(BF)
    return high, (values - high.astype(F32)).astype(BF)


def sibling(values):
    return lax.ppermute(values, "core", [(0, 1), (1, 0)])


def swap_y(values):
    return lax.all_to_all(values, "y", 0, 0)


class Stream:
    def __init__(self, plan, sems):
        self.copies = [
            pltpu.make_async_copy(source, target, sems.at[index])
            for index, (source, target) in enumerate(plan)
        ]
        for copy in self.copies:
            copy.start()
        self.at = 0

    def next(self):
        self.copies[self.at].wait()
        self.at += 1


def matrices(layer, sources, target):
    return [(source.at[layer], target.at[side]) for side, source in enumerate(sources)]


def identity(extent):
    row = lax.broadcasted_iota(jnp.int32, (extent, extent), 0)
    col = lax.broadcasted_iota(jnp.int32, (extent, extent), 1)
    return (row == col).astype(BF)


def turned(values):
    return dot_back(identity(values.shape[1]), values)


def turned_wide(values):
    return dot_across(values, identity(values.shape[0]))


def product_kernel(at_ref, packed_ref, w1_ref, w2_ref, out, bias_ref, out_ref, sems):
    blocks, columns, _ = packed_ref.shape
    rows, hidden = w1_ref.shape
    cells = out_ref.shape[0] // STEPS
    pick_row = lax.broadcasted_iota(jnp.int32, (rows, columns), 0)
    pick_col = lax.broadcasted_iota(jnp.int32, (rows, columns), 1)
    mine = (pick_col == pick_row + rows * at_ref[1]).astype(BF)
    total = jnp.zeros((columns, cells), F32)
    for block in range(blocks):
        total = total + packed_ref[block, :, :cells].astype(F32)
    mean = jnp.sum(total, axis=0, keepdims=True) / (blocks * columns)
    local = dot(mine, packed_ref[at_ref[0]])
    high, low = split(local[:, :cells] - mean)
    out_rows = local[:, 2 * cells : 3 * cells].astype(BF)

    def modulation(index):
        block = dot(mine, packed_ref[at_ref[2 * index + 2]]).astype(BF)[:, 3 * cells :]
        row = lax.broadcasted_iota(jnp.int32, (block.shape[1], 8), 0)
        kind = lax.broadcasted_iota(jnp.int32, (block.shape[1], 8), 1)
        want = (row == 3 * (kind + LAYERS) + at_ref[2 * index + 3]) & (kind < STEPS)
        return dot(block, want.astype(BF)).astype(BF)

    shift, scale, gate = modulation(0), modulation(1), modulation(2)
    cell_row = lax.broadcasted_iota(jnp.int32, (cells, cells * STEPS), 0)
    cell_col = lax.broadcasted_iota(jnp.int32, (cells, cells * STEPS), 1)
    by_cell = (cell_col // STEPS == cell_row).astype(BF)
    step_row = lax.broadcasted_iota(jnp.int32, (8, cells * STEPS), 0)
    step_col = lax.broadcasted_iota(jnp.int32, (8, cells * STEPS), 1)
    by_step = (step_col % STEPS == step_row).astype(BF)
    left_in = (dot(high, by_cell) + dot(low, by_cell)) * (1.0 + dot(scale, by_step))
    left_out = dot(out_rows, by_cell) * dot(gate, by_step)
    gap = -hidden % 128
    out_ref[:, :hidden] = dot_across(left_in.astype(BF), w1_ref[...]).astype(BF)
    out_ref[:, hidden : hidden + gap] = jnp.zeros((cells * STEPS, gap), BF)
    out_ref[:, hidden + gap :] = dot_across(left_out.astype(BF), w2_ref[...]).astype(BF)
    send = pltpu.make_async_copy(out_ref, out, sems.at[0])
    send.start()
    bias_ref[...] = dot_across(shift, w1_ref[...]).astype(BF)
    send.wait()


def select_kernel(step_ref, parts_ref, bias_ref, out, out_ref, sems):
    samples, piece, _ = parts_ref.shape
    hidden = bias_ref.shape[1]
    chunk = piece // STEPS

    def at_step(extent):
        row = lax.broadcasted_iota(jnp.int32, (samples * 8, extent), 0)
        step = jnp.zeros((samples * 8, extent), jnp.int32)
        for sample in range(samples):
            step = jnp.where(row // 8 == sample, step_ref[sample] - 1, step)
        return row % 8, lax.broadcasted_iota(jnp.int32, (samples * 8, extent), 1), step

    total = parts_ref[0].astype(F32)
    for source in range(1, samples):
        total = total + parts_ref[source].astype(F32)
    place, col, step = at_step(piece)
    pick = ((col == place * STEPS + step) & (place < chunk)).astype(BF)
    chosen = dot(pick, total.astype(BF))
    out_ref[...] = chosen.astype(BF)
    place, col, step = at_step(8)
    pick = ((col == step) & (place == chunk)).astype(BF)
    out_ref[:, :hidden] = (chosen[:, :hidden] + dot(pick, bias_ref[...])).astype(BF)
    send = pltpu.make_async_copy(out_ref, out, sems.at[0])
    send.start()
    send.wait()


def student_kernel(where_ref, x_ref, packed_ref, mat_ref, mine_ref, other_ref, all_ref):
    cells, seq = x_ref.shape
    width = packed_ref.shape[0]
    lanes, wide = mat_ref.shape
    hidden = wide // 2 - (wide // 2) % 64
    gap = wide - 2 * hidden
    group = lanes * 4 // cells
    x = turned_wide(x_ref[...]).astype(BF)
    proj = packed_ref[:, :cells]
    centered = proj.astype(F32)
    centered = centered - jnp.mean(centered, axis=0, keepdims=True)
    high, low = split(centered)
    gram = dot_across(high, high) + (dot_across(high, low) + dot_across(low, high))
    direct = dot_across(proj, packed_ref[:, 2 * cells : 3 * cells])

    def times(matrix):
        first, second = split(matrix)
        return dot(x, first) + dot(x, second)

    var = jnp.sum(times(gram) * x.astype(F32), axis=1, keepdims=True) / width
    inverse = lax.rsqrt(jnp.maximum(var, 0.0) + 1e-06)
    row = lax.broadcasted_iota(jnp.int32, (cells, lanes), 0)
    col = lax.broadcasted_iota(jnp.int32, (cells, lanes), 1)
    spread = (col == group * (row // 4) + row % 4).astype(BF)
    bias_col = lax.broadcasted_iota(jnp.int32, (8, lanes), 1)
    bias = dot((bias_col % group == 4).astype(BF), mat_ref[:, :hidden])[:1]
    z = inverse * dot(dot(x, spread).astype(BF), mat_ref[:, :hidden]) + bias
    active = gelu_both(z)[0].astype(BF)
    high, low = split(dot_back(active, mat_ref[:, hidden + gap :]))
    all_ref[...] = dot_back(high, spread) + dot_back(low, spread) + 0.125 * times(direct)
    half = seq // 2
    core = where_ref[2]
    mine_ref[...] = all_ref[pl.ds(pl.multiple_of(core * half, half), half), :]
    other_ref[...] = all_ref[pl.ds(pl.multiple_of((1 - core) * half, half), half), :]


def first_product_kernel(packed_ref, up, out_ref, vector_ref, up_ref, left_ref, sems):
    blocks, columns, _ = packed_ref.shape
    cells = out_ref.shape[0] - 8
    stream = Stream(matrices(0, (up,), up_ref), sems)
    total = jnp.zeros((columns, cells), F32)
    for block in range(blocks):
        total = total + packed_ref[block, :, cells : 2 * cells].astype(F32)
    mean = jnp.sum(total, axis=0, keepdims=True) / (blocks * columns)

    def vector(kind, block):
        at = kind * blocks + block
        return packed_ref[at // 3, :, 3 * cells + at % 3 : 3 * cells + at % 3 + 1].astype(F32)

    for block in range(blocks):
        centered = packed_ref[block, :, cells : 2 * cells].astype(F32) - mean
        scaled = centered * (1.0 + vector(1, block))
        shift = jnp.broadcast_to(vector(0, block), (columns, 8))
        left_ref[block * columns : (block + 1) * columns, :] = jnp.concatenate(
            [scaled, shift], axis=1
        ).astype(BF)
    for source in range(blocks):
        rows = turned(packed_ref[source, :, 3 * cells : 3 * cells + 3 * LAYERS])
        for third in range(3):
            kind, block = divmod(source * 3 + third, blocks)
            for layer in range(LAYERS):
                vector_ref[
                    3 * layer + kind : 3 * layer + kind + 1, block * columns : (block + 1) * columns
                ] = rows[3 * layer + third : 3 * layer + third + 1]
    left = turned(left_ref[...]).astype(BF)
    stream.next()
    out_ref[...] = dot_back(left, up_ref[0])


def first_forward_kernel(
    where_ref, student_ref, teacher_ref, velocity_ref, x_ref, noise_ref, packed_ref, mat_own, mat_sib, own, sib,
    y_out, slope_out, latents_ref, noised_ref, g_ref, back_ref,
    w_ref, y_ref, slope_ref, both_ref, sems
):
    cells, seq = x_ref.shape
    half = seq // 2
    stream = Stream(matrices(0, (own, sib), w_ref), sems)
    sample = where_ref[0]
    sigma_s = student_ref[sample].astype(F32) * 0.25
    sigma_t = teacher_ref[sample].astype(F32) * 0.001
    both_ref[0] = turned_wide(x_ref[...])
    both_ref[1] = turned_wide(noise_ref[...])
    mine = pl.ds(pl.multiple_of(where_ref[2] * half, half), half)
    latents = (both_ref[0, mine, :] - sigma_s * velocity_ref[...]).astype(BF)
    latents_ref[...] = latents
    x = ((1.0 - sigma_t) * latents.astype(F32) + sigma_t * both_ref[1, mine, :]).astype(BF)
    noised_ref[...] = x
    proj = packed_ref[:, cells : 2 * cells]
    g_0 = dot_back(x, proj).astype(BF)
    g_ref[...] = g_0
    normed, inverse = normalize(g_0.astype(F32))
    back_ref[:, :cells] = dot(normed.astype(BF), proj)
    back_ref[:, cells:] = jnp.broadcast_to(inverse, (half, cells))
    twice = jnp.concatenate([x, x], axis=1)
    actives = []
    for side, mat_ref in enumerate((mat_own, mat_sib)):
        high, low = split(mat_ref[:cells])
        z = inverse * dot(twice, jnp.concatenate([high, low], axis=0)) + mat_ref[cells : cells + 1]
        active, slope = gelu_both(z)
        slope_ref[side] = slope.astype(BF)
        actives.append(active.astype(BF))
    keep = pltpu.make_async_copy(slope_ref, slope_out, sems.at[2])
    keep.start()
    stream.next()
    y = dot(actives[0], w_ref[0])
    stream.next()
    y_ref[...] = (y + dot(actives[1], w_ref[1])).astype(BF)
    send = pltpu.make_async_copy(y_ref, y_out, sems.at[3])
    send.start()
    keep.wait()
    send.wait()


def forward_kernel(
    g_ref, vector_ref, up_own, up_sib, down_own, down_sib, y_out, slope_out,
    up_ref, down_ref, y_ref, slope_ref, sems
):
    stream = Stream(
        matrices(1, (up_own, up_sib), up_ref) + matrices(1, (down_own, down_sib), down_ref), sems
    )
    normed, _ = normalize(g_ref[...].astype(F32))
    u = (normed * (1.0 + vector_ref[4:5]) + vector_ref[3:4]).astype(BF)
    actives = []
    for side in range(2):
        stream.next()
        active, slope = gelu_both(dot_back(u, up_ref[side]))
        slope_ref[side] = slope.astype(BF)
        actives.append(active.astype(BF))
    keep = pltpu.make_async_copy(slope_ref, slope_out, sems.at[4])
    keep.start()
    stream.next()
    y = dot(actives[0], down_ref[0])
    stream.next()
    y_ref[...] = (y + dot(actives[1], down_ref[1])).astype(BF)
    send = pltpu.make_async_copy(y_ref, y_out, sems.at[5])
    send.start()
    keep.wait()
    send.wait()


def backward_kernel(
    dy_ref, vector_ref, slope, head, up_own, up_sib, down_own, down_sib, out,
    up_ref, down_ref, slope_ref, head_ref, out_ref, sems
):
    stream = Stream(
        [(slope, slope_ref)]
        + matrices(1, (down_own, down_sib), down_ref)
        + matrices(1, (up_own, up_sib), up_ref)
        + [(head, head_ref)],
        sems,
    )
    dy = dy_ref[...]
    stream.next()
    dz = []
    for side in range(2):
        stream.next()
        dz.append((dot_back(dy, down_ref[side]) * slope_ref[side].astype(F32)).astype(BF))
    stream.next()
    du = dot(dz[0], up_ref[0])
    stream.next()
    du = du + dot(dz[1], up_ref[1])
    stream.next()
    out_ref[...] = (du * (1.0 + vector_ref[4:5]) + head_ref[...].astype(F32)).astype(BF)
    send = pltpu.make_async_copy(out_ref, out, sems.at[6])
    send.start()
    send.wait()


def first_backward_kernel(
    where_ref, teacher_ref, dy_ref, x_ref, back_ref, score_1, score_2, direct_ref, mat_own, mat_sib, slope, own, sib,
    out_ref, w_ref, slope_ref, all_ref, sems
):
    cells = x_ref.shape[1]
    stream = Stream([(slope, slope_ref)] + matrices(0, (own, sib), w_ref), sems)
    dy = dy_ref[...]
    stream.next()
    total = None
    for side, mat_ref in enumerate((mat_own, mat_sib)):
        high, low = split(mat_ref[:cells])
        stream.next()
        dz = (dot_back(dy, w_ref[side]) * slope_ref[side].astype(F32)).astype(BF)
        part = dot_back(dz, high) + dot_back(dz, low)
        total = part if total is None else total + part
    inverse = back_ref[:, cells : cells + 1]
    cross = inverse * jnp.sum(x_ref[...].astype(F32) * total, axis=1, keepdims=True) / dy.shape[1]
    rest = 1.0 - teacher_ref[where_ref[0]].astype(F32) * 0.001
    all_ref[:, :cells] = rest * (inverse * (total - back_ref[:, :cells] * cross))
    all_ref[:, cells:] = score_1[:, :cells] + score_2[:, :cells]
    rows = direct_ref.shape[0]
    mine = pl.ds(pl.multiple_of(where_ref[1] * rows, rows), rows)
    all_ref[mine, :cells] += rest * direct_ref[...]
    out_ref[...] = all_ref[...].T[: out_ref.shape[0]]


def modulation_kernel(cond_s_ref, cond_t_ref, s_ref, t_ref, in_s, in_t, out_proj, out_ref, proj_ref):
    samples = cond_t_ref.shape[0]

    def product(cond, weight):
        extent = cond.shape[0]
        high, rest = split(cond)
        rest = cond - high.astype(F32)
        middle, low = split(rest)
        parts = dot(jnp.concatenate([high, middle, low], axis=0), weight)
        return (parts[:extent] + (parts[extent : 2 * extent] + parts[2 * extent :])).astype(BF)

    def place(extent, first, every):
        row = lax.broadcasted_iota(jnp.int32, (samples * 8, extent), 0)
        col = lax.broadcasted_iota(jnp.int32, (samples * 8, extent), 1)
        if every:
            return (row % 8 == first + col).astype(BF)
        return ((row // 8 == col) & (row % 8 == first)).astype(BF)

    total = dot(place(16, LAYERS, True), product(cond_s_ref[...], s_ref[...]))
    for layer in range(LAYERS):
        part = product(cond_t_ref[...], t_ref[layer])
        total = total + dot(place(samples, layer, False), part)
    out_ref[...] = total.astype(BF)
    stacked = jnp.concatenate([in_s[...], in_t[...], out_proj[...]], axis=0)
    proj_ref[...] = turned_wide(stacked).astype(BF)


def sum_parts(parts_ref):
    total = parts_ref[0].astype(F32)
    for source in range(1, parts_ref.shape[0]):
        total = total + parts_ref[source].astype(F32)
    return total


def share(values, all_ref):
    for target in range(all_ref.shape[0]):
        all_ref[target] = values


def first_middle_kernel(where_ref, parts_ref, g_ref, vector_ref, mine_ref, all_ref):
    rows = mine_ref.shape[0]
    before = g_ref[pl.ds(pl.multiple_of(where_ref[1] * rows, rows), rows), :].astype(F32)
    after = (before + vector_ref[2:3] * sum_parts(parts_ref)).astype(BF)
    mine_ref[...] = after
    share(after, all_ref)


def last_middle_kernel(parts_ref, g_ref, vector_ref, mine_ref, all_ref):
    after = (g_ref[...].astype(F32) + vector_ref[5:6] * sum_parts(parts_ref)).astype(BF)
    mine_ref[...] = after
    share(after, all_ref)


def last_back_kernel(parts_ref, g_ref, vector_ref, grad_ref, all_ref):
    normed, inverse = normalize(g_ref[...].astype(F32))
    grad = ln_back(sum_parts(parts_ref), normed, inverse)
    grad_ref[...] = grad
    share((vector_ref[5:6] * grad).astype(BF), all_ref)


def first_back_kernel(parts_ref, g_ref, old_ref, vector_ref, packed_ref, direct_ref, all_ref):
    normed, inverse = normalize(g_ref[...].astype(F32))
    grad = old_ref[...] + ln_back(sum_parts(parts_ref), normed, inverse)
    cells = direct_ref.shape[1]
    direct_ref[...] = dot(grad.astype(BF), packed_ref[:, cells : 2 * cells])
    share((vector_ref[2:3] * grad).astype(BF), all_ref)


def head_kernel(layer, pick_ref, g_ref, out_own, out_sib, own, sib, back_out, score_ref, weight_ref, back_ref, use_ref, sems):
    stream = Stream([(own, weight_ref.at[0]), (sib, weight_ref.at[1])], sems)
    use_ref[...] = jnp.zeros(use_ref.shape, F32)
    for side, outs in enumerate((out_own, out_sib)):
        for head in range(2):
            use = jnp.where(pick_ref[head] == layer, 1.0, 0.0)
            use_ref[side, head : head + 1, : outs.shape[1]] = use * outs[head : head + 1, :]
    normed, _ = normalize(g_ref[...].astype(F32))
    quantised = normed.astype(BF)
    back = None
    scores = None
    for side in range(2):
        stream.next()
        weight = weight_ref[side]
        e = dot(quantised, weight)
        sigm = 1.0 / (1.0 + jnp.exp(-e))
        active = e * sigm
        outs = use_ref[side]
        slope = sigm * (1.0 + e * (1.0 - sigm))
        part = dot_back((-(outs[0:1] + outs[1:2]) * slope).astype(BF), weight)
        back = part if back is None else back + part
        part = [jnp.sum(active * outs[head : head + 1], axis=1, keepdims=True) for head in range(2)]
        scores = part if scores is None else [old + new for old, new in zip(scores, part)]
    back_ref[...] = back.astype(BF)
    send = pltpu.make_async_copy(back_ref, back_out, sems.at[2])
    send.start()
    lane = lax.broadcasted_iota(jnp.int32, score_ref.shape, 1)
    score_ref[...] = jnp.where(lane == 0, scores[0], 0.0) + jnp.where(lane == 1, scores[1], 0.0)
    send.wait()


WHOLE = pl.BlockSpec(memory_space=pltpu.VMEM)
FAR = pl.BlockSpec(memory_space=pltpu.HBM)


def here(kernel, name, out_shape, operands, scalars=0, far=0, far_out=(), scratch=(), limit=20):
    many = isinstance(out_shape, tuple)
    near = len(operands) - scalars - far
    shapes = tuple(
        pltpu.HBM(shape.shape, shape.dtype) if index in far_out else shape
        for index, shape in enumerate(out_shape if many else (out_shape,))
    )
    operands = operands[: scalars + near] + tuple(
        pltpu.with_memory_space_constraint(operand, pltpu.HBM) for operand in operands[scalars + near :]
    )
    specs = tuple(
        FAR if index in far_out else WHOLE for index in range(len(out_shape) if many else 1)
    )
    return pl.pallas_call(
        kernel,
        name=name,
        out_shape=shapes if many else shapes[0],
        in_specs=[pl.BlockSpec(memory_space=pltpu.SMEM)] * scalars + [WHOLE] * near + [FAR] * far,
        out_specs=specs if many else specs[0],
        scratch_shapes=list(scratch),
        compiler_params=pltpu.CompilerParams(vmem_limit_bytes=limit * 2**20),
    )(*operands)


def array(shape, dtype):
    return jax.ShapeDtypeStruct(shape, dtype)


def body(
    noisy_latents,
    student_step,
    teacher_step,
    teacher_noise,
    layer_pick,
    in_proj_s,
    in_proj_t,
    out_proj,
    s_mod,
    s_w1,
    s_w2,
    t_mod,
    t_w1,
    t_w2,
    d_w1,
    d_w2,
):
    cells = in_proj_s.shape[0]
    width = in_proj_s.shape[1] * 8
    samples = student_step.shape[0]
    layers = t_w1.shape[0]
    heads = d_w2.shape[0]
    seq = noisy_latents.shape[1]
    half = seq // 2
    quarter = half // 4
    rows = s_mod.shape[0]
    hidden = s_w1.shape[1]
    columns = in_proj_s.shape[1]
    sample = lax.axis_index(SAMPLE)
    at_y = lax.axis_index("y")
    at_core = lax.axis_index("core")
    start = sample * rows

    sig_all_t = teacher_step.astype(F32) * 0.001
    sig_steps = (1 + jnp.arange(STEPS)).astype(F32) * 0.25
    cond_s = jax.nn.silu(embed_block(1000.0 * sig_steps, width, rows, start))
    cond_t = jax.nn.silu(embed_block(1000.0 * sig_all_t, width, rows, start))
    where = jnp.stack([sample, at_y, at_core]).astype(jnp.int32)
    block = sample * rows // columns
    places = [block, sample * rows // rows % (columns // rows)]
    for offset in (0, 8, 16):
        places += [(block + offset) // 3, (block + offset) % 3]
    places = jnp.stack(places).astype(jnp.int32)
    spare = -columns % 128
    head_block = jnp.pad(d_w1, ((0, 0), (0, spare)))
    picks = layer_pick[0]
    mod_part, projections = here(
        modulation_kernel,
        "modulation",
        (array((samples * 8, s_mod.shape[1]), BF), array((columns, 3 * cells), BF)),
        (
            jnp.pad(cond_s, ((0, 16 - STEPS), (0, 0))),
            cond_t,
            s_mod,
            t_mod,
            in_proj_s,
            in_proj_t,
            out_proj,
        ),
    )
    mod_part, projections, where, places, head_block, picks = lax.optimization_barrier(
        (mod_part, projections, where, places, head_block, picks)
    )
    mod_part = mod_part.reshape(samples, 8, s_mod.shape[1])
    mods = jnp.sum(lax.all_to_all(mod_part, SAMPLE, 0, 0).astype(F32), axis=0)
    kinds = layers + STEPS
    mods = mods[:kinds].reshape(kinds * 3, columns).astype(BF)
    packed = jnp.concatenate([projections, mods.T], axis=1)
    gathered = lax.all_gather(packed, TP, axis=0, tiled=False)

    gap = -hidden % 128
    both_wide = 2 * hidden + gap
    parts, part_bias = here(
        product_kernel,
        "product",
        (
            jax.ShapeDtypeStruct((cells * STEPS, both_wide), BF),
            jax.ShapeDtypeStruct((8, hidden), BF),
        ),
        (places, gathered, s_w1, s_w2.T),
        scalars=1,
        far_out=(0,),
        scratch=(pltpu.VMEM((cells * STEPS, both_wide), BF), pltpu.SemaphoreType.DMA((1,))),
    )
    piece = cells * STEPS // samples
    chunk = cells // samples
    t_w1 = jnp.swapaxes(t_w1, 1, 2)
    parts, t_w1, t_w2, d_w2 = lax.optimization_barrier((parts, t_w1, t_w2, d_w2))
    w2_sib = sibling(t_w2)
    w1_sib = sibling(t_w1)
    d_w2_sib = sibling(d_w2)
    received = lax.all_to_all(parts.reshape(samples, piece, both_wide), SAMPLE, 0, 0)

    chosen = here(
        select_kernel,
        "select",
        array((samples * 8, both_wide), BF),
        (student_step, received, part_bias),
        scalars=1,
        far_out=(0,),
        scratch=(pltpu.VMEM((samples * 8, both_wide), BF), pltpu.SemaphoreType.DMA((1,))),
    )
    mine = lax.all_to_all(chosen.reshape(samples, 8, both_wide), SAMPLE, 0, 0)
    mine = mine.reshape(samples * 8, both_wide)

    latent_in = noisy_latents[0].T
    noise = teacher_noise[0].T
    packed = gathered.reshape(width, -1)
    half_out = array((half, cells), F32)
    velocity, other = here(
        student_kernel,
        "student",
        (half_out, half_out),
        (where, latent_in, packed, mine),
        scalars=1,
        scratch=(pltpu.VMEM((seq, cells), F32),),
    )
    velocity = velocity + sibling(other)
    velocity = velocity + lax.ppermute(velocity, "y", [(0, 1), (1, 0), (2, 3), (3, 2)])
    velocity = velocity + lax.ppermute(velocity, "y", [(0, 2), (2, 0), (1, 3), (3, 1)])

    head_block, _ = lax.optimization_barrier((head_block, other))
    head_own = lax.all_gather(head_block, SAMPLE, axis=0, tiled=True)

    def both(values, axis):
        other = sibling(values)
        first = jnp.where(at_core == 0, values, other)
        second = jnp.where(at_core == 0, other, values)
        return jnp.concatenate([first, second], axis=axis)

    gathered, _ = lax.optimization_barrier((gathered, other))
    first_own, vectors = here(
        first_product_kernel,
        "first_product",
        (array((cells + 8, hidden), F32), array((8, width), F32)),
        (gathered, t_w1),
        far=1,
        scratch=(
            pltpu.VMEM((1, hidden, width), BF),
            pltpu.VMEM((width, cells + 8), BF),
            pltpu.SemaphoreType.DMA((1,)),
        ),
        limit=44,
    )
    first_sib = sibling(first_own)
    velocity, w1_sib, w2_sib, d_w2_sib = lax.optimization_barrier((velocity, w1_sib, w2_sib, d_w2_sib))

    token_rows = pltpu.VMEM((half, width), BF)
    inner = pltpu.VMEM((2, half, hidden), BF)
    matrix = pltpu.VMEM((2, hidden, width), BF)
    rows_out = array((4, quarter, width), BF)
    mine_out = array((quarter, width), BF)
    tokens_out = array((half, width), BF)
    inner_out = array((2, half, hidden), BF)
    cells_out = array((half, cells), BF)
    y_0, slope_0, latents, noised, g_0, back_0 = here(
        first_forward_kernel,
        "first_forward",
        (tokens_out, inner_out, cells_out, cells_out, tokens_out, array((half, 2 * cells), F32)),
        (
            where,
            student_step,
            teacher_step,
            velocity,
            latent_in,
            noise,
            packed,
            first_own,
            first_sib,
            t_w2,
            w2_sib,
        ),
        scalars=3,
        far=2,
        far_out=(0, 1),
        scratch=(
            matrix,
            token_rows,
            inner,
            pltpu.VMEM((2, seq, cells), F32),
            pltpu.SemaphoreType.DMA((4,)),
        ),
        limit=44,
    )

    def sums(partial):
        return swap_y(partial.reshape(4, quarter, width))

    last = (t_w1, w1_sib, t_w2, w2_sib)
    g_1_mine, g_1 = here(
        first_middle_kernel,
        "first_middle",
        (mine_out, rows_out),
        (where, sums(y_0), g_0, vectors),
        scalars=1,
    )
    g_1 = swap_y(g_1).reshape(half, width)
    y_1, slope_1 = here(
        forward_kernel,
        "forward",
        (tokens_out, inner_out),
        (g_1, vectors) + last,
        far=4,
        far_out=(0, 1),
        scratch=(matrix, matrix, token_rows, inner, pltpu.SemaphoreType.DMA((6,))),
        limit=44,
    )
    g_2_mine, g_2 = here(
        last_middle_kernel, "last_middle", (mine_out, rows_out), (sums(y_1), g_1_mine, vectors)
    )
    head_own, _ = lax.optimization_barrier((head_own, g_2_mine))
    head_sib = sibling(head_own)
    g_2 = swap_y(g_2).reshape(half, width)

    def head(name, layer, g):
        return here(
            functools.partial(head_kernel, layer),
            name,
            (tokens_out, array((half, 128), F32)),
            (picks, g, d_w2, d_w2_sib, head_own, head_sib),
            scalars=1,
            far=2,
            far_out=(0,),
            scratch=(
                pltpu.VMEM((2,) + head_own.shape, BF),
                token_rows,
                pltpu.VMEM((2, 8, head_own.shape[1]), F32),
                pltpu.SemaphoreType.DMA((3,)),
            ),
        )

    head_back_2, scores_2 = head("head_last", 1, g_2)

    dg_2, dy_1 = here(
        last_back_kernel,
        "last_back",
        (array((quarter, width), F32), rows_out),
        (sums(head_back_2), g_2_mine, vectors),
    )
    g_1, latents, _ = lax.optimization_barrier((g_1, latents, dg_2))
    latents = both(latents, 0)
    head_back_1, scores_1 = head("head_first", 0, g_1)
    du_1 = here(
        backward_kernel,
        "backward",
        tokens_out,
        (swap_y(dy_1).reshape(half, width), vectors, slope_1, head_back_1) + last,
        far=6,
        far_out=(0,),
        scratch=(matrix, matrix, inner, token_rows, token_rows, pltpu.SemaphoreType.DMA((7,))),
        limit=44,
    )
    direct, dy_0 = here(
        first_back_kernel,
        "first_back",
        (array((quarter, cells), F32), rows_out),
        (sums(du_1), g_1_mine, dg_2, vectors, packed),
    )
    final = here(
        first_backward_kernel,
        "first_backward",
        array((cells + 8, half), F32),
        (
            where,
            teacher_step,
            swap_y(dy_0).reshape(half, width),
            noised,
            back_0,
            scores_1,
            scores_2,
            direct,
            first_own,
            first_sib,
            slope_0,
            t_w2,
            w2_sib,
        ),
        scalars=2,
        far=3,
        scratch=(matrix, inner, pltpu.VMEM((half, 2 * cells), F32), pltpu.SemaphoreType.DMA((3,))),
        limit=44,
    )
    final = final + lax.ppermute(final, "y", [(0, 1), (1, 0), (2, 3), (3, 2)])
    final = final + lax.ppermute(final, "y", [(0, 2), (2, 0), (1, 3), (3, 1)])
    final = both(final, 1)
    return (latents[None], final[cells : cells + heads][None], final[:cells].T[None])


def solution(mesh):
    names = list(mesh.axis_names)
    shape = list(mesh.devices.shape)
    at = names.index("tp")
    names[at : at + 1] = ["y", "core"]
    shape[at : at + 1] = [4, 2]
    fine = Mesh(mesh.devices.reshape(shape), tuple(names))
    placed = (
        P(SAMPLE, None, None),
        P(),
        P(),
        P(SAMPLE, None, None),
        P(SAMPLE, None),
        P(None, TP),
        P(None, TP),
        P(None, TP),
        P(SAMPLE, TP),
        P(SAMPLE, TP),
        P(TP, SAMPLE),
        P(None, SAMPLE, TP),
        P(None, None, TP),
        P(None, TP, None),
        P(SAMPLE, TP),
        P(None, TP),
    )
    return jax.shard_map(
        body,
        mesh=fine,
        in_specs=placed,
        out_specs=(P(SAMPLE, None, None), P(SAMPLE, None, None), P(SAMPLE, None, None)),
        check_vma=False,
    )
```

```python
import functools
import math

import jax
import jax.numpy as jnp
from jax import lax
from jax.experimental import pallas as pl
from jax.experimental.pallas import tpu as pltpu
from jax.sharding import Mesh
from jax.sharding import PartitionSpec as P

HIGH = lax.Precision.HIGHEST
SAMPLE = ("fsdp", "grp")
TP = ("y", "core")
STEPS = 4
LAYERS = 2
BF = jnp.bfloat16
F32 = jnp.float32


def embed_block(times, width, block, start):
    half = width // 2
    column = start + jnp.arange(block)
    steps = jnp.where(column < half, column, column - half).astype(F32)
    freq = jnp.exp(-math.log(10000.0) * steps / half)
    angle = times[:, None] * freq[None, :]
    return jnp.where((column < half)[None, :], jnp.cos(angle), jnp.sin(angle))


def normalize(values):
    mean = jnp.mean(values, axis=-1, keepdims=True)
    centered = values - mean
    inverse = lax.rsqrt(jnp.mean(centered * centered, axis=-1, keepdims=True) + 1e-06)
    return (centered * inverse, inverse)


def ln_back(grad, normed, inverse):
    mean_grad = jnp.mean(grad, axis=-1, keepdims=True)
    mean_cross = jnp.mean(grad * normed, axis=-1, keepdims=True)
    return inverse * (grad - mean_grad - normed * mean_cross)


def gelu_both(values):
    inner = 0.7978845608 * (values + 0.044715 * values * values * values)
    tangent = jnp.tanh(inner)
    halved = 0.5 * (1.0 + tangent)
    slope = halved + 0.5 * values * (1.0 - tangent * tangent) * 0.7978845608 * (
        1.0 + 3.0 * 0.044715 * values * values
    )
    return values * halved, slope


def dot(left, right):
    return jnp.dot(left, right, preferred_element_type=F32)


def dot_back(left, right):
    return lax.dot_general(left, right, (((1,), (1,)), ((), ())), preferred_element_type=F32)


def dot_across(left, right):
    return lax.dot_general(left, right, (((0,), (0,)), ((), ())), preferred_element_type=F32)


def split(values):
    high = values.astype(BF)
    return high, (values - high.astype(F32)).astype(BF)


def sibling(values):
    return lax.ppermute(values, "core", [(0, 1), (1, 0)])


def swap_y(values):
    return lax.all_to_all(values, "y", 0, 0)


class Stream:
    def __init__(self, plan, sems):
        self.copies = [
            pltpu.make_async_copy(source, target, sems.at[index])
            for index, (source, target) in enumerate(plan)
        ]
        for copy in self.copies:
            copy.start()
        self.at = 0

    def next(self):
        self.copies[self.at].wait()
        self.at += 1


def matrices(layer, sources, target):
    return [(source.at[layer], target.at[side]) for side, source in enumerate(sources)]


def identity(extent):
    row = lax.broadcasted_iota(jnp.int32, (extent, extent), 0)
    col = lax.broadcasted_iota(jnp.int32, (extent, extent), 1)
    return (row == col).astype(BF)


def turned(values):
    return dot_back(identity(values.shape[1]), values)


def turned_wide(values):
    return dot_across(values, identity(values.shape[0]))


def product_kernel(at_ref, packed_ref, w1_ref, w2_ref, out, bias_ref, out_ref, sems):
    blocks, columns, _ = packed_ref.shape
    rows, hidden = w1_ref.shape
    cells = out_ref.shape[0] // STEPS
    pick_row = lax.broadcasted_iota(jnp.int32, (rows, columns), 0)
    pick_col = lax.broadcasted_iota(jnp.int32, (rows, columns), 1)
    mine = (pick_col == pick_row + rows * at_ref[1]).astype(BF)
    total = jnp.zeros((columns, cells), F32)
    for block in range(blocks):
        total = total + packed_ref[block, :, :cells].astype(F32)
    mean = jnp.sum(total, axis=0, keepdims=True) / (blocks * columns)
    local = dot(mine, packed_ref[at_ref[0]])
    high, low = split(local[:, :cells] - mean)
    out_rows = local[:, 2 * cells : 3 * cells].astype(BF)

    def modulation(index):
        block = dot(mine, packed_ref[at_ref[2 * index + 2]]).astype(BF)[:, 3 * cells :]
        row = lax.broadcasted_iota(jnp.int32, (block.shape[1], 8), 0)
        kind = lax.broadcasted_iota(jnp.int32, (block.shape[1], 8), 1)
        want = (row == 3 * (kind + LAYERS) + at_ref[2 * index + 3]) & (kind < STEPS)
        return dot(block, want.astype(BF)).astype(BF)

    shift, scale, gate = modulation(0), modulation(1), modulation(2)
    cell_row = lax.broadcasted_iota(jnp.int32, (cells, cells * STEPS), 0)
    cell_col = lax.broadcasted_iota(jnp.int32, (cells, cells * STEPS), 1)
    by_cell = (cell_col // STEPS == cell_row).astype(BF)
    step_row = lax.broadcasted_iota(jnp.int32, (8, cells * STEPS), 0)
    step_col = lax.broadcasted_iota(jnp.int32, (8, cells * STEPS), 1)
    by_step = (step_col % STEPS == step_row).astype(BF)
    left_in = (dot(high, by_cell) + dot(low, by_cell)) * (1.0 + dot(scale, by_step))
    left_out = dot(out_rows, by_cell) * dot(gate, by_step)
    gap = -hidden % 128
    out_ref[:, :hidden] = dot_across(left_in.astype(BF), w1_ref[...]).astype(BF)
    out_ref[:, hidden : hidden + gap] = jnp.zeros((cells * STEPS, gap), BF)
    out_ref[:, hidden + gap : 2 * hidden + gap] = dot_across(left_out.astype(BF), w2_ref[...]).astype(BF)
    out_ref[:, 2 * hidden + gap :] = jnp.zeros((cells * STEPS, gap), BF)
    send = pltpu.make_async_copy(out_ref, out, sems.at[0])
    send.start()
    bias_ref[...] = dot_across(shift, w1_ref[...]).astype(BF)
    send.wait()


def select_kernel(step_ref, parts_ref, bias_ref, out, out_ref, sems):
    samples, piece, _ = parts_ref.shape
    hidden = bias_ref.shape[1]
    chunk = piece // STEPS

    def at_step(extent):
        row = lax.broadcasted_iota(jnp.int32, (samples * 8, extent), 0)
        step = jnp.zeros((samples * 8, extent), jnp.int32)
        for sample in range(samples):
            step = jnp.where(row // 8 == sample, step_ref[sample] - 1, step)
        return row % 8, lax.broadcasted_iota(jnp.int32, (samples * 8, extent), 1), step

    total = parts_ref[0].astype(F32)
    for source in range(1, samples):
        total = total + parts_ref[source].astype(F32)
    place, col, step = at_step(piece)
    pick = ((col == place * STEPS + step) & (place < chunk)).astype(BF)
    chosen = dot(pick, total.astype(BF))
    out_ref[...] = chosen.astype(BF)
    place, col, step = at_step(8)
    pick = ((col == step) & (place == chunk)).astype(BF)
    out_ref[:, :hidden] = (chosen[:, :hidden] + dot(pick, bias_ref[...])).astype(BF)
    send = pltpu.make_async_copy(out_ref, out, sems.at[0])
    send.start()
    send.wait()


def student_kernel(hidden, where_ref, x_ref, packed_ref, mat_ref, mine_ref, other_ref, all_ref):
    cells, seq = x_ref.shape
    width = packed_ref.shape[0]
    lanes, wide = mat_ref.shape
    second_at = wide // 2
    group = lanes * 4 // cells
    x = turned_wide(x_ref[...]).astype(BF)
    proj = packed_ref[:, :cells]
    centered = proj.astype(F32)
    centered = centered - jnp.mean(centered, axis=0, keepdims=True)
    high, low = split(centered)
    gram = dot_across(high, high) + (dot_across(high, low) + dot_across(low, high))
    direct = dot_across(proj, packed_ref[:, 2 * cells : 3 * cells])

    def times(matrix):
        first, second = split(matrix)
        return dot(x, first) + dot(x, second)

    var = jnp.sum(times(gram) * x.astype(F32), axis=1, keepdims=True) / width
    inverse = lax.rsqrt(jnp.maximum(var, 0.0) + 1e-06)
    row = lax.broadcasted_iota(jnp.int32, (cells, lanes), 0)
    col = lax.broadcasted_iota(jnp.int32, (cells, lanes), 1)
    spread = (col == group * (row // 4) + row % 4).astype(BF)
    bias_col = lax.broadcasted_iota(jnp.int32, (8, lanes), 1)
    bias = dot((bias_col % group == 4).astype(BF), mat_ref[:, :hidden])[:1]
    z = inverse * dot(dot(x, spread).astype(BF), mat_ref[:, :hidden]) + bias
    active = gelu_both(z)[0].astype(BF)
    high, low = split(dot_back(active, mat_ref[:, second_at : second_at + hidden]))
    all_ref[...] = dot_back(high, spread) + dot_back(low, spread) + 0.125 * times(direct)
    half = seq // 2
    core = where_ref[2]
    mine_ref[...] = all_ref[pl.ds(pl.multiple_of(core * half, half), half), :]
    other_ref[...] = all_ref[pl.ds(pl.multiple_of((1 - core) * half, half), half), :]


def first_product_kernel(packed_ref, up, out_ref, vector_ref, up_ref, left_ref, sems):
    blocks, columns, _ = packed_ref.shape
    cells = out_ref.shape[0] - 8
    stream = Stream(matrices(0, (up,), up_ref), sems)
    total = jnp.zeros((columns, cells), F32)
    for block in range(blocks):
        total = total + packed_ref[block, :, cells : 2 * cells].astype(F32)
    mean = jnp.sum(total, axis=0, keepdims=True) / (blocks * columns)

    def vector(kind, block):
        at = kind * blocks + block
        return packed_ref[at // 3, :, 3 * cells + at % 3 : 3 * cells + at % 3 + 1].astype(F32)

    for block in range(blocks):
        centered = packed_ref[block, :, cells : 2 * cells].astype(F32) - mean
        scaled = centered * (1.0 + vector(1, block))
        shift = jnp.broadcast_to(vector(0, block), (columns, 8))
        left_ref[block * columns : (block + 1) * columns, :] = jnp.concatenate(
            [scaled, shift], axis=1
        ).astype(BF)
    for source in range(blocks):
        rows = turned(packed_ref[source, :, 3 * cells : 3 * cells + 3 * LAYERS])
        for third in range(3):
            kind, block = divmod(source * 3 + third, blocks)
            for layer in range(LAYERS):
                vector_ref[
                    3 * layer + kind : 3 * layer + kind + 1, block * columns : (block + 1) * columns
                ] = rows[3 * layer + third : 3 * layer + third + 1]
    left = turned(left_ref[...]).astype(BF)
    stream.next()
    out_ref[...] = dot_back(left, up_ref[0])


def first_forward_kernel(
    where_ref, student_ref, teacher_ref, velocity_ref, x_ref, noise_ref, packed_ref, mat_own, mat_sib, own, sib,
    y_out, slope_out, latents_ref, noised_ref, g_ref, back_ref,
    w_ref, y_ref, slope_ref, both_ref, sems
):
    cells, seq = x_ref.shape
    half = seq // 2
    stream = Stream(matrices(0, (own, sib), w_ref), sems)
    sample = where_ref[0]
    sigma_s = student_ref[sample].astype(F32) * 0.25
    sigma_t = teacher_ref[sample].astype(F32) * 0.001
    both_ref[0] = turned_wide(x_ref[...])
    both_ref[1] = turned_wide(noise_ref[...])
    mine = pl.ds(pl.multiple_of(where_ref[2] * half, half), half)
    latents = (both_ref[0, mine, :] - sigma_s * sum_parts(velocity_ref)).astype(BF)
    latents_ref[...] = latents
    x = ((1.0 - sigma_t) * latents.astype(F32) + sigma_t * both_ref[1, mine, :]).astype(BF)
    noised_ref[...] = x
    proj = packed_ref[:, cells : 2 * cells]
    g_0 = dot_back(x, proj).astype(BF)
    g_ref[...] = g_0
    normed, inverse = normalize(g_0.astype(F32))
    back_ref[:, :cells] = dot(normed.astype(BF), proj)
    back_ref[:, cells:] = jnp.broadcast_to(inverse, (half, cells))
    twice = jnp.concatenate([x, x], axis=1)
    actives = []
    for side, mat_ref in enumerate((mat_own, mat_sib)):
        high, low = split(mat_ref[:cells])
        z = inverse * dot(twice, jnp.concatenate([high, low], axis=0)) + mat_ref[cells : cells + 1]
        active, slope = gelu_both(z)
        slope_ref[side] = slope.astype(BF)
        actives.append(active.astype(BF))
    keep = pltpu.make_async_copy(slope_ref, slope_out, sems.at[2])
    keep.start()
    stream.next()
    y = dot(actives[0], w_ref[0])
    stream.next()
    y_ref[...] = (y + dot(actives[1], w_ref[1])).astype(BF)
    send = pltpu.make_async_copy(y_ref, y_out, sems.at[3])
    send.start()
    keep.wait()
    send.wait()


def forward_kernel(
    g_ref, vector_ref, up_own, up_sib, down_own, down_sib, y_out, slope_out,
    up_ref, down_ref, y_ref, slope_ref, sems
):
    stream = Stream(
        matrices(1, (up_own, up_sib), up_ref) + matrices(1, (down_own, down_sib), down_ref), sems
    )
    normed, _ = normalize(g_ref[...].astype(F32))
    u = (normed * (1.0 + vector_ref[4:5]) + vector_ref[3:4]).astype(BF)
    actives = []
    for side in range(2):
        stream.next()
        active, slope = gelu_both(dot_back(u, up_ref[side]))
        slope_ref[side] = slope.astype(BF)
        actives.append(active.astype(BF))
    keep = pltpu.make_async_copy(slope_ref, slope_out, sems.at[4])
    keep.start()
    stream.next()
    y = dot(actives[0], down_ref[0])
    stream.next()
    y_ref[...] = (y + dot(actives[1], down_ref[1])).astype(BF)
    send = pltpu.make_async_copy(y_ref, y_out, sems.at[5])
    send.start()
    keep.wait()
    send.wait()


def backward_kernel(
    dy_ref, vector_ref, slope, head, up_own, up_sib, down_own, down_sib, out,
    up_ref, down_ref, slope_ref, head_ref, out_ref, sems
):
    stream = Stream(
        [(slope, slope_ref)]
        + matrices(1, (down_own, down_sib), down_ref)
        + matrices(1, (up_own, up_sib), up_ref)
        + [(head, head_ref)],
        sems,
    )
    dy = dy_ref[...]
    stream.next()
    dz = []
    for side in range(2):
        stream.next()
        dz.append((dot_back(dy, down_ref[side]) * slope_ref[side].astype(F32)).astype(BF))
    stream.next()
    du = dot(dz[0], up_ref[0])
    stream.next()
    du = du + dot(dz[1], up_ref[1])
    stream.next()
    out_ref[...] = (du * (1.0 + vector_ref[4:5]) + head_ref[...].astype(F32)).astype(BF)
    send = pltpu.make_async_copy(out_ref, out, sems.at[6])
    send.start()
    send.wait()


def first_backward_kernel(
    where_ref, teacher_ref, dy_ref, x_ref, back_ref, score_1, score_2, direct_ref, mat_own, mat_sib, slope, own, sib,
    out_ref, w_ref, slope_ref, all_ref, sems
):
    cells = x_ref.shape[1]
    stream = Stream([(slope, slope_ref)] + matrices(0, (own, sib), w_ref), sems)
    dy = dy_ref[...]
    stream.next()
    total = None
    for side, mat_ref in enumerate((mat_own, mat_sib)):
        high, low = split(mat_ref[:cells])
        stream.next()
        dz = (dot_back(dy, w_ref[side]) * slope_ref[side].astype(F32)).astype(BF)
        part = dot_back(dz, high) + dot_back(dz, low)
        total = part if total is None else total + part
    inverse = back_ref[:, cells : cells + 1]
    cross = inverse * jnp.sum(x_ref[...].astype(F32) * total, axis=1, keepdims=True) / dy.shape[1]
    rest = 1.0 - teacher_ref[where_ref[0]].astype(F32) * 0.001
    all_ref[:, :cells] = rest * (inverse * (total - back_ref[:, :cells] * cross))
    all_ref[:, cells:] = score_1[:, :cells] + score_2[:, :cells]
    rows = direct_ref.shape[0]
    mine = pl.ds(pl.multiple_of(where_ref[1] * rows, rows), rows)
    all_ref[mine, :cells] += rest * direct_ref[...]
    final = all_ref[...].T[: out_ref.shape[1]]
    for target in range(out_ref.shape[0]):
        out_ref[target] = final


def modulation_kernel(
    cond_s_ref, cond_t_ref, s_mod, t_mod, in_s, in_t, out_proj, head, out, proj_ref, head_out,
    s_ref, t_ref, stack_ref, head_ref, out_ref, head_all, sems
):
    samples = cond_t_ref.shape[0]
    cells = in_s.shape[0]
    hidden = s_mod.shape[1]
    stream = Stream(
        [(head, head_ref), (s_mod, s_ref), (t_mod, t_ref)]
        + [
            (source, stack_ref.at[pl.ds(index * cells, cells)])
            for index, source in enumerate((in_s, in_t, out_proj))
        ],
        sems,
    )
    stream.next()
    head_all[:, : head_ref.shape[1]] = head_ref[...]
    head_all[:, head_ref.shape[1] :] = jnp.zeros(
        (head_ref.shape[0], head_all.shape[1] - head_ref.shape[1]), BF
    )
    keep = pltpu.make_async_copy(head_all, head_out, sems.at[6])
    keep.start()
    stream.next()

    def product(cond, weight):
        extent = cond.shape[0]
        high, rest = split(cond)
        rest = cond - high.astype(F32)
        middle, low = split(rest)
        parts = dot(jnp.concatenate([high, middle, low], axis=0), weight)
        return (parts[:extent] + (parts[extent : 2 * extent] + parts[2 * extent :])).astype(BF)

    def place(extent, first, every):
        row = lax.broadcasted_iota(jnp.int32, (samples * 8, extent), 0)
        col = lax.broadcasted_iota(jnp.int32, (samples * 8, extent), 1)
        if every:
            return (row % 8 == first + col).astype(BF)
        return ((row // 8 == col) & (row % 8 == first)).astype(BF)

    total = dot(place(16, LAYERS, True), product(cond_s_ref[...], s_ref[...]))
    stream.next()
    for layer in range(LAYERS):
        part = product(cond_t_ref[...], t_ref[layer])
        total = total + dot(place(samples, layer, False), part)
    out_ref[:, :hidden] = total.astype(BF)
    out_ref[:, hidden:] = jnp.zeros((samples * 8, out_ref.shape[1] - hidden), BF)
    send = pltpu.make_async_copy(out_ref, out, sems.at[7])
    send.start()
    for _ in range(3):
        stream.next()
    proj_ref[...] = turned_wide(stack_ref[...]).astype(BF)
    keep.wait()
    send.wait()


def sum_parts(parts_ref):
    total = parts_ref[0].astype(F32)
    for source in range(1, parts_ref.shape[0]):
        total = total + parts_ref[source].astype(F32)
    return total


def share(values_ref, everyone, sems):
    copies = [
        pltpu.make_async_copy(values_ref, everyone.at[target], sems.at[target])
        for target in range(everyone.shape[0])
    ]
    for copy in copies:
        copy.start()
    for copy in copies:
        copy.wait()


def first_middle_kernel(where_ref, parts_ref, g_ref, vector_ref, mine_ref, everyone, sems):
    rows = mine_ref.shape[0]
    before = g_ref[pl.ds(pl.multiple_of(where_ref[1] * rows, rows), rows), :].astype(F32)
    after = (before + vector_ref[2:3] * sum_parts(parts_ref)).astype(BF)
    mine_ref[...] = after
    share(mine_ref, everyone, sems)


def last_middle_kernel(parts_ref, g_ref, vector_ref, mine_ref, everyone, sems):
    after = (g_ref[...].astype(F32) + vector_ref[5:6] * sum_parts(parts_ref)).astype(BF)
    mine_ref[...] = after
    share(mine_ref, everyone, sems)


def last_back_kernel(parts_ref, g_ref, vector_ref, grad_ref, everyone, share_ref, sems):
    normed, inverse = normalize(g_ref[...].astype(F32))
    grad = ln_back(sum_parts(parts_ref), normed, inverse)
    grad_ref[...] = grad
    share_ref[...] = (vector_ref[5:6] * grad).astype(BF)
    share(share_ref, everyone, sems)


def first_back_kernel(parts_ref, g_ref, old_ref, vector_ref, packed_ref, direct_ref, everyone, share_ref, sems):
    normed, inverse = normalize(g_ref[...].astype(F32))
    grad = old_ref[...] + ln_back(sum_parts(parts_ref), normed, inverse)
    cells = direct_ref.shape[1]
    direct_ref[...] = dot(grad.astype(BF), packed_ref[:, cells : 2 * cells])
    share_ref[...] = (vector_ref[2:3] * grad).astype(BF)
    share(share_ref, everyone, sems)


def block_owner(fsdp, block):
    x_hi, z = fsdp // 4, fsdp % 4
    return (x_hi ^ (block & 1)) * 4 + (z ^ ((block >> 1 & 1) ^ (block >> 2 & 1) * 3))


def swap_fsdp(values, pattern):
    other = lax.ppermute(values, "fsdp", [(at, at ^ pattern) for at in range(8)])
    return jnp.concatenate([values, other], axis=0)


def head_kernel(layer, pick_ref, where_ref, g_ref, out_own, out_sib, own, sib, back_out, score_ref, weight_ref, back_ref, use_ref, sems):
    blocks = 8
    size = own.shape[0] // blocks
    plan = []
    for side, source in enumerate((own, sib)):
        for block in range(blocks):
            row = pl.multiple_of(block_owner(where_ref[3], block) * size, size)
            plan.append(
                (source.at[pl.ds(block * size, size)], weight_ref.at[side, pl.ds(row, size)])
            )
    stream = Stream(plan, sems)
    use_ref[...] = jnp.zeros(use_ref.shape, F32)
    for side, outs in enumerate((out_own, out_sib)):
        for head in range(2):
            use = jnp.where(pick_ref[head] == layer, 1.0, 0.0)
            use_ref[side, head : head + 1, : outs.shape[1]] = use * outs[head : head + 1, :]
    normed, _ = normalize(g_ref[...].astype(F32))
    quantised = normed.astype(BF)
    back = None
    scores = None
    for side in range(2):
        for _ in range(blocks):
            stream.next()
        weight = weight_ref[side]
        e = dot(quantised, weight)
        sigm = 1.0 / (1.0 + jnp.exp(-e))
        active = e * sigm
        outs = use_ref[side]
        slope = sigm * (1.0 + e * (1.0 - sigm))
        part = dot_back((-(outs[0:1] + outs[1:2]) * slope).astype(BF), weight)
        back = part if back is None else back + part
        part = [jnp.sum(active * outs[head : head + 1], axis=1, keepdims=True) for head in range(2)]
        scores = part if scores is None else [old + new for old, new in zip(scores, part)]
    back_ref[...] = back.astype(BF)
    send = pltpu.make_async_copy(back_ref, back_out, sems.at[2 * blocks])
    send.start()
    lane = lax.broadcasted_iota(jnp.int32, score_ref.shape, 1)
    score_ref[...] = jnp.where(lane == 0, scores[0], 0.0) + jnp.where(lane == 1, scores[1], 0.0)
    send.wait()


WHOLE = pl.BlockSpec(memory_space=pltpu.VMEM)
FAR = pl.BlockSpec(memory_space=pltpu.HBM)


def here(kernel, name, out_shape, operands, scalars=0, far=0, far_out=(), scratch=(), limit=20):
    many = isinstance(out_shape, tuple)
    near = len(operands) - scalars - far
    shapes = tuple(
        pltpu.HBM(shape.shape, shape.dtype) if index in far_out else shape
        for index, shape in enumerate(out_shape if many else (out_shape,))
    )
    operands = operands[: scalars + near] + tuple(
        pltpu.with_memory_space_constraint(operand, pltpu.HBM) for operand in operands[scalars + near :]
    )
    specs = tuple(
        FAR if index in far_out else WHOLE for index in range(len(out_shape) if many else 1)
    )
    return pl.pallas_call(
        kernel,
        name=name,
        out_shape=shapes if many else shapes[0],
        in_specs=[pl.BlockSpec(memory_space=pltpu.SMEM)] * scalars + [WHOLE] * near + [FAR] * far,
        out_specs=specs if many else specs[0],
        scratch_shapes=list(scratch),
        compiler_params=pltpu.CompilerParams(vmem_limit_bytes=limit * 2**20),
    )(*operands)


def array(shape, dtype):
    return jax.ShapeDtypeStruct(shape, dtype)


def body(
    noisy_latents,
    student_step,
    teacher_step,
    teacher_noise,
    layer_pick,
    in_proj_s,
    in_proj_t,
    out_proj,
    s_mod,
    s_w1,
    s_w2,
    t_mod,
    t_w1,
    t_w2,
    d_w1,
    d_w2,
):
    cells = in_proj_s.shape[0]
    width = in_proj_s.shape[1] * 8
    samples = student_step.shape[0]
    layers = t_w1.shape[0]
    heads = d_w2.shape[0]
    seq = noisy_latents.shape[1]
    half = seq // 2
    quarter = half // 4
    rows = s_mod.shape[0]
    hidden = s_w1.shape[1]
    columns = in_proj_s.shape[1]
    sample = lax.axis_index(SAMPLE)
    at_y = lax.axis_index("y")
    at_core = lax.axis_index("core")
    start = sample * rows

    sig_all_t = teacher_step.astype(F32) * 0.001
    sig_steps = (1 + jnp.arange(STEPS)).astype(F32) * 0.25
    cond_s = jax.nn.silu(embed_block(1000.0 * sig_steps, width, rows, start))
    cond_t = jax.nn.silu(embed_block(1000.0 * sig_all_t, width, rows, start))
    at_grp = lax.axis_index("grp")
    where = jnp.stack([sample, at_y, at_core, lax.axis_index("fsdp")]).astype(jnp.int32)
    block = sample * rows // columns
    places = [block, sample * rows // rows % (columns // rows)]
    for offset in (0, 8, 16):
        places += [(block + offset) // 3, (block + offset) % 3]
    places = jnp.stack(places).astype(jnp.int32)
    head_wide = columns + -columns % 128
    mod_wide = s_mod.shape[1] + -s_mod.shape[1] % 128
    picks = layer_pick[0]
    mod_part, projections, head_block = here(
        modulation_kernel,
        "modulation",
        (
            array((samples * 8, mod_wide), BF),
            array((columns, 3 * cells), BF),
            array((rows, head_wide), BF),
        ),
        (
            jnp.pad(cond_s, ((0, 16 - STEPS), (0, 0))),
            cond_t,
            s_mod,
            t_mod,
            in_proj_s,
            in_proj_t,
            out_proj,
            d_w1,
        ),
        far=6,
        far_out=(0, 2),
        scratch=(
            pltpu.VMEM(s_mod.shape, BF),
            pltpu.VMEM(t_mod.shape, BF),
            pltpu.VMEM((3 * cells, columns), BF),
            pltpu.VMEM(d_w1.shape, BF),
            pltpu.VMEM((samples * 8, mod_wide), BF),
            pltpu.VMEM((rows, head_wide), BF),
            pltpu.SemaphoreType.DMA((8,)),
        ),
    )
    mod_part, projections, where, places, head_block, picks = lax.optimization_barrier(
        (mod_part, projections, where, places, head_block, picks)
    )
    mod_part = mod_part.reshape(samples, 8, mod_wide)
    mods = jnp.sum(lax.all_to_all(mod_part, SAMPLE, 0, 0).astype(F32), axis=0)
    kinds = layers + STEPS
    mods = mods[:kinds, : 3 * columns].reshape(kinds * 3, columns).astype(BF)
    packed = jnp.concatenate([projections, mods.T], axis=1)
    gathered = lax.all_gather(packed, TP, axis=0, tiled=False)

    gap = -hidden % 128
    both_wide = 2 * (hidden + gap)
    parts, part_bias = here(
        product_kernel,
        "product",
        (
            jax.ShapeDtypeStruct((cells * STEPS, both_wide), BF),
            jax.ShapeDtypeStruct((8, hidden), BF),
        ),
        (places, gathered, s_w1, s_w2.T),
        scalars=1,
        far_out=(0,),
        scratch=(pltpu.VMEM((cells * STEPS, both_wide), BF), pltpu.SemaphoreType.DMA((1,))),
    )
    piece = cells * STEPS // samples
    chunk = cells // samples
    t_w1 = jnp.swapaxes(t_w1, 1, 2)
    parts, gathered, t_w1, t_w2, d_w2 = lax.optimization_barrier((parts, gathered, t_w1, t_w2, d_w2))
    w2_sib = sibling(t_w2)
    w1_sib = sibling(t_w1)
    d_w2_sib = sibling(d_w2)
    received = lax.all_to_all(parts.reshape(samples, piece, both_wide), SAMPLE, 0, 0)

    first_own, vectors = here(
        first_product_kernel,
        "first_product",
        (array((cells + 8, hidden), F32), array((8, width), F32)),
        (gathered, t_w1),
        far=1,
        scratch=(
            pltpu.VMEM((1, hidden, width), BF),
            pltpu.VMEM((width, cells + 8), BF),
            pltpu.SemaphoreType.DMA((1,)),
        ),
        limit=44,
    )
    received, first_own, vectors = lax.optimization_barrier((received, first_own, vectors))

    chosen = here(
        select_kernel,
        "select",
        array((samples * 8, both_wide), BF),
        (student_step, received, part_bias),
        scalars=1,
        far_out=(0,),
        scratch=(pltpu.VMEM((samples * 8, both_wide), BF), pltpu.SemaphoreType.DMA((1,))),
    )
    mine = lax.all_to_all(chosen.reshape(samples, 8, both_wide), SAMPLE, 0, 0)
    mine = mine.reshape(samples * 8, both_wide)

    latent_in = noisy_latents[0].T
    noise = teacher_noise[0].T
    packed = gathered.reshape(width, -1)
    half_out = array((half, cells), F32)
    velocity, other = here(
        functools.partial(student_kernel, hidden),
        "student",
        (half_out, half_out),
        (where, latent_in, packed, mine),
        scalars=1,
        scratch=(pltpu.VMEM((seq, cells), F32),),
    )
    velocity = velocity + sibling(other)
    head_block, _ = lax.optimization_barrier((head_block, mine))
    head_other = lax.ppermute(head_block, "grp", [(0, 1), (1, 0)])
    head_other, _ = lax.optimization_barrier((head_other, velocity))
    head_pair = jnp.concatenate(
        [
            jnp.where(at_grp == 0, head_block, head_other),
            jnp.where(at_grp == 0, head_other, head_block),
        ],
        axis=0,
    )
    head_two = swap_fsdp(head_pair, 4)
    velocity = swap_y(jnp.broadcast_to(velocity[None], (4,) + velocity.shape))

    def both(values, axis):
        other = sibling(values)
        first = jnp.where(at_core == 0, values, other)
        second = jnp.where(at_core == 0, other, values)
        return jnp.concatenate([first, second], axis=axis)

    first_sib = sibling(first_own)
    velocity, w1_sib, w2_sib, d_w2_sib = lax.optimization_barrier((velocity, w1_sib, w2_sib, d_w2_sib))

    token_rows = pltpu.VMEM((half, width), BF)
    inner = pltpu.VMEM((2, half, hidden), BF)
    matrix = pltpu.VMEM((2, hidden, width), BF)
    rows_out = array((4, quarter, width), BF)
    mine_out = array((quarter, width), BF)
    tokens_out = array((half, width), BF)
    inner_out = array((2, half, hidden), BF)
    cells_out = array((half, cells), BF)
    y_0, slope_0, latents, noised, g_0, back_0 = here(
        first_forward_kernel,
        "first_forward",
        (tokens_out, inner_out, cells_out, cells_out, tokens_out, array((half, 2 * cells), F32)),
        (
            where,
            student_step,
            teacher_step,
            velocity,
            latent_in,
            noise,
            packed,
            first_own,
            first_sib,
            t_w2,
            w2_sib,
        ),
        scalars=3,
        far=2,
        far_out=(0, 1),
        scratch=(
            matrix,
            token_rows,
            inner,
            pltpu.VMEM((2, seq, cells), F32),
            pltpu.SemaphoreType.DMA((4,)),
        ),
        limit=44,
    )

    def sums(partial):
        return swap_y(partial.reshape(4, quarter, width))

    last = (t_w1, w1_sib, t_w2, w2_sib)
    four = pltpu.SemaphoreType.DMA((4,))
    quarter_rows = pltpu.VMEM((quarter, width), BF)
    g_1_mine, g_1 = here(
        first_middle_kernel,
        "first_middle",
        (mine_out, rows_out),
        (where, sums(y_0), g_0, vectors),
        scalars=1,
        far_out=(1,),
        scratch=(four,),
    )
    head_two, _ = lax.optimization_barrier((head_two, y_0))
    head_four = swap_fsdp(head_two, 1)
    head_four, _ = lax.optimization_barrier((head_four, g_1_mine))
    head_own = swap_fsdp(head_four, 3)
    g_1 = swap_y(g_1).reshape(half, width)
    y_1, slope_1 = here(
        forward_kernel,
        "forward",
        (tokens_out, inner_out),
        (g_1, vectors) + last,
        far=4,
        far_out=(0, 1),
        scratch=(matrix, matrix, token_rows, inner, pltpu.SemaphoreType.DMA((6,))),
        limit=44,
    )
    g_2_mine, g_2 = here(
        last_middle_kernel,
        "last_middle",
        (mine_out, rows_out),
        (sums(y_1), g_1_mine, vectors),
        far_out=(1,),
        scratch=(four,),
    )
    head_own, _ = lax.optimization_barrier((head_own, g_2_mine))
    head_sib = sibling(head_own)
    g_2 = swap_y(g_2).reshape(half, width)

    def head(name, layer, g):
        return here(
            functools.partial(head_kernel, layer),
            name,
            (tokens_out, array((half, 128), F32)),
            (picks, where, g, d_w2, d_w2_sib, head_own, head_sib),
            scalars=2,
            far=2,
            far_out=(0,),
            scratch=(
                pltpu.VMEM((2,) + head_own.shape, BF),
                token_rows,
                pltpu.VMEM((2, 8, head_own.shape[1]), F32),
                pltpu.SemaphoreType.DMA((17,)),
            ),
        )

    head_back_2, scores_2 = head("head_last", 1, g_2)

    dg_2, dy_1 = here(
        last_back_kernel,
        "last_back",
        (array((quarter, width), F32), rows_out),
        (sums(head_back_2), g_2_mine, vectors),
        far_out=(1,),
        scratch=(quarter_rows, four),
    )
    g_1, latents, _ = lax.optimization_barrier((g_1, latents, dg_2))
    latents = both(latents, 0)
    head_back_1, scores_1 = head("head_first", 0, g_1)
    du_1 = here(
        backward_kernel,
        "backward",
        tokens_out,
        (swap_y(dy_1).reshape(half, width), vectors, slope_1, head_back_1) + last,
        far=6,
        far_out=(0,),
        scratch=(matrix, matrix, inner, token_rows, token_rows, pltpu.SemaphoreType.DMA((7,))),
        limit=44,
    )
    direct, dy_0 = here(
        first_back_kernel,
        "first_back",
        (array((quarter, cells), F32), rows_out),
        (sums(du_1), g_1_mine, dg_2, vectors, packed),
        far_out=(1,),
        scratch=(quarter_rows, four),
    )
    final = here(
        first_backward_kernel,
        "first_backward",
        array((4, cells + 8, half), F32),
        (
            where,
            teacher_step,
            swap_y(dy_0).reshape(half, width),
            noised,
            back_0,
            scores_1,
            scores_2,
            direct,
            first_own,
            first_sib,
            slope_0,
            t_w2,
            w2_sib,
        ),
        scalars=2,
        far=3,
        scratch=(matrix, inner, pltpu.VMEM((half, 2 * cells), F32), pltpu.SemaphoreType.DMA((3,))),
        limit=44,
    )
    final = both(jnp.sum(swap_y(final), axis=0), 1)
    return (latents[None], final[cells : cells + heads][None], final[:cells].T[None])


def solution(mesh):
    names = list(mesh.axis_names)
    shape = list(mesh.devices.shape)
    at = names.index("tp")
    names[at : at + 1] = ["y", "core"]
    shape[at : at + 1] = [4, 2]
    fine = Mesh(mesh.devices.reshape(shape), tuple(names))
    placed = (
        P(SAMPLE, None, None),
        P(),
        P(),
        P(SAMPLE, None, None),
        P(SAMPLE, None),
        P(None, TP),
        P(None, TP),
        P(None, TP),
        P(SAMPLE, TP),
        P(SAMPLE, TP),
        P(TP, SAMPLE),
        P(None, SAMPLE, TP),
        P(None, None, TP),
        P(None, TP, None),
        P(SAMPLE, TP),
        P(None, TP),
    )
    return jax.shard_map(
        body,
        mesh=fine,
        in_specs=placed,
        out_specs=(P(SAMPLE, None, None), P(SAMPLE, None, None), P(SAMPLE, None, None)),
        check_vma=False,
    )
```

```python
import functools
import math

import jax
import jax.numpy as jnp
from jax import lax
from jax.experimental import pallas as pl
from jax.experimental.pallas import tpu as pltpu
from jax.sharding import Mesh
from jax.sharding import PartitionSpec as P

HIGH = lax.Precision.HIGHEST
SAMPLE = ("fsdp", "grp")
TP = ("y", "core")
STEPS = 4
LAYERS = 2
BF = jnp.bfloat16
F32 = jnp.float32


def embed_block(times, width, block, start):
    half = width // 2
    column = start + jnp.arange(block)
    steps = jnp.where(column < half, column, column - half).astype(F32)
    freq = jnp.exp(-math.log(10000.0) * steps / half)
    angle = times[:, None] * freq[None, :]
    return jnp.where((column < half)[None, :], jnp.cos(angle), jnp.sin(angle))


def normalize(values):
    mean = jnp.mean(values, axis=-1, keepdims=True)
    centered = values - mean
    inverse = lax.rsqrt(jnp.mean(centered * centered, axis=-1, keepdims=True) + 1e-06)
    return (centered * inverse, inverse)


def ln_back(grad, normed, inverse):
    mean_grad = jnp.mean(grad, axis=-1, keepdims=True)
    mean_cross = jnp.mean(grad * normed, axis=-1, keepdims=True)
    return inverse * (grad - mean_grad - normed * mean_cross)


def gelu_both(values):
    inner = 0.7978845608 * (values + 0.044715 * values * values * values)
    tangent = jnp.tanh(inner)
    halved = 0.5 * (1.0 + tangent)
    slope = halved + 0.5 * values * (1.0 - tangent * tangent) * 0.7978845608 * (
        1.0 + 3.0 * 0.044715 * values * values
    )
    return values * halved, slope


def dot(left, right):
    return jnp.dot(left, right, preferred_element_type=F32)


def dot_back(left, right):
    return lax.dot_general(left, right, (((1,), (1,)), ((), ())), preferred_element_type=F32)


def dot_across(left, right):
    return lax.dot_general(left, right, (((0,), (0,)), ((), ())), preferred_element_type=F32)


def split(values):
    high = values.astype(BF)
    return high, (values - high.astype(F32)).astype(BF)


def sibling(values):
    return lax.ppermute(values, "core", [(0, 1), (1, 0)])


def swap_y(values):
    return lax.all_to_all(values, "y", 0, 0)


class Stream:
    def __init__(self, plan, sems):
        self.copies = [
            pltpu.make_async_copy(source, target, sems.at[index])
            for index, (source, target) in enumerate(plan)
        ]
        for copy in self.copies:
            copy.start()
        self.at = 0

    def next(self):
        self.copies[self.at].wait()
        self.at += 1


def matrices(layer, sources, target):
    return [(source.at[layer], target.at[side]) for side, source in enumerate(sources)]


def halves(extent):
    cut = extent // 2 // 128 * 128 + 128
    return ((0, cut), (cut, extent - cut))


def matrix_halves(layer, source, target, side):
    return [
        (source.at[layer, pl.ds(at, size)], target.at[side, pl.ds(at, size)])
        for at, size in halves(target.shape[1])
    ]


def finish(total, stream, left, right_ref, last, out_ref, out, sems):
    (first_at, first_size), (next_at, next_size) = halves(right_ref.shape[1])
    stream.next()
    total = total + dot(left[:, :first_size], right_ref[1, :first_size, :])
    stream.next()
    sends = []
    for index, (at, size) in enumerate(halves(right_ref.shape[2])):
        columns = slice(at, at + size)
        part = total[:, columns] + dot(left[:, next_at:], right_ref[1, next_at:, columns])
        out_ref[:, columns] = last(part, columns).astype(BF)
        send = pltpu.make_async_copy(
            out_ref.at[:, pl.ds(at, size)], out.at[:, pl.ds(at, size)], sems.at[index]
        )
        send.start()
        sends.append(send)
    for send in sends:
        send.wait()


def identity(extent):
    row = lax.broadcasted_iota(jnp.int32, (extent, extent), 0)
    col = lax.broadcasted_iota(jnp.int32, (extent, extent), 1)
    return (row == col).astype(BF)


def turned(values):
    return dot_back(identity(values.shape[1]), values)


def turned_wide(values):
    return dot_across(values, identity(values.shape[0]))


def product_kernel(at_ref, packed_ref, w1_ref, w2_ref, out, bias_ref, out_ref, sems):
    blocks, columns, _ = packed_ref.shape
    rows, hidden = w1_ref.shape
    cells = out_ref.shape[0] // STEPS
    pick_row = lax.broadcasted_iota(jnp.int32, (rows, columns), 0)
    pick_col = lax.broadcasted_iota(jnp.int32, (rows, columns), 1)
    mine = (pick_col == pick_row + rows * at_ref[1]).astype(BF)
    total = jnp.zeros((columns, cells), F32)
    for block in range(blocks):
        total = total + packed_ref[block, :, :cells].astype(F32)
    mean = jnp.sum(total, axis=0, keepdims=True) / (blocks * columns)
    local = dot(mine, packed_ref[at_ref[0]])
    high, low = split(local[:, :cells] - mean)
    out_rows = local[:, 2 * cells : 3 * cells].astype(BF)

    def modulation(index):
        block = dot(mine, packed_ref[at_ref[2 * index + 2]]).astype(BF)[:, 3 * cells :]
        row = lax.broadcasted_iota(jnp.int32, (block.shape[1], 8), 0)
        kind = lax.broadcasted_iota(jnp.int32, (block.shape[1], 8), 1)
        want = (row == 3 * (kind + LAYERS) + at_ref[2 * index + 3]) & (kind < STEPS)
        return dot(block, want.astype(BF)).astype(BF)

    shift, scale, gate = modulation(0), modulation(1), modulation(2)
    cell_row = lax.broadcasted_iota(jnp.int32, (cells, cells * STEPS), 0)
    cell_col = lax.broadcasted_iota(jnp.int32, (cells, cells * STEPS), 1)
    by_cell = (cell_col // STEPS == cell_row).astype(BF)
    step_row = lax.broadcasted_iota(jnp.int32, (8, cells * STEPS), 0)
    step_col = lax.broadcasted_iota(jnp.int32, (8, cells * STEPS), 1)
    by_step = (step_col % STEPS == step_row).astype(BF)
    left_in = (dot(high, by_cell) + dot(low, by_cell)) * (1.0 + dot(scale, by_step))
    left_out = dot(out_rows, by_cell) * dot(gate, by_step)
    gap = -hidden % 128
    out_ref[:, :hidden] = dot_across(left_in.astype(BF), w1_ref[...]).astype(BF)
    out_ref[:, hidden : hidden + gap] = jnp.zeros((cells * STEPS, gap), BF)
    out_ref[:, hidden + gap : 2 * hidden + gap] = dot_across(left_out.astype(BF), w2_ref[...]).astype(BF)
    out_ref[:, 2 * hidden + gap :] = jnp.zeros((cells * STEPS, gap), BF)
    send = pltpu.make_async_copy(out_ref, out, sems.at[0])
    send.start()
    bias_ref[...] = dot_across(shift, w1_ref[...]).astype(BF)
    send.wait()


def select_kernel(step_ref, parts_ref, bias_ref, out, out_ref, sems):
    samples, piece, _ = parts_ref.shape
    hidden = bias_ref.shape[1]
    chunk = piece // STEPS

    def at_step(extent):
        row = lax.broadcasted_iota(jnp.int32, (samples * 8, extent), 0)
        step = jnp.zeros((samples * 8, extent), jnp.int32)
        for sample in range(samples):
            step = jnp.where(row // 8 == sample, step_ref[sample] - 1, step)
        return row % 8, lax.broadcasted_iota(jnp.int32, (samples * 8, extent), 1), step

    total = parts_ref[0].astype(F32)
    for source in range(1, samples):
        total = total + parts_ref[source].astype(F32)
    place, col, step = at_step(piece)
    pick = ((col == place * STEPS + step) & (place < chunk)).astype(BF)
    chosen = dot(pick, total.astype(BF))
    out_ref[...] = chosen.astype(BF)
    place, col, step = at_step(8)
    pick = ((col == step) & (place == chunk)).astype(BF)
    out_ref[:, :hidden] = (chosen[:, :hidden] + dot(pick, bias_ref[...])).astype(BF)
    send = pltpu.make_async_copy(out_ref, out, sems.at[0])
    send.start()
    send.wait()


def student_kernel(hidden, x_ref, packed_ref, mat_ref, out_ref):
    cells, seq = x_ref.shape
    width = packed_ref.shape[0]
    lanes, wide = mat_ref.shape
    second_at = wide // 2
    group = lanes * 4 // cells
    x = turned_wide(x_ref[...]).astype(BF)
    proj = packed_ref[:, :cells]
    centered = proj.astype(F32)
    centered = centered - jnp.mean(centered, axis=0, keepdims=True)
    high, low = split(centered)
    gram = dot_across(high, high) + (dot_across(high, low) + dot_across(low, high))
    direct = dot_across(proj, packed_ref[:, 2 * cells : 3 * cells])

    def times(matrix):
        first, second = split(matrix)
        return dot(x, first) + dot(x, second)

    var = jnp.sum(times(gram) * x.astype(F32), axis=1, keepdims=True) / width
    inverse = lax.rsqrt(jnp.maximum(var, 0.0) + 1e-06)
    row = lax.broadcasted_iota(jnp.int32, (cells, lanes), 0)
    col = lax.broadcasted_iota(jnp.int32, (cells, lanes), 1)
    spread = (col == group * (row // 4) + row % 4).astype(BF)
    bias_col = lax.broadcasted_iota(jnp.int32, (8, lanes), 1)
    bias = dot((bias_col % group == 4).astype(BF), mat_ref[:, :hidden])[:1]
    z = inverse * dot(dot(x, spread).astype(BF), mat_ref[:, :hidden]) + bias
    active = gelu_both(z)[0].astype(BF)
    high, low = split(dot_back(active, mat_ref[:, second_at : second_at + hidden]))
    velocity = dot_back(high, spread) + dot_back(low, spread) + 0.125 * times(direct)
    half = seq // 2
    for target in range(out_ref.shape[0]):
        at = target % 2 * half
        out_ref[target] = velocity[at : at + half]


def first_product_kernel(packed_ref, up, out_ref, vector_ref, up_ref, left_ref, sems):
    blocks, columns, _ = packed_ref.shape
    cells = out_ref.shape[0] - 8
    stream = Stream(matrices(0, (up,), up_ref), sems)
    total = jnp.zeros((columns, cells), F32)
    for block in range(blocks):
        total = total + packed_ref[block, :, cells : 2 * cells].astype(F32)
    mean = jnp.sum(total, axis=0, keepdims=True) / (blocks * columns)

    def vector(kind, block):
        at = kind * blocks + block
        return packed_ref[at // 3, :, 3 * cells + at % 3 : 3 * cells + at % 3 + 1].astype(F32)

    for block in range(blocks):
        centered = packed_ref[block, :, cells : 2 * cells].astype(F32) - mean
        scaled = centered * (1.0 + vector(1, block))
        shift = jnp.broadcast_to(vector(0, block), (columns, 8))
        left_ref[block * columns : (block + 1) * columns, :] = jnp.concatenate(
            [scaled, shift], axis=1
        ).astype(BF)
    for source in range(blocks):
        rows = turned(packed_ref[source, :, 3 * cells : 3 * cells + 3 * LAYERS])
        for third in range(3):
            kind, block = divmod(source * 3 + third, blocks)
            for layer in range(LAYERS):
                vector_ref[
                    3 * layer + kind : 3 * layer + kind + 1, block * columns : (block + 1) * columns
                ] = rows[3 * layer + third : 3 * layer + third + 1]
    left = turned(left_ref[...]).astype(BF)
    stream.next()
    out_ref[...] = dot_back(left, up_ref[0])


def first_forward_kernel(
    where_ref, student_ref, teacher_ref, velocity_ref, x_ref, noise_ref, packed_ref, mat_own, mat_sib, own, sib,
    y_out, slope_out, latents_ref, noised_ref, g_ref, back_ref,
    w_ref, y_ref, slope_ref, both_ref, sems
):
    cells, seq = x_ref.shape
    half = seq // 2
    stream = Stream(
        matrices(0, (own,), w_ref) + matrix_halves(0, sib, w_ref, 1), sems
    )
    sample = where_ref[0]
    sigma_s = student_ref[sample].astype(F32) * 0.25
    sigma_t = teacher_ref[sample].astype(F32) * 0.001
    both_ref[0] = turned_wide(x_ref[...])
    both_ref[1] = turned_wide(noise_ref[...])
    mine = pl.ds(pl.multiple_of(where_ref[2] * half, half), half)
    latents = (both_ref[0, mine, :] - sigma_s * sum_parts(velocity_ref)).astype(BF)
    latents_ref[...] = latents
    x = ((1.0 - sigma_t) * latents.astype(F32) + sigma_t * both_ref[1, mine, :]).astype(BF)
    noised_ref[...] = x
    proj = packed_ref[:, cells : 2 * cells]
    g_0 = dot_back(x, proj).astype(BF)
    g_ref[...] = g_0
    normed, inverse = normalize(g_0.astype(F32))
    back_ref[:, :cells] = dot(normed.astype(BF), proj)
    back_ref[:, cells:] = jnp.broadcast_to(inverse, (half, cells))
    twice = jnp.concatenate([x, x], axis=1)
    actives = []
    for side, mat_ref in enumerate((mat_own, mat_sib)):
        high, low = split(mat_ref[:cells])
        z = inverse * dot(twice, jnp.concatenate([high, low], axis=0)) + mat_ref[cells : cells + 1]
        active, slope = gelu_both(z)
        slope_ref[side] = slope.astype(BF)
        actives.append(active.astype(BF))
    keep = pltpu.make_async_copy(slope_ref, slope_out, sems.at[3])
    keep.start()
    stream.next()
    y = dot(actives[0], w_ref[0])
    finish(y, stream, actives[1], w_ref, lambda part, _: part, y_ref, y_out, sems.at[pl.ds(4, 2)])
    keep.wait()


def forward_kernel(
    g_ref, vector_ref, up_own, up_sib, down_own, down_sib, y_out, slope_out,
    up_ref, down_ref, y_ref, slope_ref, sems
):
    stream = Stream(
        matrices(1, (up_own, up_sib), up_ref)
        + matrices(1, (down_own,), down_ref)
        + matrix_halves(1, down_sib, down_ref, 1),
        sems,
    )
    normed, _ = normalize(g_ref[...].astype(F32))
    u = (normed * (1.0 + vector_ref[4:5]) + vector_ref[3:4]).astype(BF)
    actives = []
    for side in range(2):
        stream.next()
        active, slope = gelu_both(dot_back(u, up_ref[side]))
        slope_ref[side] = slope.astype(BF)
        actives.append(active.astype(BF))
    keep = pltpu.make_async_copy(slope_ref, slope_out, sems.at[5])
    keep.start()
    stream.next()
    y = dot(actives[0], down_ref[0])
    finish(y, stream, actives[1], down_ref, lambda part, _: part, y_ref, y_out, sems.at[pl.ds(6, 2)])
    keep.wait()


def backward_kernel(
    dy_ref, vector_ref, slope, head, up_own, up_sib, down_own, down_sib, out,
    up_ref, down_ref, slope_ref, head_ref, out_ref, sems
):
    stream = Stream(
        [(slope, slope_ref)]
        + matrices(1, (down_own, down_sib), down_ref)
        + [(head, head_ref)]
        + matrices(1, (up_own,), up_ref)
        + matrix_halves(1, up_sib, up_ref, 1),
        sems,
    )
    dy = dy_ref[...]
    stream.next()
    dz = []
    for side in range(2):
        stream.next()
        dz.append((dot_back(dy, down_ref[side]) * slope_ref[side].astype(F32)).astype(BF))
    stream.next()
    stream.next()
    du = dot(dz[0], up_ref[0])

    def last(part, columns):
        return part * (1.0 + vector_ref[4:5, columns]) + head_ref[:, columns].astype(F32)

    finish(du, stream, dz[1], up_ref, last, out_ref, out, sems.at[pl.ds(7, 2)])


def first_backward_kernel(
    where_ref, teacher_ref, dy_ref, x_ref, back_ref, score_1, score_2, direct_ref, mat_own, mat_sib, slope, own, sib,
    out_ref, w_ref, slope_ref, all_ref, sems
):
    cells = x_ref.shape[1]
    ranges = halves(w_ref.shape[1])
    plan = matrix_halves(0, own, w_ref, 0) + matrix_halves(0, sib, w_ref, 1)
    stream = Stream([(slope, slope_ref)] + plan, sems)
    dy = dy_ref[...]
    stream.next()
    total = None
    for side, mat_ref in enumerate((mat_own, mat_sib)):
        high, low = split(mat_ref[:cells])
        for at, size in ranges:
            stream.next()
            da = dot_back(dy, w_ref[side, at : at + size, :])
            dz = (da * slope_ref[side, :, at : at + size].astype(F32)).astype(BF)
            part = dot_back(dz, high[:, at : at + size]) + dot_back(dz, low[:, at : at + size])
            total = part if total is None else total + part
    inverse = back_ref[:, cells : cells + 1]
    cross = inverse * jnp.sum(x_ref[...].astype(F32) * total, axis=1, keepdims=True) / dy.shape[1]
    rest = 1.0 - teacher_ref[where_ref[0]].astype(F32) * 0.001
    all_ref[:, :cells] = rest * (inverse * (total - back_ref[:, :cells] * cross))
    all_ref[:, cells:] = score_1[:, :cells] + score_2[:, :cells]
    rows = direct_ref.shape[0]
    mine = pl.ds(pl.multiple_of(where_ref[1] * rows, rows), rows)
    all_ref[mine, :cells] += rest * direct_ref[...]
    final = all_ref[...].T[: out_ref.shape[1]]
    for target in range(out_ref.shape[0]):
        out_ref[target] = final


def modulation_kernel(
    cond_s_ref, cond_t_ref, s_mod, t_mod, in_s, in_t, out_proj, head, out, proj_ref, head_out,
    s_ref, t_ref, stack_ref, head_ref, out_ref, head_all, sems
):
    samples = cond_t_ref.shape[0]
    cells = in_s.shape[0]
    hidden = s_mod.shape[1]
    stream = Stream(
        [(head, head_ref), (s_mod, s_ref), (t_mod, t_ref)]
        + [
            (source, stack_ref.at[pl.ds(index * cells, cells)])
            for index, source in enumerate((in_s, in_t, out_proj))
        ],
        sems,
    )
    stream.next()
    head_all[:, : head_ref.shape[1]] = head_ref[...]
    head_all[:, head_ref.shape[1] :] = jnp.zeros(
        (head_ref.shape[0], head_all.shape[1] - head_ref.shape[1]), BF
    )
    keep = pltpu.make_async_copy(head_all, head_out, sems.at[6])
    keep.start()
    stream.next()

    def product(cond, weight):
        extent = cond.shape[0]
        high, rest = split(cond)
        rest = cond - high.astype(F32)
        middle, low = split(rest)
        parts = dot(jnp.concatenate([high, middle, low], axis=0), weight)
        return (parts[:extent] + (parts[extent : 2 * extent] + parts[2 * extent :])).astype(BF)

    def place(extent, first, every):
        row = lax.broadcasted_iota(jnp.int32, (samples * 8, extent), 0)
        col = lax.broadcasted_iota(jnp.int32, (samples * 8, extent), 1)
        if every:
            return (row % 8 == first + col).astype(BF)
        return ((row // 8 == col) & (row % 8 == first)).astype(BF)

    total = dot(place(16, LAYERS, True), product(cond_s_ref[...], s_ref[...]))
    stream.next()
    for layer in range(LAYERS):
        part = product(cond_t_ref[...], t_ref[layer])
        total = total + dot(place(samples, layer, False), part)
    out_ref[:, :hidden] = total.astype(BF)
    out_ref[:, hidden:] = jnp.zeros((samples * 8, out_ref.shape[1] - hidden), BF)
    send = pltpu.make_async_copy(out_ref, out, sems.at[7])
    send.start()
    for _ in range(3):
        stream.next()
    proj_ref[...] = turned_wide(stack_ref[...]).astype(BF)
    keep.wait()
    send.wait()


def sum_parts(parts_ref):
    total = parts_ref[0].astype(F32)
    for source in range(1, parts_ref.shape[0]):
        total = total + parts_ref[source].astype(F32)
    return total


def share(values_ref, everyone, sems):
    copies = [
        pltpu.make_async_copy(values_ref, everyone.at[target], sems.at[target])
        for target in range(everyone.shape[0])
    ]
    for copy in copies:
        copy.start()
    for copy in copies:
        copy.wait()


def output_kernel(parts_ref, grad_ref, score_ref):
    cells = grad_ref.shape[0]
    half = parts_ref.shape[2]
    for core in range(2):
        total = parts_ref[core]
        for source in range(core + 2, parts_ref.shape[0], 2):
            total = total + parts_ref[source]
        columns = slice(core * half, (core + 1) * half)
        grad_ref[:, columns] = total[:cells]
        score_ref[:, columns] = total[cells : cells + score_ref.shape[0]]


def first_middle_kernel(where_ref, parts_ref, g_ref, vector_ref, mine_ref, everyone, sems):
    rows = mine_ref.shape[0]
    before = g_ref[pl.ds(pl.multiple_of(where_ref[1] * rows, rows), rows), :].astype(F32)
    after = (before + vector_ref[2:3] * sum_parts(parts_ref)).astype(BF)
    mine_ref[...] = after
    share(mine_ref, everyone, sems)


def last_middle_kernel(parts_ref, g_ref, vector_ref, mine_ref, everyone, sems):
    after = (g_ref[...].astype(F32) + vector_ref[5:6] * sum_parts(parts_ref)).astype(BF)
    mine_ref[...] = after
    share(mine_ref, everyone, sems)


def last_back_kernel(parts_ref, g_ref, vector_ref, grad_ref, everyone, share_ref, sems):
    normed, inverse = normalize(g_ref[...].astype(F32))
    grad = ln_back(sum_parts(parts_ref), normed, inverse)
    grad_ref[...] = grad
    share_ref[...] = (vector_ref[5:6] * grad).astype(BF)
    share(share_ref, everyone, sems)


def first_back_kernel(parts_ref, g_ref, old_ref, vector_ref, packed_ref, direct_ref, everyone, share_ref, sems):
    normed, inverse = normalize(g_ref[...].astype(F32))
    grad = old_ref[...] + ln_back(sum_parts(parts_ref), normed, inverse)
    cells = direct_ref.shape[1]
    direct_ref[...] = dot(grad.astype(BF), packed_ref[:, cells : 2 * cells])
    share_ref[...] = (vector_ref[2:3] * grad).astype(BF)
    share(share_ref, everyone, sems)


def block_owner(fsdp, block):
    x_hi, z = fsdp // 4, fsdp % 4
    return (x_hi ^ (block & 1)) * 4 + (z ^ ((block >> 1 & 1) ^ (block >> 2 & 1) * 3))


def swap_fsdp(values, pattern):
    other = lax.ppermute(values, "fsdp", [(at, at ^ pattern) for at in range(8)])
    return jnp.concatenate([values, other], axis=0)


def head_kernel(layer, pick_ref, where_ref, g_ref, out_own, out_sib, near, rest, back_out, score_ref, weight_ref, back_ref, use_ref, sems):
    blocks = 8
    size = near.shape[0] * 2 // blocks
    wide = near.shape[1] // 2
    plan = []
    for block in range(blocks):
        row = pl.multiple_of(block_owner(where_ref[3], block) * size, size)
        source = near if block < blocks // 2 else rest
        plan.append(
            (source.at[pl.ds(block % (blocks // 2) * size, size)], weight_ref.at[pl.ds(row, size)])
        )
    stream = Stream(plan, sems)
    use_ref[...] = jnp.zeros(use_ref.shape, F32)
    for side, outs in enumerate((out_own, out_sib)):
        for head in range(2):
            use = jnp.where(pick_ref[head] == layer, 1.0, 0.0)
            use_ref[head : head + 1, side * wide : side * wide + outs.shape[1]] = (
                use * outs[head : head + 1, :]
            )
    normed, _ = normalize(g_ref[...].astype(F32))
    quantised = normed.astype(BF)
    for _ in plan:
        stream.next()
    weight = weight_ref[...]
    e = dot(quantised, weight)
    sigm = 1.0 / (1.0 + jnp.exp(-e))
    active = e * sigm
    outs = use_ref[...]
    slope = sigm * (1.0 + e * (1.0 - sigm))
    back_ref[...] = dot_back((-(outs[0:1] + outs[1:2]) * slope).astype(BF), weight).astype(BF)
    send = pltpu.make_async_copy(back_ref, back_out, sems.at[blocks])
    send.start()
    scores = [jnp.sum(active * outs[head : head + 1], axis=1, keepdims=True) for head in range(2)]
    lane = lax.broadcasted_iota(jnp.int32, score_ref.shape, 1)
    score_ref[...] = jnp.where(lane == 0, scores[0], 0.0) + jnp.where(lane == 1, scores[1], 0.0)
    send.wait()


WHOLE = pl.BlockSpec(memory_space=pltpu.VMEM)
FAR = pl.BlockSpec(memory_space=pltpu.HBM)


def here(kernel, name, out_shape, operands, scalars=0, far=0, far_out=(), scratch=(), limit=20):
    many = isinstance(out_shape, tuple)
    near = len(operands) - scalars - far
    shapes = tuple(
        pltpu.HBM(shape.shape, shape.dtype) if index in far_out else shape
        for index, shape in enumerate(out_shape if many else (out_shape,))
    )
    operands = operands[: scalars + near] + tuple(
        pltpu.with_memory_space_constraint(operand, pltpu.HBM) for operand in operands[scalars + near :]
    )
    specs = tuple(
        FAR if index in far_out else WHOLE for index in range(len(out_shape) if many else 1)
    )
    return pl.pallas_call(
        kernel,
        name=name,
        out_shape=shapes if many else shapes[0],
        in_specs=[pl.BlockSpec(memory_space=pltpu.SMEM)] * scalars + [WHOLE] * near + [FAR] * far,
        out_specs=specs if many else specs[0],
        scratch_shapes=list(scratch),
        compiler_params=pltpu.CompilerParams(vmem_limit_bytes=limit * 2**20),
    )(*operands)


def array(shape, dtype):
    return jax.ShapeDtypeStruct(shape, dtype)


def body(
    noisy_latents,
    student_step,
    teacher_step,
    teacher_noise,
    layer_pick,
    in_proj_s,
    in_proj_t,
    out_proj,
    s_mod,
    s_w1,
    s_w2,
    t_mod,
    t_w1,
    t_w2,
    d_w1,
    d_w2,
):
    cells = in_proj_s.shape[0]
    width = in_proj_s.shape[1] * 8
    samples = student_step.shape[0]
    layers = t_w1.shape[0]
    heads = d_w2.shape[0]
    seq = noisy_latents.shape[1]
    half = seq // 2
    quarter = half // 4
    rows = s_mod.shape[0]
    hidden = s_w1.shape[1]
    columns = in_proj_s.shape[1]
    sample = lax.axis_index(SAMPLE)
    at_y = lax.axis_index("y")
    at_core = lax.axis_index("core")
    start = sample * rows

    sig_all_t = teacher_step.astype(F32) * 0.001
    sig_steps = (1 + jnp.arange(STEPS)).astype(F32) * 0.25
    cond_s = jax.nn.silu(embed_block(1000.0 * sig_steps, width, rows, start))
    cond_t = jax.nn.silu(embed_block(1000.0 * sig_all_t, width, rows, start))
    at_grp = lax.axis_index("grp")
    where = jnp.stack([sample, at_y, at_core, lax.axis_index("fsdp")]).astype(jnp.int32)
    block = sample * rows // columns
    places = [block, sample * rows // rows % (columns // rows)]
    for offset in (0, 8, 16):
        places += [(block + offset) // 3, (block + offset) % 3]
    places = jnp.stack(places).astype(jnp.int32)
    head_wide = columns + -columns % 128
    mod_wide = s_mod.shape[1] + -s_mod.shape[1] % 128
    picks = layer_pick[0]
    mod_part, projections, head_block = here(
        modulation_kernel,
        "modulation",
        (
            array((samples * 8, mod_wide), BF),
            array((columns, 3 * cells), BF),
            array((rows, head_wide), BF),
        ),
        (
            jnp.pad(cond_s, ((0, 16 - STEPS), (0, 0))),
            cond_t,
            s_mod,
            t_mod,
            in_proj_s,
            in_proj_t,
            out_proj,
            d_w1,
        ),
        far=6,
        far_out=(0, 2),
        scratch=(
            pltpu.VMEM(s_mod.shape, BF),
            pltpu.VMEM(t_mod.shape, BF),
            pltpu.VMEM((3 * cells, columns), BF),
            pltpu.VMEM(d_w1.shape, BF),
            pltpu.VMEM((samples * 8, mod_wide), BF),
            pltpu.VMEM((rows, head_wide), BF),
            pltpu.SemaphoreType.DMA((8,)),
        ),
    )
    mod_part, projections, where, places, head_block, picks = lax.optimization_barrier(
        (mod_part, projections, where, places, head_block, picks)
    )
    mod_part = mod_part.reshape(samples, 8, mod_wide)
    mods = jnp.sum(lax.all_to_all(mod_part, SAMPLE, 0, 0).astype(F32), axis=0)
    kinds = layers + STEPS
    mods = mods[:kinds, : 3 * columns].reshape(kinds * 3, columns).astype(BF)
    packed = jnp.concatenate([projections, mods.T], axis=1)
    head_block = jnp.concatenate([head_block, sibling(head_block)], axis=1)
    head_other = lax.ppermute(head_block, "grp", [(0, 1), (1, 0)])
    gathered = lax.all_gather(packed, TP, axis=0, tiled=False)
    gathered, head_other = lax.optimization_barrier((gathered, head_other))

    gap = -hidden % 128
    both_wide = 2 * (hidden + gap)
    parts, part_bias = here(
        product_kernel,
        "product",
        (
            jax.ShapeDtypeStruct((cells * STEPS, both_wide), BF),
            jax.ShapeDtypeStruct((8, hidden), BF),
        ),
        (places, gathered, s_w1, s_w2.T),
        scalars=1,
        far_out=(0,),
        scratch=(pltpu.VMEM((cells * STEPS, both_wide), BF), pltpu.SemaphoreType.DMA((1,))),
    )
    piece = cells * STEPS // samples
    chunk = cells // samples
    t_w1 = jnp.swapaxes(t_w1, 1, 2)
    parts, gathered, t_w1, t_w2, d_w2 = lax.optimization_barrier((parts, gathered, t_w1, t_w2, d_w2))
    w2_sib = sibling(t_w2)
    w1_sib = sibling(t_w1)
    d_w2_sib = sibling(d_w2)
    received = lax.all_to_all(parts.reshape(samples, piece, both_wide), SAMPLE, 0, 0)
    head_block, head_other, _ = lax.optimization_barrier((head_block, head_other, parts))
    head_pair = jnp.concatenate(
        [
            jnp.where(at_grp == 0, head_block, head_other),
            jnp.where(at_grp == 0, head_other, head_block),
        ],
        axis=0,
    )

    first_own, vectors = here(
        first_product_kernel,
        "first_product",
        (array((cells + 8, hidden), F32), array((8, width), F32)),
        (gathered, t_w1),
        far=1,
        scratch=(
            pltpu.VMEM((1, hidden, width), BF),
            pltpu.VMEM((width, cells + 8), BF),
            pltpu.SemaphoreType.DMA((1,)),
        ),
        limit=44,
    )
    received, first_own, vectors = lax.optimization_barrier((received, first_own, vectors))

    chosen = here(
        select_kernel,
        "select",
        array((samples * 8, both_wide), BF),
        (student_step, received, part_bias),
        scalars=1,
        far_out=(0,),
        scratch=(pltpu.VMEM((samples * 8, both_wide), BF), pltpu.SemaphoreType.DMA((1,))),
    )
    mine = lax.all_to_all(chosen.reshape(samples, 8, both_wide), SAMPLE, 0, 0)
    mine = mine.reshape(samples * 8, both_wide)

    latent_in = noisy_latents[0].T
    noise = teacher_noise[0].T
    packed = gathered.reshape(width, -1)
    velocity = here(
        functools.partial(student_kernel, hidden),
        "student",
        array((8, half, cells), F32),
        (latent_in, packed, mine),
    )
    head_pair, _ = lax.optimization_barrier((head_pair, mine))
    head_other = lax.ppermute(head_pair, "fsdp", [(at, at ^ 4) for at in range(8)])
    velocity = lax.all_to_all(velocity, TP, 0, 0)
    head_pair, head_other, _ = lax.optimization_barrier((head_pair, head_other, velocity))
    head_two = jnp.concatenate([head_pair, head_other], axis=0)
    head_four = swap_fsdp(head_two, 1)

    def both(values, axis):
        other = sibling(values)
        first = jnp.where(at_core == 0, values, other)
        second = jnp.where(at_core == 0, other, values)
        return jnp.concatenate([first, second], axis=axis)

    first_sib = sibling(first_own)
    velocity, w1_sib, w2_sib, d_w2_sib = lax.optimization_barrier((velocity, w1_sib, w2_sib, d_w2_sib))

    token_rows = pltpu.VMEM((half, width), BF)
    inner = pltpu.VMEM((2, half, hidden), BF)
    matrix = pltpu.VMEM((2, hidden, width), BF)
    rows_out = array((4, quarter, width), BF)
    mine_out = array((quarter, width), BF)
    tokens_out = array((half, width), BF)
    inner_out = array((2, half, hidden), BF)
    cells_out = array((half, cells), BF)
    y_0, slope_0, latents, noised, g_0, back_0 = here(
        first_forward_kernel,
        "first_forward",
        (tokens_out, inner_out, cells_out, cells_out, tokens_out, array((half, 2 * cells), F32)),
        (
            where,
            student_step,
            teacher_step,
            velocity,
            latent_in,
            noise,
            packed,
            first_own,
            first_sib,
            t_w2,
            w2_sib,
        ),
        scalars=3,
        far=2,
        far_out=(0, 1),
        scratch=(
            matrix,
            token_rows,
            inner,
            pltpu.VMEM((2, seq, cells), F32),
            pltpu.SemaphoreType.DMA((6,)),
        ),
        limit=44,
    )

    def sums(partial):
        return swap_y(partial.reshape(4, quarter, width))

    last = (t_w1, w1_sib, t_w2, w2_sib)
    four = pltpu.SemaphoreType.DMA((4,))
    quarter_rows = pltpu.VMEM((quarter, width), BF)
    g_1_mine, g_1 = here(
        first_middle_kernel,
        "first_middle",
        (mine_out, rows_out),
        (where, sums(y_0), g_0, vectors),
        scalars=1,
        far_out=(1,),
        scratch=(four,),
    )
    head_four, _ = lax.optimization_barrier((head_four, y_0))
    head_rest = lax.ppermute(head_four, "fsdp", [(at, at ^ 3) for at in range(8)])
    g_1 = swap_y(g_1).reshape(half, width)
    y_1, slope_1 = here(
        forward_kernel,
        "forward",
        (tokens_out, inner_out),
        (g_1, vectors) + last,
        far=4,
        far_out=(0, 1),
        scratch=(matrix, matrix, token_rows, inner, pltpu.SemaphoreType.DMA((8,))),
        limit=44,
    )
    g_2_mine, g_2 = here(
        last_middle_kernel,
        "last_middle",
        (mine_out, rows_out),
        (sums(y_1), g_1_mine, vectors),
        far_out=(1,),
        scratch=(four,),
    )
    g_2 = swap_y(g_2).reshape(half, width)

    def head(name, layer, g):
        return here(
            functools.partial(head_kernel, layer),
            name,
            (tokens_out, array((half, 128), F32)),
            (picks, where, g, d_w2, d_w2_sib, head_four, head_rest),
            scalars=2,
            far=2,
            far_out=(0,),
            scratch=(
                pltpu.VMEM((width, 2 * head_wide), BF),
                token_rows,
                pltpu.VMEM((8, 2 * head_wide), F32),
                pltpu.SemaphoreType.DMA((9,)),
            ),
        )

    head_back_2, scores_2 = head("head_last", 1, g_2)

    dg_2, dy_1 = here(
        last_back_kernel,
        "last_back",
        (array((quarter, width), F32), rows_out),
        (sums(head_back_2), g_2_mine, vectors),
        far_out=(1,),
        scratch=(quarter_rows, four),
    )
    g_1, latents, _ = lax.optimization_barrier((g_1, latents, dg_2))
    latents = both(latents, 0)
    head_back_1, scores_1 = head("head_first", 0, g_1)
    du_1 = here(
        backward_kernel,
        "backward",
        tokens_out,
        (swap_y(dy_1).reshape(half, width), vectors, slope_1, head_back_1) + last,
        far=6,
        far_out=(0,),
        scratch=(matrix, matrix, inner, token_rows, token_rows, pltpu.SemaphoreType.DMA((9,))),
        limit=44,
    )
    direct, dy_0 = here(
        first_back_kernel,
        "first_back",
        (array((quarter, cells), F32), rows_out),
        (sums(du_1), g_1_mine, dg_2, vectors, packed),
        far_out=(1,),
        scratch=(quarter_rows, four),
    )
    dy_0, latents = lax.optimization_barrier((swap_y(dy_0).reshape(half, width), latents))
    final = here(
        first_backward_kernel,
        "first_backward",
        array((8, cells + 8, half), F32),
        (
            where,
            teacher_step,
            dy_0,
            noised,
            back_0,
            scores_1,
            scores_2,
            direct,
            first_own,
            first_sib,
            slope_0,
            t_w2,
            w2_sib,
        ),
        scalars=2,
        far=3,
        scratch=(matrix, inner, pltpu.VMEM((half, 2 * cells), F32), pltpu.SemaphoreType.DMA((5,))),
        limit=44,
    )
    grad, scores = here(
        output_kernel,
        "output",
        (array((cells, seq), F32), array((heads, seq), F32)),
        (lax.all_to_all(final, TP, 0, 0),),
    )
    return (latents[None], scores[None], grad.T[None])


def solution(mesh):
    names = list(mesh.axis_names)
    shape = list(mesh.devices.shape)
    at = names.index("tp")
    names[at : at + 1] = ["y", "core"]
    shape[at : at + 1] = [4, 2]
    fine = Mesh(mesh.devices.reshape(shape), tuple(names))
    placed = (
        P(SAMPLE, None, None),
        P(),
        P(),
        P(SAMPLE, None, None),
        P(SAMPLE, None),
        P(None, TP),
        P(None, TP),
        P(None, TP),
        P(SAMPLE, TP),
        P(SAMPLE, TP),
        P(TP, SAMPLE),
        P(None, SAMPLE, TP),
        P(None, None, TP),
        P(None, TP, None),
        P(SAMPLE, TP),
        P(None, TP),
    )
    return jax.shard_map(
        body,
        mesh=fine,
        in_specs=placed,
        out_specs=(P(SAMPLE, None, None), P(SAMPLE, None, None), P(SAMPLE, None, None)),
        check_vma=False,
    )
```

```python
import functools
import math

import jax
import jax.numpy as jnp
from jax import lax
from jax.experimental import pallas as pl
from jax.experimental.pallas import tpu as pltpu
from jax.sharding import Mesh
from jax.sharding import PartitionSpec as P

HIGH = lax.Precision.HIGHEST
SAMPLE = ("fsdp", "grp")
TP = ("y", "core")
STEPS = 4
LAYERS = 2
BF = jnp.bfloat16
F32 = jnp.float32


def embed_block(times, width, block, start):
    half = width // 2
    column = start + jnp.arange(block)
    steps = jnp.where(column < half, column, column - half).astype(F32)
    freq = jnp.exp(-math.log(10000.0) * steps / half)
    angle = times[:, None] * freq[None, :]
    return jnp.where((column < half)[None, :], jnp.cos(angle), jnp.sin(angle))


def normalize(values):
    mean = jnp.mean(values, axis=-1, keepdims=True)
    centered = values - mean
    inverse = lax.rsqrt(jnp.mean(centered * centered, axis=-1, keepdims=True) + 1e-06)
    return (centered * inverse, inverse)


def ln_back(grad, normed, inverse):
    mean_grad = jnp.mean(grad, axis=-1, keepdims=True)
    mean_cross = jnp.mean(grad * normed, axis=-1, keepdims=True)
    return inverse * (grad - mean_grad - normed * mean_cross)


def gelu_both(values):
    inner = 0.7978845608 * (values + 0.044715 * values * values * values)
    tangent = jnp.tanh(inner)
    halved = 0.5 * (1.0 + tangent)
    slope = halved + 0.5 * values * (1.0 - tangent * tangent) * 0.7978845608 * (
        1.0 + 3.0 * 0.044715 * values * values
    )
    return values * halved, slope


def dot(left, right):
    return jnp.dot(left, right, preferred_element_type=F32)


def dot_back(left, right):
    return lax.dot_general(left, right, (((1,), (1,)), ((), ())), preferred_element_type=F32)


def dot_across(left, right):
    return lax.dot_general(left, right, (((0,), (0,)), ((), ())), preferred_element_type=F32)


def split(values):
    high = values.astype(BF)
    return high, (values - high.astype(F32)).astype(BF)


def sibling(values):
    return lax.ppermute(values, "core", [(0, 1), (1, 0)])


def swap_y(values):
    return lax.all_to_all(values, "y", 0, 0)


class Stream:
    def __init__(self, plan, sems):
        self.copies = [
            pltpu.make_async_copy(source, target, sems.at[index])
            for index, (source, target) in enumerate(plan)
        ]
        for copy in self.copies:
            copy.start()
        self.at = 0

    def next(self):
        self.copies[self.at].wait()
        self.at += 1


def matrices(layer, sources, target):
    return [(source.at[layer], target.at[side]) for side, source in enumerate(sources)]


def halves(extent):
    cut = extent // 2 // 128 * 128 + 128
    return ((0, cut), (cut, extent - cut))


def matrix_halves(layer, source, target, side):
    return [
        (source.at[layer, pl.ds(at, size)], target.at[side, pl.ds(at, size)])
        for at, size in halves(target.shape[1])
    ]


def finish(total, stream, left, right_ref, last, out_ref, out, sems):
    (first_at, first_size), (next_at, next_size) = halves(right_ref.shape[1])
    stream.next()
    total = total + dot(left[:, :first_size], right_ref[1, :first_size, :])
    stream.next()
    sends = []
    for index, (at, size) in enumerate(halves(right_ref.shape[2])):
        columns = slice(at, at + size)
        part = total[:, columns] + dot(left[:, next_at:], right_ref[1, next_at:, columns])
        out_ref[:, columns] = last(part, columns).astype(BF)
        send = pltpu.make_async_copy(
            out_ref.at[:, pl.ds(at, size)], out.at[:, pl.ds(at, size)], sems.at[index]
        )
        send.start()
        sends.append(send)
    for send in sends:
        send.wait()


def identity(extent):
    row = lax.broadcasted_iota(jnp.int32, (extent, extent), 0)
    col = lax.broadcasted_iota(jnp.int32, (extent, extent), 1)
    return (row == col).astype(BF)


def turned(values):
    return dot_back(identity(values.shape[1]), values)


def turned_wide(values):
    return dot_across(values, identity(values.shape[0]))


def product_kernel(at_ref, packed_ref, w1_ref, w2_ref, out, bias_ref, out_ref, sems):
    blocks, columns, _ = packed_ref.shape
    rows, hidden = w1_ref.shape
    cells = out_ref.shape[0] // STEPS
    pick_row = lax.broadcasted_iota(jnp.int32, (rows, columns), 0)
    pick_col = lax.broadcasted_iota(jnp.int32, (rows, columns), 1)
    mine = (pick_col == pick_row + rows * at_ref[1]).astype(BF)
    total = jnp.zeros((columns, cells), F32)
    for block in range(blocks):
        total = total + packed_ref[block, :, :cells].astype(F32)
    mean = jnp.sum(total, axis=0, keepdims=True) / (blocks * columns)
    local = dot(mine, packed_ref[at_ref[0]])
    high, low = split(local[:, :cells] - mean)
    out_rows = local[:, 2 * cells : 3 * cells].astype(BF)

    def modulation(index):
        block = dot(mine, packed_ref[at_ref[2 * index + 2]]).astype(BF)[:, 3 * cells :]
        row = lax.broadcasted_iota(jnp.int32, (block.shape[1], 8), 0)
        kind = lax.broadcasted_iota(jnp.int32, (block.shape[1], 8), 1)
        want = (row == 3 * (kind + LAYERS) + at_ref[2 * index + 3]) & (kind < STEPS)
        return dot(block, want.astype(BF)).astype(BF)

    shift, scale, gate = modulation(0), modulation(1), modulation(2)
    cell_row = lax.broadcasted_iota(jnp.int32, (cells, cells * STEPS), 0)
    cell_col = lax.broadcasted_iota(jnp.int32, (cells, cells * STEPS), 1)
    by_cell = (cell_col // STEPS == cell_row).astype(BF)
    step_row = lax.broadcasted_iota(jnp.int32, (8, cells * STEPS), 0)
    step_col = lax.broadcasted_iota(jnp.int32, (8, cells * STEPS), 1)
    by_step = (step_col % STEPS == step_row).astype(BF)
    left_in = (dot(high, by_cell) + dot(low, by_cell)) * (1.0 + dot(scale, by_step))
    left_out = dot(out_rows, by_cell) * dot(gate, by_step)
    gap = -hidden % 128
    out_ref[:, :hidden] = dot_across(left_in.astype(BF), w1_ref[...]).astype(BF)
    out_ref[:, hidden : hidden + gap] = jnp.zeros((cells * STEPS, gap), BF)
    out_ref[:, hidden + gap : 2 * hidden + gap] = dot_across(left_out.astype(BF), w2_ref[...]).astype(BF)
    out_ref[:, 2 * hidden + gap :] = jnp.zeros((cells * STEPS, gap), BF)
    send = pltpu.make_async_copy(out_ref, out, sems.at[0])
    send.start()
    bias_ref[...] = dot_across(shift, w1_ref[...]).astype(BF)
    send.wait()


def select_kernel(step_ref, parts_ref, bias_ref, out, out_ref, sems):
    samples, piece, _ = parts_ref.shape
    hidden = bias_ref.shape[1]
    chunk = piece // STEPS

    def at_step(extent):
        row = lax.broadcasted_iota(jnp.int32, (samples * 8, extent), 0)
        step = jnp.zeros((samples * 8, extent), jnp.int32)
        for sample in range(samples):
            step = jnp.where(row // 8 == sample, step_ref[sample] - 1, step)
        return row % 8, lax.broadcasted_iota(jnp.int32, (samples * 8, extent), 1), step

    total = parts_ref[0].astype(F32)
    for source in range(1, samples):
        total = total + parts_ref[source].astype(F32)
    place, col, step = at_step(piece)
    pick = ((col == place * STEPS + step) & (place < chunk)).astype(BF)
    chosen = dot(pick, total.astype(BF))
    out_ref[...] = chosen.astype(BF)
    place, col, step = at_step(8)
    pick = ((col == step) & (place == chunk)).astype(BF)
    out_ref[:, :hidden] = (chosen[:, :hidden] + dot(pick, bias_ref[...])).astype(BF)
    send = pltpu.make_async_copy(out_ref, out, sems.at[0])
    send.start()
    send.wait()


def student_kernel(hidden, x_ref, packed_ref, mat_ref, out_ref):
    cells, seq = x_ref.shape
    width = packed_ref.shape[0]
    lanes, wide = mat_ref.shape
    second_at = wide // 2
    group = lanes * 4 // cells
    x = turned_wide(x_ref[...]).astype(BF)
    proj = packed_ref[:, :cells]
    centered = proj.astype(F32)
    centered = centered - jnp.mean(centered, axis=0, keepdims=True)
    high, low = split(centered)
    gram = dot_across(high, high) + (dot_across(high, low) + dot_across(low, high))
    direct = dot_across(proj, packed_ref[:, 2 * cells : 3 * cells])

    def times(matrix):
        first, second = split(matrix)
        return dot(x, first) + dot(x, second)

    var = jnp.sum(times(gram) * x.astype(F32), axis=1, keepdims=True) / width
    inverse = lax.rsqrt(jnp.maximum(var, 0.0) + 1e-06)
    row = lax.broadcasted_iota(jnp.int32, (cells, lanes), 0)
    col = lax.broadcasted_iota(jnp.int32, (cells, lanes), 1)
    spread = (col == group * (row // 4) + row % 4).astype(BF)
    bias_col = lax.broadcasted_iota(jnp.int32, (8, lanes), 1)
    bias = dot((bias_col % group == 4).astype(BF), mat_ref[:, :hidden])[:1]
    z = inverse * dot(dot(x, spread).astype(BF), mat_ref[:, :hidden]) + bias
    active = gelu_both(z)[0].astype(BF)
    high, low = split(dot_back(active, mat_ref[:, second_at : second_at + hidden]))
    velocity = dot_back(high, spread) + dot_back(low, spread) + 0.125 * times(direct)
    half = seq // 2
    for target in range(out_ref.shape[0]):
        at = target % 2 * half
        out_ref[target] = velocity[at : at + half]


def first_product_kernel(packed_ref, up, out_ref, vector_ref, up_ref, left_ref, sems):
    blocks, columns, _ = packed_ref.shape
    cells = out_ref.shape[0] - 8
    stream = Stream(matrices(0, (up,), up_ref), sems)
    total = jnp.zeros((columns, cells), F32)
    for block in range(blocks):
        total = total + packed_ref[block, :, cells : 2 * cells].astype(F32)
    mean = jnp.sum(total, axis=0, keepdims=True) / (blocks * columns)

    def vector(kind, block):
        at = kind * blocks + block
        return packed_ref[at // 3, :, 3 * cells + at % 3 : 3 * cells + at % 3 + 1].astype(F32)

    for block in range(blocks):
        centered = packed_ref[block, :, cells : 2 * cells].astype(F32) - mean
        scaled = centered * (1.0 + vector(1, block))
        shift = jnp.broadcast_to(vector(0, block), (columns, 8))
        left_ref[block * columns : (block + 1) * columns, :] = jnp.concatenate(
            [scaled, shift], axis=1
        ).astype(BF)
    for source in range(blocks):
        rows = turned(packed_ref[source, :, 3 * cells : 3 * cells + 3 * LAYERS])
        for third in range(3):
            kind, block = divmod(source * 3 + third, blocks)
            for layer in range(LAYERS):
                vector_ref[
                    3 * layer + kind : 3 * layer + kind + 1, block * columns : (block + 1) * columns
                ] = rows[3 * layer + third : 3 * layer + third + 1]
    left = turned(left_ref[...]).astype(BF)
    stream.next()
    out_ref[...] = dot_back(left, up_ref[0])


def first_forward_kernel(
    where_ref, student_ref, teacher_ref, velocity_ref, x_ref, noise_ref, packed_ref, mat_own, mat_sib, own, sib,
    y_out, slope_out, latents_ref, noised_ref, g_ref, back_ref,
    w_ref, y_ref, slope_ref, both_ref, sems
):
    cells, seq = x_ref.shape
    half = seq // 2
    stream = Stream(
        matrices(0, (own,), w_ref) + matrix_halves(0, sib, w_ref, 1), sems
    )
    sample = where_ref[0]
    sigma_s = student_ref[sample].astype(F32) * 0.25
    sigma_t = teacher_ref[sample].astype(F32) * 0.001
    both_ref[0] = turned_wide(x_ref[...])
    both_ref[1] = turned_wide(noise_ref[...])
    mine = pl.ds(pl.multiple_of(where_ref[2] * half, half), half)
    latents = (both_ref[0, mine, :] - sigma_s * sum_parts(velocity_ref)).astype(BF)
    latents_ref[...] = latents
    x = ((1.0 - sigma_t) * latents.astype(F32) + sigma_t * both_ref[1, mine, :]).astype(BF)
    noised_ref[...] = x
    proj = packed_ref[:, cells : 2 * cells]
    g_0 = dot_back(x, proj).astype(BF)
    g_ref[...] = g_0
    normed, inverse = normalize(g_0.astype(F32))
    back_ref[:, :cells] = dot(normed.astype(BF), proj)
    back_ref[:, cells:] = jnp.broadcast_to(inverse, (half, cells))
    twice = jnp.concatenate([x, x], axis=1)
    actives = []
    for side, mat_ref in enumerate((mat_own, mat_sib)):
        high, low = split(mat_ref[:cells])
        z = inverse * dot(twice, jnp.concatenate([high, low], axis=0)) + mat_ref[cells : cells + 1]
        active, slope = gelu_both(z)
        slope_ref[side] = slope.astype(BF)
        actives.append(active.astype(BF))
    keep = pltpu.make_async_copy(slope_ref, slope_out, sems.at[3])
    keep.start()
    stream.next()
    y = dot(actives[0], w_ref[0])
    finish(y, stream, actives[1], w_ref, lambda part, _: part, y_ref, y_out, sems.at[pl.ds(4, 2)])
    keep.wait()


def forward_kernel(
    g_ref, vector_ref, up_own, up_sib, down_own, down_sib, y_out, slope_out,
    up_ref, down_ref, y_ref, slope_ref, sems
):
    stream = Stream(
        matrices(1, (up_own, up_sib), up_ref)
        + matrices(1, (down_own,), down_ref)
        + matrix_halves(1, down_sib, down_ref, 1),
        sems,
    )
    normed, _ = normalize(g_ref[...].astype(F32))
    u = (normed * (1.0 + vector_ref[4:5]) + vector_ref[3:4]).astype(BF)
    actives = []
    for side in range(2):
        stream.next()
        active, slope = gelu_both(dot_back(u, up_ref[side]))
        slope_ref[side] = slope.astype(BF)
        actives.append(active.astype(BF))
    keep = pltpu.make_async_copy(slope_ref, slope_out, sems.at[5])
    keep.start()
    stream.next()
    y = dot(actives[0], down_ref[0])
    finish(y, stream, actives[1], down_ref, lambda part, _: part, y_ref, y_out, sems.at[pl.ds(6, 2)])
    keep.wait()


def backward_kernel(
    dy_ref, vector_ref, slope, head, up_own, up_sib, down_own, down_sib, out,
    up_ref, down_ref, slope_ref, head_ref, out_ref, sems
):
    stream = Stream(
        [(slope, slope_ref)]
        + matrices(1, (down_own, down_sib), down_ref)
        + [(head, head_ref)]
        + matrices(1, (up_own,), up_ref)
        + matrix_halves(1, up_sib, up_ref, 1),
        sems,
    )
    dy = dy_ref[...]
    stream.next()
    dz = []
    for side in range(2):
        stream.next()
        dz.append((dot_back(dy, down_ref[side]) * slope_ref[side].astype(F32)).astype(BF))
    stream.next()
    stream.next()
    du = dot(dz[0], up_ref[0])

    def last(part, columns):
        return part * (1.0 + vector_ref[4:5, columns]) + head_ref[:, columns].astype(F32)

    finish(du, stream, dz[1], up_ref, last, out_ref, out, sems.at[pl.ds(7, 2)])


def first_backward_kernel(
    where_ref, teacher_ref, dy_ref, x_ref, back_ref, score_1, score_2, direct_ref, mat_own, mat_sib, slope, own, sib,
    out_ref, w_ref, slope_ref, all_ref, sems
):
    cells = x_ref.shape[1]
    ranges = halves(w_ref.shape[1])
    plan = matrix_halves(0, own, w_ref, 0) + matrix_halves(0, sib, w_ref, 1)
    stream = Stream([(slope, slope_ref)] + plan, sems)
    dy = dy_ref[...]
    stream.next()
    total = None
    for side, mat_ref in enumerate((mat_own, mat_sib)):
        high, low = split(mat_ref[:cells])
        for at, size in ranges:
            stream.next()
            da = dot_back(dy, w_ref[side, at : at + size, :])
            dz = (da * slope_ref[side, :, at : at + size].astype(F32)).astype(BF)
            part = dot_back(dz, high[:, at : at + size]) + dot_back(dz, low[:, at : at + size])
            total = part if total is None else total + part
    inverse = back_ref[:, cells : cells + 1]
    cross = inverse * jnp.sum(x_ref[...].astype(F32) * total, axis=1, keepdims=True) / dy.shape[1]
    rest = 1.0 - teacher_ref[where_ref[0]].astype(F32) * 0.001
    all_ref[:, :cells] = rest * (inverse * (total - back_ref[:, :cells] * cross))
    all_ref[:, cells:] = score_1[:, :cells] + score_2[:, :cells]
    rows = direct_ref.shape[0]
    mine = pl.ds(pl.multiple_of(where_ref[1] * rows, rows), rows)
    all_ref[mine, :cells] += rest * direct_ref[...]
    final = all_ref[...].T[: out_ref.shape[1]]
    for target in range(out_ref.shape[0]):
        out_ref[target] = final


def modulation_kernel(
    cond_s_ref, cond_t_ref, s_ref, t_ref, head_ref, in_s, in_t, out_proj, out, proj_ref, head_all,
    stack_ref, out_ref, sems
):
    samples = cond_t_ref.shape[0]
    cells = in_s.shape[0]
    hidden = s_ref.shape[1]
    stream = Stream(
        [
            (source, stack_ref.at[pl.ds(index * cells, cells)])
            for index, source in enumerate((in_s, in_t, out_proj))
        ],
        sems,
    )
    head_all[:, : head_ref.shape[1]] = head_ref[...]
    head_all[:, head_ref.shape[1] :] = jnp.zeros(
        (head_ref.shape[0], head_all.shape[1] - head_ref.shape[1]), BF
    )

    def product(cond, weight):
        extent = cond.shape[0]
        high, rest = split(cond)
        rest = cond - high.astype(F32)
        middle, low = split(rest)
        parts = dot(jnp.concatenate([high, middle, low], axis=0), weight)
        return (parts[:extent] + (parts[extent : 2 * extent] + parts[2 * extent :])).astype(BF)

    def place(extent, first, every):
        row = lax.broadcasted_iota(jnp.int32, (samples * 8, extent), 0)
        col = lax.broadcasted_iota(jnp.int32, (samples * 8, extent), 1)
        if every:
            return (row % 8 == first + col).astype(BF)
        return ((row // 8 == col) & (row % 8 == first)).astype(BF)

    total = dot(place(16, LAYERS, True), product(cond_s_ref[...], s_ref[...]))
    for layer in range(LAYERS):
        part = product(cond_t_ref[...], t_ref[layer])
        total = total + dot(place(samples, layer, False), part)
    out_ref[:, :hidden] = total.astype(BF)
    out_ref[:, hidden:] = jnp.zeros((samples * 8, out_ref.shape[1] - hidden), BF)
    send = pltpu.make_async_copy(out_ref, out, sems.at[3])
    send.start()
    for _ in range(3):
        stream.next()
    proj_ref[...] = turned_wide(stack_ref[...]).astype(BF)
    send.wait()


def sum_parts(parts_ref):
    total = parts_ref[0].astype(F32)
    for source in range(1, parts_ref.shape[0]):
        total = total + parts_ref[source].astype(F32)
    return total


def share(values_ref, everyone, sems):
    copies = [
        pltpu.make_async_copy(values_ref, everyone.at[target], sems.at[target])
        for target in range(everyone.shape[0])
    ]
    for copy in copies:
        copy.start()
    for copy in copies:
        copy.wait()


def output_kernel(parts_ref, grad_ref, score_ref):
    cells = grad_ref.shape[0]
    half = parts_ref.shape[2]
    for core in range(2):
        total = parts_ref[core]
        for source in range(core + 2, parts_ref.shape[0], 2):
            total = total + parts_ref[source]
        columns = slice(core * half, (core + 1) * half)
        grad_ref[:, columns] = total[:cells]
        score_ref[:, columns] = total[cells : cells + score_ref.shape[0]]


def first_middle_kernel(where_ref, parts_ref, g_ref, vector_ref, mine_ref, everyone, sems):
    rows = mine_ref.shape[0]
    before = g_ref[pl.ds(pl.multiple_of(where_ref[1] * rows, rows), rows), :].astype(F32)
    after = (before + vector_ref[2:3] * sum_parts(parts_ref)).astype(BF)
    mine_ref[...] = after
    share(mine_ref, everyone, sems)


def last_middle_kernel(parts_ref, g_ref, vector_ref, mine_ref, everyone, sems):
    after = (g_ref[...].astype(F32) + vector_ref[5:6] * sum_parts(parts_ref)).astype(BF)
    mine_ref[...] = after
    share(mine_ref, everyone, sems)


def last_back_kernel(parts_ref, g_ref, vector_ref, grad_ref, everyone, share_ref, sems):
    normed, inverse = normalize(g_ref[...].astype(F32))
    grad = ln_back(sum_parts(parts_ref), normed, inverse)
    grad_ref[...] = grad
    share_ref[...] = (vector_ref[5:6] * grad).astype(BF)
    share(share_ref, everyone, sems)


def first_back_kernel(parts_ref, g_ref, old_ref, vector_ref, packed_ref, direct_ref, everyone, share_ref, sems):
    normed, inverse = normalize(g_ref[...].astype(F32))
    grad = old_ref[...] + ln_back(sum_parts(parts_ref), normed, inverse)
    cells = direct_ref.shape[1]
    direct_ref[...] = dot(grad.astype(BF), packed_ref[:, cells : 2 * cells])
    share_ref[...] = (vector_ref[2:3] * grad).astype(BF)
    share(share_ref, everyone, sems)


def block_owner(fsdp, block):
    x_hi, z = fsdp // 4, fsdp % 4
    return (x_hi ^ (block & 1)) * 4 + (z ^ ((block >> 1 & 1) ^ (block >> 2 & 1) * 3))


def swap_fsdp(values, pattern):
    other = lax.ppermute(values, "fsdp", [(at, at ^ pattern) for at in range(8)])
    return jnp.concatenate([values, other], axis=0)


def head_kernel(layer, pick_ref, where_ref, g_ref, out_own, out_sib, near, rest, back_out, score_ref, weight_ref, back_ref, use_ref, sems):
    blocks = 8
    size = near.shape[0] * 2 // blocks
    wide = near.shape[1] // 2
    plan = []
    for block in range(blocks):
        row = pl.multiple_of(block_owner(where_ref[3], block) * size, size)
        source = near if block < blocks // 2 else rest
        plan.append(
            (source.at[pl.ds(block % (blocks // 2) * size, size)], weight_ref.at[pl.ds(row, size)])
        )
    stream = Stream(plan, sems)
    use_ref[...] = jnp.zeros(use_ref.shape, F32)
    for side, outs in enumerate((out_own, out_sib)):
        for head in range(2):
            use = jnp.where(pick_ref[head] == layer, 1.0, 0.0)
            use_ref[head : head + 1, side * wide : side * wide + outs.shape[1]] = (
                use * outs[head : head + 1, :]
            )
    normed, _ = normalize(g_ref[...].astype(F32))
    quantised = normed.astype(BF)
    for _ in plan:
        stream.next()
    weight = weight_ref[...]
    e = dot(quantised, weight)
    sigm = 1.0 / (1.0 + jnp.exp(-e))
    active = e * sigm
    outs = use_ref[...]
    slope = sigm * (1.0 + e * (1.0 - sigm))
    back_ref[...] = dot_back((-(outs[0:1] + outs[1:2]) * slope).astype(BF), weight).astype(BF)
    send = pltpu.make_async_copy(back_ref, back_out, sems.at[blocks])
    send.start()
    scores = [jnp.sum(active * outs[head : head + 1], axis=1, keepdims=True) for head in range(2)]
    lane = lax.broadcasted_iota(jnp.int32, score_ref.shape, 1)
    score_ref[...] = jnp.where(lane == 0, scores[0], 0.0) + jnp.where(lane == 1, scores[1], 0.0)
    send.wait()


WHOLE = pl.BlockSpec(memory_space=pltpu.VMEM)
FAR = pl.BlockSpec(memory_space=pltpu.HBM)


def here(kernel, name, out_shape, operands, scalars=0, far=0, far_out=(), scratch=(), limit=20):
    many = isinstance(out_shape, tuple)
    near = len(operands) - scalars - far
    shapes = tuple(
        pltpu.HBM(shape.shape, shape.dtype) if index in far_out else shape
        for index, shape in enumerate(out_shape if many else (out_shape,))
    )
    operands = operands[: scalars + near] + tuple(
        pltpu.with_memory_space_constraint(operand, pltpu.HBM) for operand in operands[scalars + near :]
    )
    specs = tuple(
        FAR if index in far_out else WHOLE for index in range(len(out_shape) if many else 1)
    )
    return pl.pallas_call(
        kernel,
        name=name,
        out_shape=shapes if many else shapes[0],
        in_specs=[pl.BlockSpec(memory_space=pltpu.SMEM)] * scalars + [WHOLE] * near + [FAR] * far,
        out_specs=specs if many else specs[0],
        scratch_shapes=list(scratch),
        compiler_params=pltpu.CompilerParams(vmem_limit_bytes=limit * 2**20),
    )(*operands)


def array(shape, dtype):
    return jax.ShapeDtypeStruct(shape, dtype)


def body(
    noisy_latents,
    student_step,
    teacher_step,
    teacher_noise,
    layer_pick,
    in_proj_s,
    in_proj_t,
    out_proj,
    s_mod,
    s_w1,
    s_w2,
    t_mod,
    t_w1,
    t_w2,
    d_w1,
    d_w2,
):
    cells = in_proj_s.shape[0]
    width = in_proj_s.shape[1] * 8
    samples = student_step.shape[0]
    layers = t_w1.shape[0]
    heads = d_w2.shape[0]
    seq = noisy_latents.shape[1]
    half = seq // 2
    quarter = half // 4
    rows = s_mod.shape[0]
    hidden = s_w1.shape[1]
    columns = in_proj_s.shape[1]
    sample = lax.axis_index(SAMPLE)
    at_y = lax.axis_index("y")
    at_core = lax.axis_index("core")
    start = sample * rows

    sig_all_t = teacher_step.astype(F32) * 0.001
    sig_steps = (1 + jnp.arange(STEPS)).astype(F32) * 0.25
    cond_s = jax.nn.silu(embed_block(1000.0 * sig_steps, width, rows, start))
    cond_t = jax.nn.silu(embed_block(1000.0 * sig_all_t, width, rows, start))
    at_grp = lax.axis_index("grp")
    where = jnp.stack([sample, at_y, at_core, lax.axis_index("fsdp")]).astype(jnp.int32)
    block = sample * rows // columns
    places = [block, sample * rows // rows % (columns // rows)]
    for offset in (0, 8, 16):
        places += [(block + offset) // 3, (block + offset) % 3]
    places = jnp.stack(places).astype(jnp.int32)
    head_wide = columns + -columns % 128
    mod_wide = s_mod.shape[1] + -s_mod.shape[1] % 128
    picks = layer_pick[0]
    mod_part, projections, head_block = here(
        modulation_kernel,
        "modulation",
        (
            array((samples * 8, mod_wide), BF),
            array((columns, 3 * cells), BF),
            array((rows, head_wide), BF),
        ),
        (
            jnp.pad(cond_s, ((0, 16 - STEPS), (0, 0))),
            cond_t,
            s_mod,
            t_mod,
            d_w1,
            in_proj_s,
            in_proj_t,
            out_proj,
        ),
        far=3,
        far_out=(0,),
        scratch=(
            pltpu.VMEM((3 * cells, columns), BF),
            pltpu.VMEM((samples * 8, mod_wide), BF),
            pltpu.SemaphoreType.DMA((4,)),
        ),
    )
    mod_part, projections, where, places, head_block, picks = lax.optimization_barrier(
        (mod_part, projections, where, places, head_block, picks)
    )
    mod_part = mod_part.reshape(samples, 8, mod_wide)
    mods = jnp.sum(lax.all_to_all(mod_part, SAMPLE, 0, 0).astype(F32), axis=0)
    kinds = layers + STEPS
    mods = mods[:kinds, : 3 * columns].reshape(kinds * 3, columns).astype(BF)
    packed = jnp.concatenate([projections, mods.T], axis=1)
    head_block = jnp.concatenate([head_block, sibling(head_block)], axis=1)
    head_other = lax.ppermute(head_block, "grp", [(0, 1), (1, 0)])
    gathered = lax.all_gather(packed, TP, axis=0, tiled=False)
    gathered, head_other = lax.optimization_barrier((gathered, head_other))

    gap = -hidden % 128
    both_wide = 2 * (hidden + gap)
    parts, part_bias = here(
        product_kernel,
        "product",
        (
            jax.ShapeDtypeStruct((cells * STEPS, both_wide), BF),
            jax.ShapeDtypeStruct((8, hidden), BF),
        ),
        (places, gathered, s_w1, s_w2.T),
        scalars=1,
        far_out=(0,),
        scratch=(pltpu.VMEM((cells * STEPS, both_wide), BF), pltpu.SemaphoreType.DMA((1,))),
    )
    piece = cells * STEPS // samples
    chunk = cells // samples
    t_w1 = jnp.swapaxes(t_w1, 1, 2)
    parts, gathered, t_w1, t_w2, d_w2 = lax.optimization_barrier((parts, gathered, t_w1, t_w2, d_w2))
    w2_sib = sibling(t_w2)
    w1_sib = sibling(t_w1)
    d_w2_sib = sibling(d_w2)
    received = lax.all_to_all(parts.reshape(samples, piece, both_wide), SAMPLE, 0, 0)
    head_block, head_other, _ = lax.optimization_barrier((head_block, head_other, parts))
    head_pair = jnp.concatenate(
        [
            jnp.where(at_grp == 0, head_block, head_other),
            jnp.where(at_grp == 0, head_other, head_block),
        ],
        axis=0,
    )

    first_own, vectors = here(
        first_product_kernel,
        "first_product",
        (array((cells + 8, hidden), F32), array((8, width), F32)),
        (gathered, t_w1),
        far=1,
        scratch=(
            pltpu.VMEM((1, hidden, width), BF),
            pltpu.VMEM((width, cells + 8), BF),
            pltpu.SemaphoreType.DMA((1,)),
        ),
        limit=44,
    )
    received, first_own, vectors = lax.optimization_barrier((received, first_own, vectors))

    chosen = here(
        select_kernel,
        "select",
        array((samples * 8, both_wide), BF),
        (student_step, received, part_bias),
        scalars=1,
        far_out=(0,),
        scratch=(pltpu.VMEM((samples * 8, both_wide), BF), pltpu.SemaphoreType.DMA((1,))),
    )
    mine = lax.all_to_all(chosen.reshape(samples, 8, both_wide), SAMPLE, 0, 0)
    mine = mine.reshape(samples * 8, both_wide)

    latent_in = noisy_latents[0].T
    noise = teacher_noise[0].T
    packed = gathered.reshape(width, -1)
    velocity = here(
        functools.partial(student_kernel, hidden),
        "student",
        array((8, half, cells), F32),
        (latent_in, packed, mine),
    )
    head_pair, _ = lax.optimization_barrier((head_pair, mine))
    head_other = lax.ppermute(head_pair, "fsdp", [(at, at ^ 4) for at in range(8)])
    velocity = lax.all_to_all(velocity, TP, 0, 0)
    head_pair, head_other, _ = lax.optimization_barrier((head_pair, head_other, velocity))
    head_two = jnp.concatenate([head_pair, head_other], axis=0)
    head_four = swap_fsdp(head_two, 1)

    def both(values, axis):
        other = sibling(values)
        first = jnp.where(at_core == 0, values, other)
        second = jnp.where(at_core == 0, other, values)
        return jnp.concatenate([first, second], axis=axis)

    first_sib = sibling(first_own)
    velocity, w1_sib, w2_sib, d_w2_sib = lax.optimization_barrier((velocity, w1_sib, w2_sib, d_w2_sib))

    token_rows = pltpu.VMEM((half, width), BF)
    inner = pltpu.VMEM((2, half, hidden), BF)
    matrix = pltpu.VMEM((2, hidden, width), BF)
    rows_out = array((4, quarter, width), BF)
    mine_out = array((quarter, width), BF)
    tokens_out = array((half, width), BF)
    inner_out = array((2, half, hidden), BF)
    cells_out = array((half, cells), BF)
    y_0, slope_0, latents, noised, g_0, back_0 = here(
        first_forward_kernel,
        "first_forward",
        (tokens_out, inner_out, cells_out, cells_out, tokens_out, array((half, 2 * cells), F32)),
        (
            where,
            student_step,
            teacher_step,
            velocity,
            latent_in,
            noise,
            packed,
            first_own,
            first_sib,
            t_w2,
            w2_sib,
        ),
        scalars=3,
        far=2,
        far_out=(0, 1),
        scratch=(
            matrix,
            token_rows,
            inner,
            pltpu.VMEM((2, seq, cells), F32),
            pltpu.SemaphoreType.DMA((6,)),
        ),
        limit=44,
    )

    def sums(partial):
        return swap_y(partial.reshape(4, quarter, width))

    last = (t_w1, w1_sib, t_w2, w2_sib)
    four = pltpu.SemaphoreType.DMA((4,))
    quarter_rows = pltpu.VMEM((quarter, width), BF)
    g_1_mine, g_1 = here(
        first_middle_kernel,
        "first_middle",
        (mine_out, rows_out),
        (where, sums(y_0), g_0, vectors),
        scalars=1,
        far_out=(1,),
        scratch=(four,),
    )
    head_four, _ = lax.optimization_barrier((head_four, y_0))
    head_rest = lax.ppermute(head_four, "fsdp", [(at, at ^ 3) for at in range(8)])
    g_1 = swap_y(g_1).reshape(half, width)
    y_1, slope_1 = here(
        forward_kernel,
        "forward",
        (tokens_out, inner_out),
        (g_1, vectors) + last,
        far=4,
        far_out=(0, 1),
        scratch=(matrix, matrix, token_rows, inner, pltpu.SemaphoreType.DMA((8,))),
        limit=44,
    )
    g_2_mine, g_2 = here(
        last_middle_kernel,
        "last_middle",
        (mine_out, rows_out),
        (sums(y_1), g_1_mine, vectors),
        far_out=(1,),
        scratch=(four,),
    )
    g_2 = swap_y(g_2).reshape(half, width)

    def head(name, layer, g):
        return here(
            functools.partial(head_kernel, layer),
            name,
            (tokens_out, array((half, 128), F32)),
            (picks, where, g, d_w2, d_w2_sib, head_four, head_rest),
            scalars=2,
            far=2,
            far_out=(0,),
            scratch=(
                pltpu.VMEM((width, 2 * head_wide), BF),
                token_rows,
                pltpu.VMEM((8, 2 * head_wide), F32),
                pltpu.SemaphoreType.DMA((9,)),
            ),
        )

    head_back_2, scores_2 = head("head_last", 1, g_2)

    dg_2, dy_1 = here(
        last_back_kernel,
        "last_back",
        (array((quarter, width), F32), rows_out),
        (sums(head_back_2), g_2_mine, vectors),
        far_out=(1,),
        scratch=(quarter_rows, four),
    )
    g_1, latents, _ = lax.optimization_barrier((g_1, latents, dg_2))
    latents = both(latents, 0)
    head_back_1, scores_1 = head("head_first", 0, g_1)
    du_1 = here(
        backward_kernel,
        "backward",
        tokens_out,
        (swap_y(dy_1).reshape(half, width), vectors, slope_1, head_back_1) + last,
        far=6,
        far_out=(0,),
        scratch=(matrix, matrix, inner, token_rows, token_rows, pltpu.SemaphoreType.DMA((9,))),
        limit=44,
    )
    direct, dy_0 = here(
        first_back_kernel,
        "first_back",
        (array((quarter, cells), F32), rows_out),
        (sums(du_1), g_1_mine, dg_2, vectors, packed),
        far_out=(1,),
        scratch=(quarter_rows, four),
    )
    dy_0, latents = lax.optimization_barrier((swap_y(dy_0).reshape(half, width), latents))
    final = here(
        first_backward_kernel,
        "first_backward",
        array((8, cells + 8, half), F32),
        (
            where,
            teacher_step,
            dy_0,
            noised,
            back_0,
            scores_1,
            scores_2,
            direct,
            first_own,
            first_sib,
            slope_0,
            t_w2,
            w2_sib,
        ),
        scalars=2,
        far=3,
        scratch=(matrix, inner, pltpu.VMEM((half, 2 * cells), F32), pltpu.SemaphoreType.DMA((5,))),
        limit=44,
    )
    grad, scores = here(
        output_kernel,
        "output",
        (array((cells, seq), F32), array((heads, seq), F32)),
        (lax.all_to_all(final, TP, 0, 0),),
    )
    return (latents[None], scores[None], grad.T[None])


def solution(mesh):
    names = list(mesh.axis_names)
    shape = list(mesh.devices.shape)
    at = names.index("tp")
    names[at : at + 1] = ["y", "core"]
    shape[at : at + 1] = [4, 2]
    fine = Mesh(mesh.devices.reshape(shape), tuple(names))
    placed = (
        P(SAMPLE, None, None),
        P(),
        P(),
        P(SAMPLE, None, None),
        P(SAMPLE, None),
        P(None, TP),
        P(None, TP),
        P(None, TP),
        P(SAMPLE, TP),
        P(SAMPLE, TP),
        P(TP, SAMPLE),
        P(None, SAMPLE, TP),
        P(None, None, TP),
        P(None, TP, None),
        P(SAMPLE, TP),
        P(None, TP),
    )
    return jax.shard_map(
        body,
        mesh=fine,
        in_specs=placed,
        out_specs=(P(SAMPLE, None, None), P(SAMPLE, None, None), P(SAMPLE, None, None)),
        check_vma=False,
    )
```

```python
import functools
import math

import jax
import jax.numpy as jnp
from jax import lax
from jax.experimental import pallas as pl
from jax.experimental.pallas import tpu as pltpu
from jax.sharding import Mesh
from jax.sharding import PartitionSpec as P

HIGH = lax.Precision.HIGHEST
SAMPLE = ("fsdp", "grp")
TP = ("y", "core")
STEPS = 4
LAYERS = 2
BF = jnp.bfloat16
F32 = jnp.float32


def embed_block(times, width, block, start):
    half = width // 2
    column = start + jnp.arange(block)
    steps = jnp.where(column < half, column, column - half).astype(F32)
    freq = jnp.exp(-math.log(10000.0) * steps / half)
    angle = times[:, None] * freq[None, :]
    return jnp.where((column < half)[None, :], jnp.cos(angle), jnp.sin(angle))


def normalize(values):
    mean = jnp.mean(values, axis=-1, keepdims=True)
    centered = values - mean
    inverse = lax.rsqrt(jnp.mean(centered * centered, axis=-1, keepdims=True) + 1e-06)
    return (centered * inverse, inverse)


def ln_back(grad, normed, inverse):
    mean_grad = jnp.mean(grad, axis=-1, keepdims=True)
    mean_cross = jnp.mean(grad * normed, axis=-1, keepdims=True)
    return inverse * (grad - mean_grad - normed * mean_cross)


def gelu_both(values):
    inner = 0.7978845608 * (values + 0.044715 * values * values * values)
    tangent = jnp.tanh(inner)
    halved = 0.5 * (1.0 + tangent)
    slope = halved + 0.5 * values * (1.0 - tangent * tangent) * 0.7978845608 * (
        1.0 + 3.0 * 0.044715 * values * values
    )
    return values * halved, slope


def dot(left, right):
    return jnp.dot(left, right, preferred_element_type=F32)


def dot_back(left, right):
    return lax.dot_general(left, right, (((1,), (1,)), ((), ())), preferred_element_type=F32)


def dot_across(left, right):
    return lax.dot_general(left, right, (((0,), (0,)), ((), ())), preferred_element_type=F32)


def split(values):
    high = values.astype(BF)
    return high, (values - high.astype(F32)).astype(BF)


def sibling(values):
    return lax.ppermute(values, "core", [(0, 1), (1, 0)])


def swap_y(values):
    return lax.all_to_all(values, "y", 0, 0)


class Stream:
    def __init__(self, plan, sems):
        self.copies = [
            pltpu.make_async_copy(source, target, sems.at[index])
            for index, (source, target) in enumerate(plan)
        ]
        for copy in self.copies:
            copy.start()
        self.at = 0

    def next(self):
        self.copies[self.at].wait()
        self.at += 1


def matrices(layer, sources, target):
    return [(source.at[layer], target.at[side]) for side, source in enumerate(sources)]


def halves(extent):
    cut = extent // 2 // 128 * 128 + 128
    return ((0, cut), (cut, extent - cut))


def matrix_halves(layer, source, target, side):
    return [
        (source.at[layer, pl.ds(at, size)], target.at[side, pl.ds(at, size)])
        for at, size in halves(target.shape[1])
    ]


def finish(total, stream, left, right_ref, last, out_ref, out, sems):
    (first_at, first_size), (next_at, next_size) = halves(right_ref.shape[1])
    stream.next()
    total = total + dot(left[:, :first_size], right_ref[1, :first_size, :])
    stream.next()
    sends = []
    for index, (at, size) in enumerate(halves(right_ref.shape[2])):
        columns = slice(at, at + size)
        part = total[:, columns] + dot(left[:, next_at:], right_ref[1, next_at:, columns])
        out_ref[:, columns] = last(part, columns).astype(BF)
        send = pltpu.make_async_copy(
            out_ref.at[:, pl.ds(at, size)], out.at[:, pl.ds(at, size)], sems.at[index]
        )
        send.start()
        sends.append(send)
    for send in sends:
        send.wait()


def identity(extent):
    row = lax.broadcasted_iota(jnp.int32, (extent, extent), 0)
    col = lax.broadcasted_iota(jnp.int32, (extent, extent), 1)
    return (row == col).astype(BF)


def turned(values):
    return dot_back(identity(values.shape[1]), values)


def turned_wide(values):
    return dot_across(values, identity(values.shape[0]))


def product_kernel(at_ref, packed_ref, w1_ref, w2_ref, out, bias_ref, out_ref, sems):
    blocks, columns, _ = packed_ref.shape
    rows, hidden = w1_ref.shape
    cells = out_ref.shape[0] // STEPS
    pick_row = lax.broadcasted_iota(jnp.int32, (rows, columns), 0)
    pick_col = lax.broadcasted_iota(jnp.int32, (rows, columns), 1)
    mine = (pick_col == pick_row + rows * at_ref[1]).astype(BF)
    total = jnp.zeros((columns, cells), F32)
    for block in range(blocks):
        total = total + packed_ref[block, :, :cells].astype(F32)
    mean = jnp.sum(total, axis=0, keepdims=True) / (blocks * columns)
    local = dot(mine, packed_ref[at_ref[0]])
    high, low = split(local[:, :cells] - mean)
    out_rows = local[:, 2 * cells : 3 * cells].astype(BF)

    def modulation(index):
        block = dot(mine, packed_ref[at_ref[2 * index + 2]]).astype(BF)[:, 3 * cells :]
        row = lax.broadcasted_iota(jnp.int32, (block.shape[1], 8), 0)
        kind = lax.broadcasted_iota(jnp.int32, (block.shape[1], 8), 1)
        want = (row == 3 * (kind + LAYERS) + at_ref[2 * index + 3]) & (kind < STEPS)
        return dot(block, want.astype(BF)).astype(BF)

    shift, scale, gate = modulation(0), modulation(1), modulation(2)
    cell_row = lax.broadcasted_iota(jnp.int32, (cells, cells * STEPS), 0)
    cell_col = lax.broadcasted_iota(jnp.int32, (cells, cells * STEPS), 1)
    by_cell = (cell_col // STEPS == cell_row).astype(BF)
    step_row = lax.broadcasted_iota(jnp.int32, (8, cells * STEPS), 0)
    step_col = lax.broadcasted_iota(jnp.int32, (8, cells * STEPS), 1)
    by_step = (step_col % STEPS == step_row).astype(BF)
    left_in = (dot(high, by_cell) + dot(low, by_cell)) * (1.0 + dot(scale, by_step))
    left_out = dot(out_rows, by_cell) * dot(gate, by_step)
    gap = -hidden % 128
    out_ref[:, :hidden] = dot_across(left_in.astype(BF), w1_ref[...]).astype(BF)
    out_ref[:, hidden : hidden + gap] = jnp.zeros((cells * STEPS, gap), BF)
    out_ref[:, hidden + gap : 2 * hidden + gap] = dot_across(left_out.astype(BF), w2_ref[...]).astype(BF)
    out_ref[:, 2 * hidden + gap :] = jnp.zeros((cells * STEPS, gap), BF)
    send = pltpu.make_async_copy(out_ref, out, sems.at[0])
    send.start()
    bias_ref[...] = dot_across(shift, w1_ref[...]).astype(BF)
    send.wait()


def select_kernel(step_ref, parts_ref, bias_ref, out, out_ref, sems):
    samples, piece, _ = parts_ref.shape
    hidden = bias_ref.shape[1]
    chunk = piece // STEPS

    def at_step(extent):
        row = lax.broadcasted_iota(jnp.int32, (samples * 8, extent), 0)
        step = jnp.zeros((samples * 8, extent), jnp.int32)
        for sample in range(samples):
            step = jnp.where(row // 8 == sample, step_ref[sample] - 1, step)
        return row % 8, lax.broadcasted_iota(jnp.int32, (samples * 8, extent), 1), step

    total = parts_ref[0].astype(F32)
    for source in range(1, samples):
        total = total + parts_ref[source].astype(F32)
    place, col, step = at_step(piece)
    pick = ((col == place * STEPS + step) & (place < chunk)).astype(BF)
    chosen = dot(pick, total.astype(BF))
    out_ref[...] = chosen.astype(BF)
    place, col, step = at_step(8)
    pick = ((col == step) & (place == chunk)).astype(BF)
    out_ref[:, :hidden] = (chosen[:, :hidden] + dot(pick, bias_ref[...])).astype(BF)
    send = pltpu.make_async_copy(out_ref, out, sems.at[0])
    send.start()
    send.wait()


def student_kernel(hidden, x_ref, packed_ref, mat_ref, out_ref):
    cells, seq = x_ref.shape
    width = packed_ref.shape[0]
    lanes, wide = mat_ref.shape
    second_at = wide // 2
    group = lanes * 4 // cells
    x = turned_wide(x_ref[...]).astype(BF)
    proj = packed_ref[:, :cells]
    centered = proj.astype(F32)
    centered = centered - jnp.mean(centered, axis=0, keepdims=True)
    high, low = split(centered)
    gram = dot_across(high, high) + (dot_across(high, low) + dot_across(low, high))
    direct = dot_across(proj, packed_ref[:, 2 * cells : 3 * cells])

    def times(matrix):
        first, second = split(matrix)
        return dot(x, first) + dot(x, second)

    var = jnp.sum(times(gram) * x.astype(F32), axis=1, keepdims=True) / width
    inverse = lax.rsqrt(jnp.maximum(var, 0.0) + 1e-06)
    row = lax.broadcasted_iota(jnp.int32, (cells, lanes), 0)
    col = lax.broadcasted_iota(jnp.int32, (cells, lanes), 1)
    spread = (col == group * (row // 4) + row % 4).astype(BF)
    bias_col = lax.broadcasted_iota(jnp.int32, (8, lanes), 1)
    bias = dot((bias_col % group == 4).astype(BF), mat_ref[:, :hidden])[:1]
    z = inverse * dot(dot(x, spread).astype(BF), mat_ref[:, :hidden]) + bias
    active = gelu_both(z)[0].astype(BF)
    high, low = split(dot_back(active, mat_ref[:, second_at : second_at + hidden]))
    velocity = dot_back(high, spread) + dot_back(low, spread) + 0.125 * times(direct)
    half = seq // 2
    for target in range(out_ref.shape[0]):
        at = target % 2 * half
        out_ref[target] = velocity[at : at + half]


def first_product_kernel(packed_ref, up, out_ref, vector_ref, up_ref, left_ref, sems):
    blocks, columns, _ = packed_ref.shape
    cells = out_ref.shape[0] - 8
    stream = Stream(matrices(0, (up,), up_ref), sems)
    total = jnp.zeros((columns, cells), F32)
    for block in range(blocks):
        total = total + packed_ref[block, :, cells : 2 * cells].astype(F32)
    mean = jnp.sum(total, axis=0, keepdims=True) / (blocks * columns)

    def vector(kind, block):
        at = kind * blocks + block
        return packed_ref[at // 3, :, 3 * cells + at % 3 : 3 * cells + at % 3 + 1].astype(F32)

    for block in range(blocks):
        centered = packed_ref[block, :, cells : 2 * cells].astype(F32) - mean
        scaled = centered * (1.0 + vector(1, block))
        shift = jnp.broadcast_to(vector(0, block), (columns, 8))
        left_ref[block * columns : (block + 1) * columns, :] = jnp.concatenate(
            [scaled, shift], axis=1
        ).astype(BF)
    for source in range(blocks):
        rows = turned(packed_ref[source, :, 3 * cells : 3 * cells + 3 * LAYERS])
        for third in range(3):
            kind, block = divmod(source * 3 + third, blocks)
            for layer in range(LAYERS):
                vector_ref[
                    3 * layer + kind : 3 * layer + kind + 1, block * columns : (block + 1) * columns
                ] = rows[3 * layer + third : 3 * layer + third + 1]
    left = turned(left_ref[...]).astype(BF)
    stream.next()
    out_ref[...] = dot_back(left, up_ref[0])


def first_forward_kernel(
    where_ref, student_ref, teacher_ref, velocity_ref, x_ref, noise_ref, packed_ref, mat_own, mat_sib, own, sib,
    y_out, slope_out, latents_ref, noised_ref, g_ref, back_ref,
    w_ref, y_ref, slope_ref, both_ref, sems
):
    cells, seq = x_ref.shape
    half = seq // 2
    stream = Stream(
        matrices(0, (own,), w_ref) + matrix_halves(0, sib, w_ref, 1), sems
    )
    sample = where_ref[0]
    sigma_s = student_ref[sample].astype(F32) * 0.25
    sigma_t = teacher_ref[sample].astype(F32) * 0.001
    both_ref[0] = turned_wide(x_ref[...])
    both_ref[1] = turned_wide(noise_ref[...])
    mine = pl.ds(pl.multiple_of(where_ref[2] * half, half), half)
    latents = (both_ref[0, mine, :] - sigma_s * sum_parts(velocity_ref)).astype(BF)
    latents_ref[...] = latents
    x = ((1.0 - sigma_t) * latents.astype(F32) + sigma_t * both_ref[1, mine, :]).astype(BF)
    noised_ref[...] = x
    proj = packed_ref[:, cells : 2 * cells]
    g_0 = dot_back(x, proj).astype(BF)
    g_ref[...] = g_0
    normed, inverse = normalize(g_0.astype(F32))
    back_ref[:, :cells] = dot(normed.astype(BF), proj)
    back_ref[:, cells:] = jnp.broadcast_to(inverse, (half, cells))
    twice = jnp.concatenate([x, x], axis=1)
    actives = []
    for side, mat_ref in enumerate((mat_own, mat_sib)):
        high, low = split(mat_ref[:cells])
        z = inverse * dot(twice, jnp.concatenate([high, low], axis=0)) + mat_ref[cells : cells + 1]
        active, slope = gelu_both(z)
        slope_ref[side] = slope.astype(BF)
        actives.append(active.astype(BF))
    keep = pltpu.make_async_copy(slope_ref, slope_out, sems.at[3])
    keep.start()
    stream.next()
    y = dot(actives[0], w_ref[0])
    finish(y, stream, actives[1], w_ref, lambda part, _: part, y_ref, y_out, sems.at[pl.ds(4, 2)])
    keep.wait()


def forward_kernel(
    g_ref, vector_ref, up_own, up_sib, down_own, down_sib, y_out, slope_out,
    up_ref, down_ref, y_ref, slope_ref, sems
):
    stream = Stream(
        matrices(1, (up_own, up_sib), up_ref)
        + matrices(1, (down_own,), down_ref)
        + matrix_halves(1, down_sib, down_ref, 1),
        sems,
    )
    normed, _ = normalize(g_ref[...].astype(F32))
    u = (normed * (1.0 + vector_ref[4:5]) + vector_ref[3:4]).astype(BF)
    actives = []
    for side in range(2):
        stream.next()
        active, slope = gelu_both(dot_back(u, up_ref[side]))
        slope_ref[side] = slope.astype(BF)
        actives.append(active.astype(BF))
    keep = pltpu.make_async_copy(slope_ref, slope_out, sems.at[5])
    keep.start()
    stream.next()
    y = dot(actives[0], down_ref[0])
    finish(y, stream, actives[1], down_ref, lambda part, _: part, y_ref, y_out, sems.at[pl.ds(6, 2)])
    keep.wait()


def backward_kernel(
    dy_ref, vector_ref, slope, head, up_own, up_sib, down_own, down_sib, out,
    up_ref, down_ref, slope_ref, head_ref, out_ref, sems
):
    stream = Stream(
        [(slope, slope_ref)]
        + matrices(1, (down_own, down_sib), down_ref)
        + [(head, head_ref)]
        + matrices(1, (up_own,), up_ref)
        + matrix_halves(1, up_sib, up_ref, 1),
        sems,
    )
    dy = dy_ref[...]
    stream.next()
    dz = []
    for side in range(2):
        stream.next()
        dz.append((dot_back(dy, down_ref[side]) * slope_ref[side].astype(F32)).astype(BF))
    stream.next()
    stream.next()
    du = dot(dz[0], up_ref[0])

    def last(part, columns):
        return part * (1.0 + vector_ref[4:5, columns]) + head_ref[:, columns].astype(F32)

    finish(du, stream, dz[1], up_ref, last, out_ref, out, sems.at[pl.ds(7, 2)])


def first_backward_kernel(
    where_ref, teacher_ref, dy_ref, x_ref, back_ref, score_1, score_2, direct_ref, mat_own, mat_sib, slope, own, sib,
    out_ref, w_ref, slope_ref, all_ref, sems
):
    cells = x_ref.shape[1]
    ranges = halves(w_ref.shape[1])
    plan = matrix_halves(0, own, w_ref, 0) + matrix_halves(0, sib, w_ref, 1)
    stream = Stream([(slope, slope_ref)] + plan, sems)
    dy = dy_ref[...]
    stream.next()
    total = None
    for side, mat_ref in enumerate((mat_own, mat_sib)):
        high, low = split(mat_ref[:cells])
        for at, size in ranges:
            stream.next()
            da = dot_back(dy, w_ref[side, at : at + size, :])
            dz = (da * slope_ref[side, :, at : at + size].astype(F32)).astype(BF)
            part = dot_back(dz, high[:, at : at + size]) + dot_back(dz, low[:, at : at + size])
            total = part if total is None else total + part
    inverse = back_ref[:, cells : cells + 1]
    cross = inverse * jnp.sum(x_ref[...].astype(F32) * total, axis=1, keepdims=True) / dy.shape[1]
    rest = 1.0 - teacher_ref[where_ref[0]].astype(F32) * 0.001
    all_ref[:, :cells] = rest * (inverse * (total - back_ref[:, :cells] * cross))
    all_ref[:, cells:] = score_1[:, :cells] + score_2[:, :cells]
    rows = direct_ref.shape[0]
    mine = pl.ds(pl.multiple_of(where_ref[1] * rows, rows), rows)
    all_ref[mine, :cells] += rest * direct_ref[...]
    final = all_ref[...].T[: out_ref.shape[1]]
    for target in range(out_ref.shape[0]):
        out_ref[target] = final


def modulation_kernel(
    cond_s_ref, cond_t_ref, s_mod, t_mod, in_s, in_t, out_proj, head, out, proj_ref, head_out,
    s_ref, t_ref, stack_ref, head_ref, out_ref, head_all, sems
):
    samples = cond_t_ref.shape[0]
    cells = in_s.shape[0]
    hidden = s_mod.shape[1]
    stream = Stream(
        [(head, head_ref), (s_mod, s_ref), (t_mod, t_ref)]
        + [
            (source, stack_ref.at[pl.ds(index * cells, cells)])
            for index, source in enumerate((in_s, in_t, out_proj))
        ],
        sems,
    )
    stream.next()
    head_all[:, : head_ref.shape[1]] = head_ref[...]
    head_all[:, head_ref.shape[1] :] = jnp.zeros(
        (head_ref.shape[0], head_all.shape[1] - head_ref.shape[1]), BF
    )
    keep = pltpu.make_async_copy(head_all, head_out, sems.at[6])
    keep.start()
    stream.next()

    def product(cond, weight):
        extent = cond.shape[0]
        high, rest = split(cond)
        rest = cond - high.astype(F32)
        middle, low = split(rest)
        parts = dot(jnp.concatenate([high, middle, low], axis=0), weight)
        return (parts[:extent] + (parts[extent : 2 * extent] + parts[2 * extent :])).astype(BF)

    def place(extent, first, every):
        row = lax.broadcasted_iota(jnp.int32, (samples * 8, extent), 0)
        col = lax.broadcasted_iota(jnp.int32, (samples * 8, extent), 1)
        if every:
            return (row % 8 == first + col).astype(BF)
        return ((row // 8 == col) & (row % 8 == first)).astype(BF)

    total = dot(place(16, LAYERS, True), product(cond_s_ref[...], s_ref[...]))
    stream.next()
    for layer in range(LAYERS):
        part = product(cond_t_ref[...], t_ref[layer])
        total = total + dot(place(samples, layer, False), part)
    out_ref[:, :hidden] = total.astype(BF)
    out_ref[:, hidden:] = jnp.zeros((samples * 8, out_ref.shape[1] - hidden), BF)
    send = pltpu.make_async_copy(out_ref, out, sems.at[7])
    send.start()
    for _ in range(3):
        stream.next()
    proj_ref[...] = turned_wide(stack_ref[...]).astype(BF)
    keep.wait()
    send.wait()


def sum_parts(parts_ref):
    total = parts_ref[0].astype(F32)
    for source in range(1, parts_ref.shape[0]):
        total = total + parts_ref[source].astype(F32)
    return total


def share(values_ref, everyone, sems):
    copies = [
        pltpu.make_async_copy(values_ref, everyone.at[target], sems.at[target])
        for target in range(everyone.shape[0])
    ]
    for copy in copies:
        copy.start()
    for copy in copies:
        copy.wait()


def output_kernel(parts_ref, grad_ref, score_ref):
    cells = grad_ref.shape[0]
    half = parts_ref.shape[2]
    for core in range(2):
        total = parts_ref[core]
        for source in range(core + 2, parts_ref.shape[0], 2):
            total = total + parts_ref[source]
        columns = slice(core * half, (core + 1) * half)
        grad_ref[:, columns] = total[:cells]
        score_ref[:, columns] = total[cells : cells + score_ref.shape[0]]


def first_middle_kernel(where_ref, parts_ref, g_ref, vector_ref, mine_ref, everyone, sems):
    rows = mine_ref.shape[0]
    before = g_ref[pl.ds(pl.multiple_of(where_ref[1] * rows, rows), rows), :].astype(F32)
    after = (before + vector_ref[2:3] * sum_parts(parts_ref)).astype(BF)
    mine_ref[...] = after
    share(mine_ref, everyone, sems)


def last_middle_kernel(parts_ref, g_ref, vector_ref, mine_ref, everyone, sems):
    after = (g_ref[...].astype(F32) + vector_ref[5:6] * sum_parts(parts_ref)).astype(BF)
    mine_ref[...] = after
    share(mine_ref, everyone, sems)


def last_back_kernel(parts_ref, g_ref, vector_ref, grad_ref, everyone, share_ref, sems):
    normed, inverse = normalize(g_ref[...].astype(F32))
    grad = ln_back(sum_parts(parts_ref), normed, inverse)
    grad_ref[...] = grad
    share_ref[...] = (vector_ref[5:6] * grad).astype(BF)
    share(share_ref, everyone, sems)


def first_back_kernel(parts_ref, g_ref, old_ref, vector_ref, packed_ref, direct_ref, everyone, share_ref, sems):
    normed, inverse = normalize(g_ref[...].astype(F32))
    grad = old_ref[...] + ln_back(sum_parts(parts_ref), normed, inverse)
    cells = direct_ref.shape[1]
    direct_ref[...] = dot(grad.astype(BF), packed_ref[:, cells : 2 * cells])
    share_ref[...] = (vector_ref[2:3] * grad).astype(BF)
    share(share_ref, everyone, sems)


def block_owner(fsdp, block):
    x_hi, z = fsdp // 4, fsdp % 4
    return (x_hi ^ (block & 1)) * 4 + (z ^ ((block >> 1 & 1) ^ (block >> 2 & 1) * 3))


def swap_fsdp(values, pattern):
    other = lax.ppermute(values, "fsdp", [(at, at ^ pattern) for at in range(8)])
    return jnp.concatenate([values, other], axis=0)


def head_kernel(layer, pick_ref, where_ref, g_ref, out_own, out_sib, near, rest, back_out, score_ref, weight_ref, back_ref, use_ref, sems):
    blocks = 8
    size = near.shape[0] * 2 // blocks
    wide = near.shape[1] // 2
    plan = []
    for block in range(blocks):
        row = pl.multiple_of(block_owner(where_ref[3], block) * size, size)
        source = near if block < blocks // 2 else rest
        plan.append(
            (source.at[pl.ds(block % (blocks // 2) * size, size)], weight_ref.at[pl.ds(row, size)])
        )
    stream = Stream(plan, sems)
    use_ref[...] = jnp.zeros(use_ref.shape, F32)
    for side, outs in enumerate((out_own, out_sib)):
        for head in range(2):
            use = jnp.where(pick_ref[head] == layer, 1.0, 0.0)
            use_ref[head : head + 1, side * wide : side * wide + outs.shape[1]] = (
                use * outs[head : head + 1, :]
            )
    normed, _ = normalize(g_ref[...].astype(F32))
    quantised = normed.astype(BF)
    for _ in plan:
        stream.next()
    weight = weight_ref[...]
    e = dot(quantised, weight)
    sigm = 1.0 / (1.0 + jnp.exp(-e))
    active = e * sigm
    outs = use_ref[...]
    slope = sigm * (1.0 + e * (1.0 - sigm))
    back_ref[...] = dot_back((-(outs[0:1] + outs[1:2]) * slope).astype(BF), weight).astype(BF)
    send = pltpu.make_async_copy(back_ref, back_out, sems.at[blocks])
    send.start()
    scores = [jnp.sum(active * outs[head : head + 1], axis=1, keepdims=True) for head in range(2)]
    lane = lax.broadcasted_iota(jnp.int32, score_ref.shape, 1)
    score_ref[...] = jnp.where(lane == 0, scores[0], 0.0) + jnp.where(lane == 1, scores[1], 0.0)
    send.wait()


WHOLE = pl.BlockSpec(memory_space=pltpu.VMEM)
FAR = pl.BlockSpec(memory_space=pltpu.HBM)


def here(kernel, name, out_shape, operands, scalars=0, far=0, far_out=(), scratch=(), limit=20):
    many = isinstance(out_shape, tuple)
    near = len(operands) - scalars - far
    shapes = tuple(
        pltpu.HBM(shape.shape, shape.dtype) if index in far_out else shape
        for index, shape in enumerate(out_shape if many else (out_shape,))
    )
    operands = operands[: scalars + near] + tuple(
        pltpu.with_memory_space_constraint(operand, pltpu.HBM) for operand in operands[scalars + near :]
    )
    specs = tuple(
        FAR if index in far_out else WHOLE for index in range(len(out_shape) if many else 1)
    )
    return pl.pallas_call(
        kernel,
        name=name,
        out_shape=shapes if many else shapes[0],
        in_specs=[pl.BlockSpec(memory_space=pltpu.SMEM)] * scalars + [WHOLE] * near + [FAR] * far,
        out_specs=specs if many else specs[0],
        scratch_shapes=list(scratch),
        compiler_params=pltpu.CompilerParams(vmem_limit_bytes=limit * 2**20),
    )(*operands)


def array(shape, dtype):
    return jax.ShapeDtypeStruct(shape, dtype)


def body(
    noisy_latents,
    student_step,
    teacher_step,
    teacher_noise,
    layer_pick,
    in_proj_s,
    in_proj_t,
    out_proj,
    s_mod,
    s_w1,
    s_w2,
    t_mod,
    t_w1,
    t_w2,
    d_w1,
    d_w2,
):
    cells = in_proj_s.shape[0]
    width = in_proj_s.shape[1] * 8
    samples = student_step.shape[0]
    layers = t_w1.shape[0]
    heads = d_w2.shape[0]
    seq = noisy_latents.shape[1]
    half = seq // 2
    quarter = half // 4
    rows = s_mod.shape[0]
    hidden = s_w1.shape[1]
    columns = in_proj_s.shape[1]
    sample = lax.axis_index(SAMPLE)
    at_y = lax.axis_index("y")
    at_core = lax.axis_index("core")
    start = sample * rows

    sig_all_t = teacher_step.astype(F32) * 0.001
    sig_steps = (1 + jnp.arange(STEPS)).astype(F32) * 0.25
    cond_s = jax.nn.silu(embed_block(1000.0 * sig_steps, width, rows, start))
    cond_t = jax.nn.silu(embed_block(1000.0 * sig_all_t, width, rows, start))
    at_grp = lax.axis_index("grp")
    where = jnp.stack([sample, at_y, at_core, lax.axis_index("fsdp")]).astype(jnp.int32)
    block = sample * rows // columns
    places = [block, sample * rows // rows % (columns // rows)]
    for offset in (0, 8, 16):
        places += [(block + offset) // 3, (block + offset) % 3]
    places = jnp.stack(places).astype(jnp.int32)
    head_wide = columns + -columns % 128
    mod_wide = s_mod.shape[1] + -s_mod.shape[1] % 128
    picks = layer_pick[0]
    mod_part, projections, head_block = here(
        modulation_kernel,
        "modulation",
        (
            array((samples * 8, mod_wide), BF),
            array((columns, 3 * cells), BF),
            array((rows, head_wide), BF),
        ),
        (
            jnp.pad(cond_s, ((0, 16 - STEPS), (0, 0))),
            cond_t,
            s_mod,
            t_mod,
            in_proj_s,
            in_proj_t,
            out_proj,
            d_w1,
        ),
        far=6,
        far_out=(0, 2),
        scratch=(
            pltpu.VMEM(s_mod.shape, BF),
            pltpu.VMEM(t_mod.shape, BF),
            pltpu.VMEM((3 * cells, columns), BF),
            pltpu.VMEM(d_w1.shape, BF),
            pltpu.VMEM((samples * 8, mod_wide), BF),
            pltpu.VMEM((rows, head_wide), BF),
            pltpu.SemaphoreType.DMA((8,)),
        ),
    )
    mod_part, projections, where, places, head_block, picks = lax.optimization_barrier(
        (mod_part, projections, where, places, head_block, picks)
    )
    mod_part = mod_part.reshape(samples, 8, mod_wide)
    mods = jnp.sum(lax.all_to_all(mod_part, SAMPLE, 0, 0).astype(F32), axis=0)
    kinds = layers + STEPS
    mods = mods[:kinds, : 3 * columns].reshape(kinds * 3, columns).astype(BF)
    packed = jnp.concatenate([projections, mods.T], axis=1)
    head_block = jnp.concatenate([head_block, sibling(head_block)], axis=1)
    head_other = lax.ppermute(head_block, "grp", [(0, 1), (1, 0)])
    gathered = lax.all_gather(packed, TP, axis=0, tiled=False)
    gathered, head_other = lax.optimization_barrier((gathered, head_other))

    gap = -hidden % 128
    both_wide = 2 * (hidden + gap)
    parts, part_bias = here(
        product_kernel,
        "product",
        (
            jax.ShapeDtypeStruct((cells * STEPS, both_wide), BF),
            jax.ShapeDtypeStruct((8, hidden), BF),
        ),
        (places, gathered, s_w1, s_w2.T),
        scalars=1,
        far_out=(0,),
        scratch=(pltpu.VMEM((cells * STEPS, both_wide), BF), pltpu.SemaphoreType.DMA((1,))),
    )
    piece = cells * STEPS // samples
    chunk = cells // samples
    t_w1 = jnp.swapaxes(t_w1, 1, 2)
    parts, gathered, t_w1, t_w2, d_w2 = lax.optimization_barrier((parts, gathered, t_w1, t_w2, d_w2))
    w2_sib = sibling(t_w2)
    w1_sib = sibling(t_w1)
    d_w2_sib = sibling(d_w2)
    received = lax.all_to_all(parts.reshape(samples, piece, both_wide), SAMPLE, 0, 0)
    head_block, head_other, _ = lax.optimization_barrier((head_block, head_other, parts))
    head_pair = jnp.concatenate(
        [
            jnp.where(at_grp == 0, head_block, head_other),
            jnp.where(at_grp == 0, head_other, head_block),
        ],
        axis=0,
    )

    first_own, vectors = here(
        first_product_kernel,
        "first_product",
        (array((cells + 8, hidden), F32), array((8, width), F32)),
        (gathered, t_w1),
        far=1,
        scratch=(
            pltpu.VMEM((1, hidden, width), BF),
            pltpu.VMEM((width, cells + 8), BF),
            pltpu.SemaphoreType.DMA((1,)),
        ),
        limit=44,
    )
    received, first_own, vectors = lax.optimization_barrier((received, first_own, vectors))

    chosen = here(
        select_kernel,
        "select",
        array((samples * 8, both_wide), BF),
        (student_step, received, part_bias),
        scalars=1,
        far_out=(0,),
        scratch=(pltpu.VMEM((samples * 8, both_wide), BF), pltpu.SemaphoreType.DMA((1,))),
    )
    mine = lax.all_to_all(chosen.reshape(samples, 8, both_wide), SAMPLE, 0, 0)
    mine = mine.reshape(samples * 8, both_wide)

    latent_in = noisy_latents[0].T
    noise = teacher_noise[0].T
    packed = gathered.reshape(width, -1)
    velocity = here(
        functools.partial(student_kernel, hidden),
        "student",
        array((8, half, cells), F32),
        (latent_in, packed, mine),
    )
    head_pair, _ = lax.optimization_barrier((head_pair, mine))
    head_other = lax.ppermute(head_pair, "fsdp", [(at, at ^ 4) for at in range(8)])
    velocity = lax.all_to_all(velocity, TP, 0, 0)
    head_pair, head_other, _ = lax.optimization_barrier((head_pair, head_other, velocity))
    head_two = jnp.concatenate([head_pair, head_other], axis=0)
    head_four = swap_fsdp(head_two, 1)

    def both(values, axis):
        other = sibling(values)
        first = jnp.where(at_core == 0, values, other)
        second = jnp.where(at_core == 0, other, values)
        return jnp.concatenate([first, second], axis=axis)

    first_sib = sibling(first_own)
    velocity, w1_sib, w2_sib, d_w2_sib = lax.optimization_barrier((velocity, w1_sib, w2_sib, d_w2_sib))

    token_rows = pltpu.VMEM((half, width), BF)
    inner = pltpu.VMEM((2, half, hidden), BF)
    matrix = pltpu.VMEM((2, hidden, width), BF)
    rows_out = array((4, quarter, width), BF)
    mine_out = array((quarter, width), BF)
    tokens_out = array((half, width), BF)
    inner_out = array((2, half, hidden), BF)
    cells_out = array((half, cells), BF)
    y_0, slope_0, latents, noised, g_0, back_0 = here(
        first_forward_kernel,
        "first_forward",
        (tokens_out, inner_out, cells_out, cells_out, tokens_out, array((half, 2 * cells), F32)),
        (
            where,
            student_step,
            teacher_step,
            velocity,
            latent_in,
            noise,
            packed,
            first_own,
            first_sib,
            t_w2,
            w2_sib,
        ),
        scalars=3,
        far=2,
        far_out=(0, 1),
        scratch=(
            matrix,
            token_rows,
            inner,
            pltpu.VMEM((2, seq, cells), F32),
            pltpu.SemaphoreType.DMA((6,)),
        ),
        limit=44,
    )

    def sums(partial):
        return swap_y(partial.reshape(4, quarter, width))

    last = (t_w1, w1_sib, t_w2, w2_sib)
    four = pltpu.SemaphoreType.DMA((4,))
    quarter_rows = pltpu.VMEM((quarter, width), BF)
    g_1_mine, g_1 = here(
        first_middle_kernel,
        "first_middle",
        (mine_out, rows_out),
        (where, sums(y_0), g_0, vectors),
        scalars=1,
        far_out=(1,),
        scratch=(four,),
    )
    head_four, _ = lax.optimization_barrier((head_four, y_0))
    head_rest = lax.ppermute(head_four, "fsdp", [(at, at ^ 3) for at in range(8)])
    g_1 = swap_y(g_1).reshape(half, width)
    y_1, slope_1 = here(
        forward_kernel,
        "forward",
        (tokens_out, inner_out),
        (g_1, vectors) + last,
        far=4,
        far_out=(0, 1),
        scratch=(matrix, matrix, token_rows, inner, pltpu.SemaphoreType.DMA((8,))),
        limit=44,
    )
    g_2_mine, g_2 = here(
        last_middle_kernel,
        "last_middle",
        (mine_out, rows_out),
        (sums(y_1), g_1_mine, vectors),
        far_out=(1,),
        scratch=(four,),
    )
    g_2 = swap_y(g_2).reshape(half, width)

    def head(name, layer, g):
        return here(
            functools.partial(head_kernel, layer),
            name,
            (tokens_out, array((half, 128), F32)),
            (picks, where, g, d_w2, d_w2_sib, head_four, head_rest),
            scalars=2,
            far=2,
            far_out=(0,),
            scratch=(
                pltpu.VMEM((width, 2 * head_wide), BF),
                token_rows,
                pltpu.VMEM((8, 2 * head_wide), F32),
                pltpu.SemaphoreType.DMA((9,)),
            ),
        )

    head_back_2, scores_2 = head("head_last", 1, g_2)

    dg_2, dy_1 = here(
        last_back_kernel,
        "last_back",
        (array((quarter, width), F32), rows_out),
        (sums(head_back_2), g_2_mine, vectors),
        far_out=(1,),
        scratch=(quarter_rows, four),
    )
    g_1, latents, _ = lax.optimization_barrier((g_1, latents, dg_2))
    latents = both(latents, 0)
    head_back_1, scores_1 = head("head_first", 0, g_1)
    du_1 = here(
        backward_kernel,
        "backward",
        tokens_out,
        (swap_y(dy_1).reshape(half, width), vectors, slope_1, head_back_1) + last,
        far=6,
        far_out=(0,),
        scratch=(matrix, matrix, inner, token_rows, token_rows, pltpu.SemaphoreType.DMA((9,))),
        limit=44,
    )
    direct, dy_0 = here(
        first_back_kernel,
        "first_back",
        (array((quarter, cells), F32), rows_out),
        (sums(du_1), g_1_mine, dg_2, vectors, packed),
        far_out=(1,),
        scratch=(quarter_rows, four),
    )
    dy_0, latents = lax.optimization_barrier((swap_y(dy_0).reshape(half, width), latents.T))
    final = here(
        first_backward_kernel,
        "first_backward",
        array((8, cells + 8, half), F32),
        (
            where,
            teacher_step,
            dy_0,
            noised,
            back_0,
            scores_1,
            scores_2,
            direct,
            first_own,
            first_sib,
            slope_0,
            t_w2,
            w2_sib,
        ),
        scalars=2,
        far=3,
        scratch=(matrix, inner, pltpu.VMEM((half, 2 * cells), F32), pltpu.SemaphoreType.DMA((5,))),
        limit=44,
    )
    grad, scores = here(
        output_kernel,
        "output",
        (array((cells, seq), F32), array((heads, seq), F32)),
        (lax.all_to_all(final, TP, 0, 0),),
    )
    return (latents.T[None], scores[None], grad.T[None])


def solution(mesh):
    names = list(mesh.axis_names)
    shape = list(mesh.devices.shape)
    at = names.index("tp")
    names[at : at + 1] = ["y", "core"]
    shape[at : at + 1] = [4, 2]
    fine = Mesh(mesh.devices.reshape(shape), tuple(names))
    placed = (
        P(SAMPLE, None, None),
        P(),
        P(),
        P(SAMPLE, None, None),
        P(SAMPLE, None),
        P(None, TP),
        P(None, TP),
        P(None, TP),
        P(SAMPLE, TP),
        P(SAMPLE, TP),
        P(TP, SAMPLE),
        P(None, SAMPLE, TP),
        P(None, None, TP),
        P(None, TP, None),
        P(SAMPLE, TP),
        P(None, TP),
    )
    return jax.shard_map(
        body,
        mesh=fine,
        in_specs=placed,
        out_specs=(P(SAMPLE, None, None), P(SAMPLE, None, None), P(SAMPLE, None, None)),
        check_vma=False,
    )
```
